32 devices in a mesh: var: 8 (over z, y), seg: 4 (over x, core).
Axes of the slice: x: 2, y: 2, z: 4, core: 2. Of those that a mesh axis runs over, the one named last changes fastest.
Arguments:
- tokens: bfloat16 [32, 32, 64, 256], P('seg', 'var'), may hold values from -6 to 6
- domain: int32 [32], P('seg'), may hold values from 0 to 3, as said below
- counts: int32 [4], replicated, may hold values from 1 to 32, as said below
- domain_mean: float32 [4, 256], replicated, may hold values from -3 to 3
- domain_scale: float32 [4, 256], replicated, may hold values from 0.5 to 2
- attn_inner: bfloat16 [3, 3, 256, 256], replicated, may hold values from -0.375 to 0.375
- attn_outer: bfloat16 [3, 256, 256], replicated, may hold values from -1 to 1
- attn_bias: float32 [3, 3, 256], replicated, may hold values from -1.2 to 1.2
- mlp_in: bfloat16 [2, 256, 512], replicated, may hold values from -0.375 to 0.375
- mlp_in_bias: float32 [2, 512], replicated, may hold values from -1.2 to 1.2
- mlp_out: bfloat16 [2, 512, 256], replicated, may hold values from -0.375 to 0.375
- mlp_out_bias: float32 [2, 256], replicated, may hold values from -1.2 to 1.2
- norm_gain: float32 [4, 256], replicated, may hold values from 0.5 to 1.5
- norm_bias: float32 [4, 256], replicated, may hold values from -1.2 to 1.2
- router: bfloat16 [64, 10, 256], replicated, may hold values from -6 to 6
- cotangent: bfloat16 [32, 32, 64, 256], P('seg', 'var'), may hold values from -6 to 6
Outputs:
- output: float32 [32, 32, 64, 256], P('seg', 'var')
- input_grad: float32 [32, 32, 64, 256], P('seg', 'var')
- grad_attn_inner: float32 [3, 3, 256, 256], replicated
- grad_attn_outer: float32 [3, 256, 256], replicated
- grad_attn_bias: float32 [3, 3, 256], replicated
- grad_mlp_in: float32 [2, 256, 512], replicated
- grad_mlp_in_bias: float32 [2, 512], replicated
- grad_mlp_out: float32 [2, 512, 256], replicated
- grad_mlp_out_bias: float32 [2, 256], replicated
- grad_norm_gain: float32 [4, 256], replicated
- grad_norm_bias: float32 [4, 256], replicated
- grad_router: float32 [64, 10, 256], replicated
The draws below stay inside these ranges and needn't reach their ends.
Inputs may be any that keep to these rules, and one draw needn't show every extreme that they name: The 8 series of one index of seg include one whose domain has 32 variables. Variables numbered counts[domain] and above are padding.
All inputs are finite; a program needn't handle non-finite values.
Results may differ from the reference program's by a relative error of at most 0.035.
The reference program's roundings to bfloat16 on the way count: a program that leaves them out, or rounds other values in their place, can miss the bound.
Values may be sent and summed in bfloat16 or wider, within the bound.
A program may use at most 320 MiB of HBM per device.

```python
import math
import jax
import jax.numpy as jnp
from jax import lax

D = 256
HEADS = 8
FF = 512
ROUTERS = 10
SEGS = 64
DOMAINS = 4
B_DEV = 8
BATCH = 32
NVARS = 32


def full_domain(key):
    return jax.random.randint(jax.random.fold_in(key, 7), (), 0, DOMAINS)


def draw_domain(key, part):
    chosen = full_domain(key)
    key = jax.random.fold_in(key, 11)
    key_order, key_place = jax.random.split(key)
    ordering = jax.random.permutation(key_order, jnp.arange(BATCH, dtype=jnp.int32) % DOMAINS)
    blocks = BATCH // B_DEV
    placed = jax.random.randint(key_place, (blocks,), 0, B_DEV)
    marked = (jnp.arange(B_DEV, dtype=jnp.int32)[None, :] == placed[:, None]).reshape(BATCH)
    return jnp.where(marked, chosen, ordering).astype(jnp.int32)


def draw_counts(key, part):
    chosen = full_domain(key)
    key = jax.random.fold_in(key, 13)
    drawn = jax.random.randint(key, (DOMAINS,), 1, NVARS + 1)
    return jnp.where(jnp.arange(DOMAINS, dtype=jnp.int32) == chosen, NVARS, drawn).astype(jnp.int32)


def block_scale(rng, dims, cuts, low, largest):
    level = 1.0
    for position, blocks in cuts:
        draws = jax.random.uniform(jax.random.fold_in(jax.random.fold_in(rng, 6), position), (blocks,), jnp.float32, low / len(cuts), largest / len(cuts))
        level = level * jnp.repeat(jnp.exp(draws), dims[position] // blocks).reshape((-1,) + (1,) * (len(dims) - 1 - position))
    return level


def centred(stream_key, shape, width, bound, shards=(), held_as=jnp.bfloat16):
    loudness = block_scale(stream_key, shape, shards, -0.22, 0.18) if shards else 1.0
    entries = jax.random.normal(stream_key, shape, jnp.float32) * width * loudness
    return jnp.minimum(jnp.maximum(entries, -bound), bound).astype(held_as)


def setup_inputs(seed: int = 0) -> dict:
    keys = jax.random.split(jax.random.key(seed), 17)
    return {
        "tokens": centred(keys[0], (BATCH, NVARS, SEGS, D), 1.0, 6.0, ((0, 4), (1, 8))),
        "domain": draw_domain(jax.random.fold_in(keys[16], 71), 0),
        "counts": draw_counts(jax.random.fold_in(keys[16], 71), 0),
        "domain_mean": centred(keys[3], (DOMAINS, D), 0.5, 3.0, (), jnp.float32),
        "domain_scale": jnp.clip(jnp.exp(jax.random.uniform(keys[4], (DOMAINS, D), jnp.float32, math.log(0.5), math.log(2.0))), 0.5, 2.0),
        "attn_inner": centred(keys[5], (3, 3, D, D), D ** -0.5, 0.375),
        "attn_outer": centred(keys[6], (3, D, D), (D // 8) ** -0.5, 1.0),
        "attn_bias": centred(keys[7], (3, 3, D), 0.2, 1.2, (), jnp.float32),
        "mlp_in": centred(keys[8], (2, D, FF), D ** -0.5, 0.375),
        "mlp_in_bias": centred(keys[9], (2, FF), 0.2, 1.2, (), jnp.float32),
        "mlp_out": centred(keys[10], (2, FF, D), (FF // 2) ** -0.5, 0.375),
        "mlp_out_bias": centred(keys[11], (2, D), 0.2, 1.2, (), jnp.float32),
        "norm_gain": jnp.clip(1.0 + 0.1 * jax.random.normal(keys[12], (4, D), jnp.float32), 0.5, 1.5),
        "norm_bias": centred(keys[13], (4, D), 0.2, 1.2, (), jnp.float32),
        "router": centred(keys[14], (SEGS, ROUTERS, D), 1.0, 6.0),
        "cotangent": centred(keys[15], (BATCH, NVARS, SEGS, D), 1.0, 6.0, ((0, 4), (1, 8))),
    }


highest = lax.Precision.HIGHEST
epsilon = 1e-05
masked_score = -1e+30

@jax.custom_vjp
def low(v):
    return lax.optimization_barrier(v.astype(jnp.bfloat16)).astype(jnp.float32)

@jax.custom_vjp
def low_back(v):
    return v

def low_keep(v):
    return (low(v), None)

def low_pass(kept, grad):
    return (grad,)

def back_keep(v):
    return (v, None)

def back_low(kept, grad):
    return (low(grad),)
low.defvjp(low_keep, low_pass)
low_back.defvjp(back_keep, back_low)

def product(values, weight):
    return jnp.matmul(values, weight, precision=highest)

def split_heads(values):
    return values.reshape(values.shape[:-1] + (HEADS, values.shape[-1] // HEADS))

def layer_norm(values, gain, shift):
    center = values - lax.optimization_barrier(jnp.mean(values, axis=-1, keepdims=True))
    spread = lax.optimization_barrier(jnp.mean(center * center, axis=-1, keepdims=True))
    return center * lax.rsqrt(spread + epsilon) * gain + shift

def feed(values, weight_in, bias_in, weight_out, bias_out):
    inner = low_back(product(low(values), weight_in) + bias_in)
    return low_back(product(low(jax.nn.gelu(inner)), weight_out) + bias_out)

def series_layer(series, params, offset, factor, valid):
    inner, outer, bias, up_weight, up_bias, down_weight, down_bias, gains, shifts, routes = params
    scale = (series.shape[-1] // HEADS) ** (-0.5)
    start = (series - offset) * factor
    start_low = low(start)
    time_query = split_heads(low(low_back(product(start_low, inner[0, 0]) + bias[0, 0])))
    time_key = split_heads(low(low_back(product(start_low, inner[0, 1]))))
    time_value = split_heads(low(low_back(product(start_low, inner[0, 2]) + bias[0, 1])))
    scores = low_back(jnp.einsum('nshe,nthe->nhst', time_query, time_key, precision=highest) * scale)
    probs = low(jax.nn.softmax(scores, axis=-1))
    context = low(low_back(jnp.einsum('nhst,nthe->nshe', probs, time_value, precision=highest).reshape(series.shape)))
    norm_one = layer_norm(start + low_back(product(context, outer[0]) + bias[0, 2]), gains[0], shifts[0])
    norm_two = layer_norm(norm_one + feed(norm_one, up_weight[0], up_bias[0], down_weight[0], down_bias[0]), gains[1], shifts[1])
    series_low = low(norm_two)
    send_query = split_heads(low(product(low(routes), inner[1, 0]) + bias[1, 0]))
    send_key = split_heads(low(low_back(product(series_low, inner[1, 1]))))
    send_value = split_heads(low(low_back(product(series_low, inner[1, 2]) + bias[1, 1])))
    send_scores = jnp.einsum('srhe,nshe->srhn', send_query, send_key, precision=highest) * scale
    send_prob = jax.nn.softmax(jnp.where(valid, send_scores, masked_score), axis=-1)
    gathered = jnp.einsum('srhn,nshe->srhe', send_prob, send_value, precision=highest).reshape(routes.shape)
    buffer = low(low_back(product(low(low_back(gathered)), outer[1]) + bias[1, 2]))
    recv_query = split_heads(low(low_back(product(series_low, inner[2, 0]) + bias[2, 0])))
    recv_key = split_heads(low(low_back(product(buffer, inner[2, 1]))))
    recv_value = split_heads(low(low_back(product(buffer, inner[2, 2]) + bias[2, 1])))
    recv_scores = jnp.einsum('nshe,srhe->nshr', recv_query, recv_key, precision=highest) * scale
    recv_prob = jax.nn.softmax(recv_scores, axis=-1)
    recv_out = low(low_back(jnp.einsum('nshr,srhe->nshe', recv_prob, recv_value, precision=highest).reshape(series.shape)))
    norm_three = layer_norm(norm_two + low_back(product(recv_out, outer[2]) + bias[2, 2]), gains[2], shifts[2])
    return layer_norm(norm_three + feed(norm_three, up_weight[1], up_bias[1], down_weight[1], down_bias[1]), gains[3], shifts[3])

def reference(tokens, domain, counts, domain_mean, domain_scale, attn_inner, attn_outer, attn_bias, mlp_in, mlp_in_bias, mlp_out, mlp_out_bias, norm_gain, norm_bias, router, cotangent):
    params = (attn_inner.astype(jnp.float32), attn_outer.astype(jnp.float32), attn_bias, mlp_in.astype(jnp.float32), mlp_in_bias, mlp_out.astype(jnp.float32), mlp_out_bias, norm_gain, norm_bias, router.astype(jnp.float32))

    def one_series(carry, item):
        series, label, grad_out = item
        picks = jnp.arange(DOMAINS, dtype=jnp.int32) == label
        offset = lax.optimization_barrier(jnp.sum(jnp.where(picks[:, None], domain_mean, 0.0), axis=0))
        factor = lax.optimization_barrier(jnp.sum(jnp.where(picks[:, None], domain_scale, 0.0), axis=0))
        limit = jnp.sum(jnp.where(picks, counts, 0))
        valid = jnp.arange(NVARS, dtype=jnp.int32) < limit

        def forward(values, weights):
            return series_layer(values, weights, offset, factor, valid)
        result, pull = jax.vjp(forward, series.astype(jnp.float32), params)
        grad_in, grad_params = pull(grad_out.astype(jnp.float32))
        return (jax.tree.map(jnp.add, carry, grad_params), (result, grad_in))
    zeros = jax.tree.map(jnp.zeros_like, params)
    totals, (output, input_grad) = lax.scan(one_series, zeros, (tokens, domain, cotangent))
    return (output, input_grad, totals[0], totals[1], totals[2], totals[3], totals[4], totals[5], totals[6], totals[7], totals[8], totals[9])
```

```python
import functools

import jax
import jax.numpy as jnp
import numpy as np
from jax import lax
from jax.experimental import pallas as pl
from jax.experimental.pallas import tpu as pltpu
from jax.sharding import PartitionSpec as P

HEADS = 8
SLOTS = 16
EPS = 1e-05
MASKED = -1e30
MESH = pl.DeviceIdType.MESH
F32 = jnp.float32
LOW = jnp.bfloat16
VMEM_LIMIT = 56 * 1024 * 1024


def mm(a, b):
    return jnp.dot(a, b, preferred_element_type=F32)


def mm_nt(a, b):
    return lax.dot_general(a, b, (((1,), (1,)), ((), ())), preferred_element_type=F32)


def mm_tn(a, b):
    return lax.dot_general(a, b, (((0,), (0,)), ((), ())), preferred_element_type=F32)


def ln_stats(a):
    mean = jnp.mean(a, axis=1, keepdims=True)
    center = a - mean
    var = jnp.mean(center * center, axis=1, keepdims=True)
    rstd = lax.rsqrt(var + EPS)
    return center * rstd, rstd


def ln_back(g, xhat, rstd, gain):
    gy = g * gain
    first = jnp.mean(gy, axis=1, keepdims=True)
    second = jnp.mean(gy * xhat, axis=1, keepdims=True)
    return rstd * (gy - first - xhat * second)


def gelu_both(z):
    k0 = np.float32(np.sqrt(2.0 / np.pi))
    k1 = np.float32(0.044715)
    square = z * z
    t = jnp.tanh(k0 * z * (1.0 + k1 * square))
    half = 0.5 * (1.0 + t)
    slope = half + 0.5 * z * (1.0 - t * t) * (k0 * (1.0 + 3.0 * k1 * square))
    return z * half, slope


def col_sum(x):
    return jnp.sum(x.astype(F32), axis=0, keepdims=True)


def spread_heads(x, heads_ref):
    return jnp.concatenate([x * heads_ref[h : h + 1, :] for h in range(HEADS)], axis=0)


def gather_heads(x, headsf_ref, rows):
    total = x[:rows] * headsf_ref[0:1, :]
    for h in range(1, HEADS):
        total = total + x[h * rows : (h + 1) * rows] * headsf_ref[h : h + 1, :]
    return total


def first_kernel(
    segs, lvars,
    tok_ref, cot_ref, off_ref, fac_ref, wi_ref, wo_ref, ab_ref, win_ref, bin_ref, wout_ref, bout_ref,
    gain_ref, shift_ref, heads_ref, headsf_ref, perm_ref,
    t2_ref, cots_ref, q_ref, k_ref, v_ref, p_ref, tc_ref, x1_ref, r1_ref, f1_ref, s1_ref, x2_ref, r2_ref,
):
    rows = lvars * segs
    width = tok_ref.shape[-1]
    scale = np.float32((width // HEADS) ** (-0.5))
    cots_ref[0] = mm(perm_ref[...], cot_ref[0].reshape(rows, width)).astype(LOW)
    tok = tok_ref[0].reshape(rows, width).astype(F32)
    start = (tok - off_ref[0]) * fac_ref[0]
    low = start.astype(LOW)
    q_ref[0] = (mm(low, wi_ref[0, 0]) + ab_ref[0, 0:1, :]).astype(LOW)
    k_ref[0] = mm(low, wi_ref[0, 1]).astype(LOW)
    v_ref[0] = (mm(low, wi_ref[0, 2]) + ab_ref[0, 1:2, :]).astype(LOW)
    for v in range(lvars):
        part = slice(v * segs, (v + 1) * segs)
        spread = spread_heads(q_ref[0, part, :], heads_ref)
        scores = mm_nt(k_ref[0, part, :], spread)
        top = jnp.max(scores, axis=0, keepdims=True)
        expo = jnp.exp((scores - top) * scale)
        prob = (expo / jnp.sum(expo, axis=0, keepdims=True)).astype(LOW)
        p_ref[0, part, :] = prob
        tc_ref[0, part, :] = gather_heads(mm_tn(prob, v_ref[0, part, :]), headsf_ref, segs).astype(LOW)
    a1 = start + mm(tc_ref[0], wo_ref[0]) + ab_ref[0, 2:3, :]
    x1, r1 = ln_stats(a1)
    x1_ref[0] = x1.astype(LOW)
    r1_ref[0] = jnp.broadcast_to(r1, (rows, 128))
    t1 = x1 * gain_ref[0:1, :] + shift_ref[0:1, :]
    act, slope = gelu_both(mm(t1.astype(LOW), win_ref[0]) + bin_ref[0:1, :])
    f1_ref[0] = act.astype(LOW)
    s1_ref[0] = slope.astype(LOW)
    a2 = t1 + mm(f1_ref[0], wout_ref[0]) + bout_ref[0:1, :]
    x2, r2 = ln_stats(a2)
    x2_ref[0] = x2.astype(LOW)
    r2_ref[0] = jnp.broadcast_to(r2, (rows, 128))
    t2 = (x2 * gain_ref[1:2, :] + shift_ref[1:2, :]).astype(LOW)
    t2_ref[0] = mm(perm_ref[...], t2).astype(LOW)


B_SQ, B_SK, B_SV, B_RQ, B_RK, B_RV, B_O1, B_O2, B_IN, B_OUT, B_SMALL = [256 * i for i in (0, 1, 2, 3, 4, 5, 6, 7, 8, 10, 12)]
B_ROWS = B_SMALL + 16
C_Q, C_K, C_V, C_O, C_IN, C_OUT, C_SMALL = [256 * i for i in (0, 1, 2, 3, 4, 6, 8)]
C_ROWS = C_SMALL + 16


def second_kernel(
    lsegs, nvars, routers, steps,
    t2_ref, cot_ref, lim_ref, router_ref, wi1_ref, wi2_ref, wo_ref, ab_ref, win_ref, bin_ref, wout_ref, bout_ref,
    gain_ref, shift_ref, mask_ref, grow_ref, shrink_ref, sumr_ref, perm_ref, back_ref,
    out_ref, g_ref, grads_ref, groute_ref,
    qx_ref, kq_ref,
):
    step = pl.program_id(0)
    rows, width = t2_ref.shape[1:]
    lanes = SLOTS * HEADS
    scale = np.float32((width // HEADS) ** (-0.5))

    def expand(x):
        return (mm(grow_ref[...], x).astype(LOW).reshape(-1, 16, width) * mask_ref[...][None]).reshape(-1, width)

    def contract(x):
        return mm(shrink_ref[...], (x.astype(LOW).reshape(-1, 16, width) * mask_ref[...][None]).reshape(-1, width))

    @pl.when(step == 0)
    def _():
        grads_ref[...] = jnp.zeros_like(grads_ref)
        kq_ref[...] = jnp.zeros_like(kq_ref)
        sq = (mm(router_ref[...], wi1_ref[0, 0]) + ab_ref[1, 0:1, :]).astype(LOW)
        qx_ref[...] = expand(sq)

    def per_segment(f):
        return [f(slice(s * nvars, (s + 1) * nvars), slice(s * lanes, (s + 1) * lanes)) for s in range(lsegs)]

    t2 = mm(perm_ref[...], t2_ref[0]).astype(LOW)
    sk = mm(t2, wi1_ref[0, 1]).astype(LOW)
    sv = (mm(t2, wi1_ref[0, 2]) + ab_ref[1, 1:2, :]).astype(LOW)
    rq = (mm(t2, wi2_ref[0, 0]) + ab_ref[2, 0:1, :]).astype(LOW)
    valid = lax.broadcasted_iota(jnp.int32, (nvars, lanes), 0).astype(F32) < lim_ref[0]

    def send_prob(n, l):
        scores = jnp.where(valid, mm_nt(sk[n], qx_ref[l, :]), MASKED)
        top = jnp.max(scores, axis=0, keepdims=True)
        expo = jnp.where(valid, jnp.exp((scores - top) * scale), 0.0)
        return expo / jnp.sum(expo, axis=0, keepdims=True)

    sp = per_segment(send_prob)
    sp_low = [x.astype(LOW) for x in sp]
    pre = contract(jnp.concatenate([mm_tn(sp_low[s], sv[s * nvars : (s + 1) * nvars]) for s in range(lsegs)], axis=0))
    pre_low = pre.astype(LOW)
    buffer = (mm(pre_low, wo_ref[1]) + ab_ref[1, 2:3, :]).astype(LOW)
    rkx = expand(mm(buffer, wi2_ref[0, 1]).astype(LOW))
    rvx = expand((mm(buffer, wi2_ref[0, 2]) + ab_ref[2, 1:2, :]).astype(LOW))
    scores = jnp.concatenate(per_segment(lambda n, l: mm_nt(rq[n], rkx[l])), axis=0)
    real = lax.broadcasted_iota(jnp.int32, (rows, lanes), 1) < routers * HEADS
    scores = jnp.where(real, scores, MASKED)
    top = scores
    shift = lanes // 2
    while shift >= HEADS:
        top = jnp.maximum(top, pltpu.roll(top, shift, 1))
        shift //= 2
    expo = jnp.where(real, jnp.exp((scores - top) * scale), 0.0)
    rp = expo / mm(expo.astype(LOW), sumr_ref[...])
    rp_low = rp.astype(LOW)
    rc = jnp.concatenate(per_segment(lambda n, l: mm(rp_low[n], rvx[l])), axis=0).astype(LOW)
    a3 = t2.astype(F32) + mm(rc, wo_ref[2]) + ab_ref[2, 2:3, :]
    x3, r3 = ln_stats(a3)
    t3 = x3 * gain_ref[2:3, :] + shift_ref[2:3, :]
    t3_low = t3.astype(LOW)
    act, slope = gelu_both(mm(t3_low, win_ref[0]) + bin_ref[1:2, :])
    f2 = act.astype(LOW)
    a4 = t3 + mm(f2, wout_ref[0]) + bout_ref[1:2, :]
    x4, r4 = ln_stats(a4)
    out = (x4 * gain_ref[3:4, :] + shift_ref[3:4, :]).astype(LOW)
    out_ref[0] = mm(back_ref[...], out).astype(LOW)

    def add(row, value):
        grads_ref[row : row + value.shape[0], :] += value

    small = {}
    cot = mm(perm_ref[...], cot_ref[0])
    small[10] = col_sum(cot * x4)
    small[12] = col_sum(cot)
    g4 = ln_back(cot, x4, r4, gain_ref[3:4, :])
    e4 = g4.astype(LOW)
    add(B_OUT, mm_tn(f2, e4))
    small[8] = col_sum(e4)
    e3 = (slope * mm_nt(e4, wout_ref[0])).astype(LOW)
    add(B_IN, mm_tn(t3_low, e3[:, :width]))
    add(B_IN + width, mm_tn(t3_low, e3[:, width:]))
    e3_sum = col_sum(e3)
    small[6] = e3_sum[:, :width]
    small[7] = e3_sum[:, width:]
    g3 = g4 + mm_nt(e3, win_ref[0])
    small[9] = col_sum(g3 * x3)
    small[11] = col_sum(g3)
    g3 = ln_back(g3, x3, r3, gain_ref[2:3, :])
    eo = g3.astype(LOW)
    add(B_O2, mm_tn(rc, eo))
    small[5] = col_sum(eo)
    ec = mm_nt(eo, wo_ref[2]).astype(LOW)
    dp = jnp.concatenate(per_segment(lambda n, l: mm_nt(ec[n], rvx[l])), axis=0)
    ds = (scale * rp * (dp - mm((rp * dp).astype(LOW), sumr_ref[...]))).astype(LOW)
    erq = jnp.concatenate(per_segment(lambda n, l: mm(ds[n], rkx[l])), axis=0).astype(LOW)
    erk = contract(jnp.concatenate(per_segment(lambda n, l: mm_tn(ds[n], rq[n])), axis=0)).astype(LOW)
    erv = contract(jnp.concatenate(per_segment(lambda n, l: mm_tn(rp_low[n], ec[n])), axis=0)).astype(LOW)
    add(B_RQ, mm_tn(t2, erq))
    small[3] = col_sum(erq)
    add(B_RK, mm_tn(buffer, erk))
    add(B_RV, mm_tn(buffer, erv))
    small[4] = col_sum(erv)
    eb = (mm_nt(erk, wi2_ref[0, 1]) + mm_nt(erv, wi2_ref[0, 2])).astype(LOW)
    add(B_O1, mm_tn(pre_low, eb))
    small[2] = col_sum(eb)
    epx = expand(mm_nt(eb, wo_ref[1]).astype(LOW))
    dss = []
    for s in range(lsegs):
        dps = mm_nt(sv[s * nvars : (s + 1) * nvars], epx[s * lanes : (s + 1) * lanes])
        weighted = sp[s] * dps
        center = jnp.sum(weighted, axis=0, keepdims=True)
        dss.append((scale * (weighted - sp[s] * center)).astype(LOW))
    esv = jnp.concatenate([mm(sp_low[s], epx[s * lanes : (s + 1) * lanes]) for s in range(lsegs)], axis=0).astype(LOW)
    esk = jnp.concatenate([mm(dss[s], qx_ref[s * lanes : (s + 1) * lanes, :]) for s in range(lsegs)], axis=0).astype(LOW)
    for s in range(lsegs):
        kq_ref[s * lanes : (s + 1) * lanes, :] += mm_tn(dss[s], sk[s * nvars : (s + 1) * nvars])
    add(B_SK, mm_tn(t2, esk))
    add(B_SV, mm_tn(t2, esv))
    small[1] = col_sum(esv)
    g2 = g3 + mm_nt(erq, wi2_ref[0, 0]) + mm_nt(esk, wi1_ref[0, 1]) + mm_nt(esv, wi1_ref[0, 2])
    g_ref[0] = mm(back_ref[...], g2.astype(LOW)).astype(LOW)
    for row in range(1, 13):
        add(B_SMALL + row, small[row])

    @pl.when(step == steps - 1)
    def _():
        kq = contract(kq_ref[...])
        kq_low = kq.astype(LOW)
        grads_ref[B_SQ : B_SQ + width, :] = mm_tn(router_ref[...], kq_low)
        grads_ref[B_SMALL : B_SMALL + 1, :] = col_sum(kq)
        groute_ref[...] = mm_nt(kq_low, wi1_ref[0, 0])


def third_kernel(
    segs, lvars,
    out_ref, g_ref, tok_ref, off_ref, fac_ref, wi_ref, wo_ref, win_ref, wout_ref, gain_ref, shift_ref,
    heads_ref, headsf_ref, perm_ref,
    q_ref, k_ref, v_ref, p_ref, tc_ref, x1_ref, r1_ref, f1_ref, s1_ref, x2_ref, r2_ref,
    full_ref, gin_ref, grads_ref,
    gq_ref, gk_ref, gv_ref,
):
    step = pl.program_id(0)
    rows, width = g_ref.shape[1:]
    scale = np.float32((width // HEADS) ** (-0.5))

    @pl.when(step == 0)
    def _():
        grads_ref[...] = jnp.zeros_like(grads_ref)

    def add(row, value):
        grads_ref[row : row + value.shape[0], :] += value

    def wide(ref):
        return jnp.concatenate([ref[0]] * (width // 128), axis=1)

    full_ref[0] = mm(perm_ref[...], out_ref[0]).reshape(lvars, segs, width)
    g2 = mm(perm_ref[...], g_ref[0])
    x2 = x2_ref[0].astype(F32)
    add(C_SMALL + 7, col_sum(g2 * x2))
    add(C_SMALL + 9, col_sum(g2))
    g2 = ln_back(g2, x2, wide(r2_ref), gain_ref[1:2, :])
    e2 = g2.astype(LOW)
    add(C_OUT, mm_tn(f1_ref[0], e2))
    add(C_SMALL + 5, col_sum(e2))
    e1 = (s1_ref[0].astype(F32) * mm_nt(e2, wout_ref[0])).astype(LOW)
    x1 = x1_ref[0].astype(F32)
    t1 = (x1 * gain_ref[0:1, :] + shift_ref[0:1, :]).astype(LOW)
    add(C_IN, mm_tn(t1, e1[:, :width]))
    add(C_IN + width, mm_tn(t1, e1[:, width:]))
    e1_sum = col_sum(e1)
    add(C_SMALL + 3, e1_sum[:, :width])
    add(C_SMALL + 4, e1_sum[:, width:])
    g1 = g2 + mm_nt(e1, win_ref[0])
    add(C_SMALL + 6, col_sum(g1 * x1))
    add(C_SMALL + 8, col_sum(g1))
    g1 = ln_back(g1, x1, wide(r1_ref), gain_ref[0:1, :])
    et = g1.astype(LOW)
    add(C_O, mm_tn(tc_ref[0], et))
    add(C_SMALL + 2, col_sum(et))
    etc = mm_nt(et, wo_ref[0]).astype(LOW)
    for v in range(lvars):
        part = slice(v * segs, (v + 1) * segs)
        ex = spread_heads(etc[part], heads_ref)
        prob_low = p_ref[0, part, :]
        prob = prob_low.astype(F32)
        weighted = prob * mm_nt(v_ref[0, part, :], ex)
        ets = (weighted - prob * jnp.sum(weighted, axis=0, keepdims=True)).astype(LOW)
        gv_ref[part, :] = mm(prob_low, ex).astype(LOW)
        gk_ref[part, :] = (scale * mm(ets, spread_heads(q_ref[0, part, :], heads_ref))).astype(LOW)
        gq_ref[part, :] = (scale * gather_heads(mm_tn(ets, k_ref[0, part, :]), headsf_ref, segs)).astype(LOW)
    factor = fac_ref[0]
    low = ((tok_ref[0].reshape(rows, width).astype(F32) - off_ref[0]) * factor).astype(LOW)
    gq = gq_ref[...]
    gk = gk_ref[...]
    gv = gv_ref[...]
    add(C_Q, mm_tn(low, gq))
    add(C_K, mm_tn(low, gk))
    add(C_V, mm_tn(low, gv))
    add(C_SMALL, col_sum(gq))
    add(C_SMALL + 1, col_sum(gv))
    gs = g1 + mm_nt(gq, wi_ref[0, 0]) + mm_nt(gk, wi_ref[0, 1]) + mm_nt(gv, wi_ref[0, 2])
    gin_ref[0] = (gs * factor).reshape(lvars, segs, width)


def reduce_kernel(axes, x_ref, o_ref, acc_ref, send_ref, *scratch):
    recv_refs, sems = scratch[:-4], scratch[-4:]
    scatter_send, scatter_recv, gather_send, gather_recv = sems
    position = {name: index for name, (index, _, _) in axes.items()}
    members = {name: count for name, (_, count, _) in axes.items()}
    total = x_ref.shape[0]
    half = total // 2
    barrier = pltpu.get_barrier_semaphore()
    greeted = 0
    for name, (index, count, target) in axes.items():
        for k in range(1, count):
            pl.semaphore_signal(barrier, inc=1, device_id=target(lax.rem(index + k, count)), device_id_type=MESH)
            greeted += 1
    pl.semaphore_wait(barrier, greeted)
    acc_ref[...] = x_ref[...]
    names = [name for name in axes if members[name] > 1]
    orders = [names, names[:1] + [names[2], names[1]] + names[3:]] if len(names) == 4 else [names, names]
    starts = [jnp.int32(0), jnp.int32(half)]
    sizes = [half, half]
    slot = 0
    plan = [[], []]
    counter = 0
    for level in range(len(names)):
        waits = [[], []]
        for part in range(2):
            name = orders[part][level]
            index, count, target = axes[name]
            size = sizes[part] // count
            recv = recv_refs[part * len(names) + level]
            for k in range(1, count):
                peer = lax.rem(index + k, count)
                begin = pl.multiple_of(starts[part] + peer * size, 16)
                send_ref[pl.ds(begin, size), :] = acc_ref[pl.ds(begin, size), :].astype(LOW)
                copy = pltpu.make_async_remote_copy(
                    src_ref=send_ref.at[pl.ds(begin, size), :],
                    dst_ref=recv.at[k - 1],
                    send_sem=scatter_send.at[counter],
                    recv_sem=scatter_recv.at[counter],
                    device_id=target(peer),
                    device_id_type=MESH,
                )
                copy.start()
                waits[part].append(copy)
                counter += 1
        for part in range(2):
            name = orders[part][level]
            index, count, target = axes[name]
            size = sizes[part] // count
            recv = recv_refs[part * len(names) + level]
            mine = pl.multiple_of(starts[part] + index * size, 16)
            for copy in waits[part]:
                copy.wait()
            value = acc_ref[pl.ds(mine, size), :]
            for k in range(1, count):
                value = value + recv[k - 1].astype(F32)
            acc_ref[pl.ds(mine, size), :] = value
            plan[part].append((name, starts[part], size))
            starts[part] = mine
            sizes[part] = size
    for part in range(2):
        own = pl.ds(pl.multiple_of(starts[part], 16), sizes[part])
        o_ref[own, :] = acc_ref[own, :].astype(LOW)
    counter = 0
    for level in reversed(range(len(names))):
        copies = []
        for part in range(2):
            name, base, size = plan[part][level]
            index, count, target = axes[name]
            own = pl.ds(pl.multiple_of(base + index * size, 16), size)
            for k in range(1, count):
                copy = pltpu.make_async_remote_copy(
                    src_ref=o_ref.at[own, :],
                    dst_ref=o_ref.at[own, :],
                    send_sem=gather_send.at[counter],
                    recv_sem=gather_recv.at[counter],
                    device_id=target(lax.rem(index + k, count)),
                    device_id_type=MESH,
                )
                copy.start()
                copies.append(copy)
                counter += 1
        for copy in copies:
            copy.wait()


def all_reduce(x, var_size, seg_size, collective_id):
    cores = 2 if seg_size % 2 == 0 else 1
    xs = seg_size // cores
    ys = xs if var_size % xs == 0 else 1
    zs = var_size // ys
    devices = var_size * seg_size
    rows, width = x.shape
    quantum = 2 * 16 * devices
    padded = -(-rows // quantum) * quantum
    x = jnp.pad(x, ((0, padded - rows), (0, 0)))
    counts = {"core": cores, "x": xs, "y": ys, "z": zs}

    def kernel(*refs):
        var = lax.axis_index("var")
        seg = lax.axis_index("seg")
        core, xi = lax.rem(seg, cores), lax.div(seg, cores)
        yi, zi = lax.rem(var, ys), lax.div(var, ys)
        axes = {
            "core": (core, cores, lambda i: {"seg": xi * cores + i}),
            "x": (xi, xs, lambda i: {"seg": i * cores + core}),
            "y": (yi, ys, lambda i: {"var": zi * ys + i}),
            "z": (zi, zs, lambda i: {"var": i * ys + yi}),
        }
        reduce_kernel(axes, *refs)

    names = [name for name in counts if counts[name] > 1]
    orders = [names, names[:1] + [names[2], names[1]] + names[3:]] if len(names) == 4 else [names, names]
    recv = []
    for part in range(2):
        size = padded // 2
        for name in orders[part]:
            size //= counts[name]
            recv.append(pltpu.VMEM((counts[name] - 1, size, width), LOW))
    copies = 2 * sum(counts[name] - 1 for name in names)
    out = pl.pallas_call(
        kernel,
        out_shape=jax.ShapeDtypeStruct((padded, width), LOW),
        in_specs=[pl.BlockSpec(memory_space=pltpu.VMEM)],
        out_specs=pl.BlockSpec(memory_space=pltpu.VMEM),
        scratch_shapes=[pltpu.VMEM((padded, width), F32), pltpu.VMEM((padded, width), LOW)]
        + recv
        + [pltpu.SemaphoreType.DMA((copies,))] * 4,
        compiler_params=pltpu.CompilerParams(
            collective_id=collective_id, has_side_effects=True, vmem_limit_bytes=VMEM_LIMIT
        ),
        name="reduce",
    )(x)
    return out[:rows]


def fixed(shape, index=None):
    index = (0,) * len(shape) if index is None else index
    return pl.BlockSpec(shape, lambda b: index)


def stepped(shape):
    return pl.BlockSpec((1,) + shape, lambda b: (b,) + (0,) * len(shape))


def on_device(
    var_size, seg_size,
    tokens, domain, counts, domain_mean, domain_scale, attn_inner, attn_outer, attn_bias,
    mlp_in, mlp_in_bias, mlp_out, mlp_out_bias, norm_gain, norm_bias, router, cotangent,
):
    batch, lvars, segs, width = tokens.shape
    routers = router.shape[1]
    hidden = mlp_in.shape[2]
    lsegs = segs // var_size
    nvars = lvars * var_size
    rows = lvars * segs
    lanes = SLOTS * HEADS
    domains = counts.shape[0]
    me = lax.axis_index("var")

    picks = domain[:, None] == jnp.arange(domains, dtype=jnp.int32)[None, :]
    offset = jnp.sum(jnp.where(picks[:, :, None], domain_mean[None], 0.0), axis=1)[:, None, :]
    factor = jnp.sum(jnp.where(picks[:, :, None], domain_scale[None], 0.0), axis=1)[:, None, :]
    limit = jnp.sum(jnp.where(picks, counts[None, :], 0), axis=1).astype(F32)
    limit = jnp.broadcast_to(limit[:, None, None], (batch, 1, lanes))

    heads = (np.arange(width)[None, :] // (width // HEADS) == np.arange(HEADS)[:, None]).astype(np.float32)
    heads_low = jnp.asarray(heads, LOW)
    heads_f = jnp.asarray(heads, F32)
    mask = jnp.asarray(np.concatenate([heads, heads], axis=0), LOW)
    order = np.arange(rows).reshape(lvars, var_size, lsegs).transpose(1, 0, 2).reshape(-1)
    split = np.eye(rows, dtype=np.float32)[order]
    order = np.arange(rows).reshape(nvars, lsegs).transpose(1, 0).reshape(-1)
    swap = np.eye(rows, dtype=np.float32)[order]
    group = np.arange(lsegs * lanes) // HEADS
    grow = (group[:, None] == np.arange(lsegs * SLOTS)[None, :]).astype(np.float32)
    sumr = (np.arange(lanes)[:, None] % HEADS == np.arange(lanes)[None, :] % HEADS).astype(np.float32)

    params = pltpu.CompilerParams(dimension_semantics=("arbitrary",), vmem_limit_bytes=VMEM_LIMIT)
    kept = [
        ((rows, width), LOW), ((rows, width), LOW), ((rows, width), LOW), ((rows, HEADS * segs), LOW),
        ((rows, width), LOW), ((rows, width), LOW), ((rows, 128), F32), ((rows, hidden), LOW),
        ((rows, hidden), LOW), ((rows, width), LOW), ((rows, 128), F32),
    ]
    whole = lambda x: fixed(x.shape)
    series = stepped((lvars, segs, width))
    plane = stepped((rows, width))
    inner0 = fixed((1,) + attn_inner.shape[1:])
    outer0 = fixed((1,) + attn_outer.shape[1:])
    up0 = fixed((1,) + mlp_in.shape[1:])
    down0 = fixed((1,) + mlp_out.shape[1:])
    row_spec = stepped((1, width))
    split_low = jnp.asarray(split, LOW)
    t2, cot, *residuals = pl.pallas_call(
        functools.partial(first_kernel, segs, lvars),
        grid=(batch,),
        in_specs=[
            series, series, row_spec, row_spec, inner0, outer0, whole(attn_bias), up0, whole(mlp_in_bias), down0,
            whole(mlp_out_bias), whole(norm_gain), whole(norm_bias), whole(heads_low), whole(heads_f), whole(split_low),
        ],
        out_specs=[plane, plane] + [stepped(shape) for shape, _ in kept],
        out_shape=[jax.ShapeDtypeStruct((batch, rows, width), LOW)] * 2
        + [jax.ShapeDtypeStruct((batch,) + shape, dtype) for shape, dtype in kept],
        compiler_params=params,
        name="time_forward",
    )(
        tokens, cotangent, offset, factor, attn_inner, attn_outer, attn_bias, mlp_in, mlp_in_bias, mlp_out,
        mlp_out_bias, norm_gain, norm_bias, heads_low, heads_f, split_low,
    )

    def exchange(x):
        parts = x.reshape(batch, var_size, rows // var_size, width)
        return lax.all_to_all(parts, "var", 1, 1, tiled=True).reshape(batch, rows, width)

    t2 = exchange(t2)
    cot = exchange(cot)
    mine = lax.dynamic_slice_in_dim(router, me * lsegs, lsegs, 0)
    mine = jnp.pad(mine, ((0, 0), (0, SLOTS - routers), (0, 0))).reshape(lsegs * SLOTS, width)
    inner1 = fixed((1,) + attn_inner.shape[1:], (1, 0, 0, 0))
    inner2 = fixed((1,) + attn_inner.shape[1:], (2, 0, 0, 0))
    up1 = fixed((1,) + mlp_in.shape[1:], (1, 0, 0))
    down1 = fixed((1,) + mlp_out.shape[1:], (1, 0, 0))
    consts = [mask, jnp.asarray(grow, LOW), jnp.asarray(grow.T, LOW), jnp.asarray(sumr, LOW), jnp.asarray(swap, LOW), jnp.asarray(swap.T, LOW)]
    out, g2, grads_b, groute = pl.pallas_call(
        functools.partial(second_kernel, lsegs, nvars, routers, batch),
        grid=(batch,),
        in_specs=[
            plane, plane, stepped((1, lanes)), whole(mine), inner1, inner2, whole(attn_outer), whole(attn_bias), up1,
            whole(mlp_in_bias), down1, whole(mlp_out_bias), whole(norm_gain), whole(norm_bias),
        ]
        + [whole(c) for c in consts],
        out_specs=[plane, plane, fixed((B_ROWS, width)), fixed((lsegs * SLOTS, width))],
        out_shape=[
            jax.ShapeDtypeStruct((batch, rows, width), LOW),
            jax.ShapeDtypeStruct((batch, rows, width), LOW),
            jax.ShapeDtypeStruct((B_ROWS, width), F32),
            jax.ShapeDtypeStruct((lsegs * SLOTS, width), F32),
        ],
        scratch_shapes=[pltpu.VMEM((lsegs * lanes, width), LOW), pltpu.VMEM((lsegs * lanes, width), F32)],
        compiler_params=params,
        name="router_part",
    )(
        t2, cot, limit, mine, attn_inner, attn_inner, attn_outer, attn_bias, mlp_in, mlp_in_bias, mlp_out,
        mlp_out_bias, norm_gain, norm_bias, *consts,
    )
    g2 = exchange(g2)
    out = exchange(out)
    join_low = jnp.asarray(split.T, LOW)
    output, input_grad, grads_c = pl.pallas_call(
        functools.partial(third_kernel, segs, lvars),
        grid=(batch,),
        in_specs=[
            plane, plane, series, row_spec, row_spec, inner0, outer0, up0, down0, whole(norm_gain), whole(norm_bias),
            whole(heads_low), whole(heads_f), whole(join_low),
        ]
        + [stepped(shape) for shape, _ in kept],
        out_specs=[series, series, fixed((C_ROWS, width))],
        out_shape=[
            jax.ShapeDtypeStruct(tokens.shape, F32),
            jax.ShapeDtypeStruct(tokens.shape, F32),
            jax.ShapeDtypeStruct((C_ROWS, width), F32),
        ],
        scratch_shapes=[pltpu.VMEM((rows, width), LOW)] * 3,
        compiler_params=params,
        name="time_backward",
    )(
        out, g2, tokens, offset, factor, attn_inner, attn_outer, mlp_in, mlp_out, norm_gain, norm_bias,
        heads_low, heads_f, join_low, *residuals,
    )

    groute = groute.reshape(lsegs, SLOTS, width)[:, :routers]
    routes = lax.dynamic_update_slice_in_dim(jnp.zeros(router.shape, F32), groute, me * lsegs, 0)
    routes = routes.reshape(-1, width)
    sums = all_reduce(jnp.concatenate([grads_b, grads_c, routes], axis=0), var_size, seg_size, 1).astype(F32)
    gb, gc, gr = sums[:B_ROWS], sums[B_ROWS : B_ROWS + C_ROWS], sums[B_ROWS + C_ROWS :]
    grad_inner = jnp.concatenate([gc[: 3 * width], gb[: 6 * width]], axis=0).reshape(attn_inner.shape)
    grad_outer = jnp.concatenate([gc[C_O : C_O + width], gb[B_O1 : B_O1 + 2 * width]], axis=0).reshape(attn_outer.shape)
    bs, cs = gb[B_SMALL:], gc[C_SMALL:]
    grad_bias = jnp.concatenate([cs[0:3], bs[0:6]], axis=0).reshape(attn_bias.shape)

    def up(x):
        return jnp.concatenate([x[:width], x[width : 2 * width]], axis=1)

    grad_up = jnp.stack([up(gc[C_IN:]), up(gb[B_IN:])])
    grad_up_bias = jnp.stack([cs[3:5].reshape(-1), bs[6:8].reshape(-1)])
    grad_down = jnp.stack([gc[C_OUT : C_OUT + hidden], gb[B_OUT : B_OUT + hidden]])
    grad_down_bias = jnp.stack([cs[5], bs[8]])
    grad_gain = jnp.concatenate([cs[6:8], bs[9:11]], axis=0)
    grad_shift = jnp.concatenate([cs[8:10], bs[11:13]], axis=0)
    return (
        output, input_grad, grad_inner, grad_outer, grad_bias, grad_up, grad_up_bias, grad_down, grad_down_bias,
        grad_gain, grad_shift, gr.reshape(router.shape),
    )


def solution(mesh):
    split = P("seg", "var", None, None)
    in_specs = (split, P("seg")) + (P(),) * 13 + (split,)
    out_specs = (split, split) + (P(),) * 10
    var_size, seg_size = mesh.shape["var"], mesh.shape["seg"]
    return jax.shard_map(
        functools.partial(on_device, var_size, seg_size),
        mesh=mesh, in_specs=in_specs, out_specs=out_specs, check_vma=False,
    )
```

```python
import functools

import jax
import jax.numpy as jnp
import numpy as np
from jax import lax
from jax.experimental import pallas as pl
from jax.experimental.pallas import tpu as pltpu
from jax.sharding import PartitionSpec as P

HEADS = 8
SLOTS = 16
EPS = 1e-05
MASKED = -1e30
MESH = pl.DeviceIdType.MESH
F32 = jnp.float32
LOW = jnp.bfloat16
VMEM_LIMIT = 56 * 1024 * 1024


def mm(a, b):
    return jnp.dot(a, b, preferred_element_type=F32)


def mm_nt(a, b):
    return lax.dot_general(a, b, (((1,), (1,)), ((), ())), preferred_element_type=F32)


def mm_tn(a, b):
    return lax.dot_general(a, b, (((0,), (0,)), ((), ())), preferred_element_type=F32)


def ln_stats(a):
    mean = jnp.mean(a, axis=1, keepdims=True)
    center = a - mean
    var = jnp.mean(center * center, axis=1, keepdims=True)
    rstd = lax.rsqrt(var + EPS)
    return center * rstd, rstd


def ln_back(g, xhat, rstd, gain):
    gy = g * gain
    first = jnp.mean(gy, axis=1, keepdims=True)
    second = jnp.mean(gy * xhat, axis=1, keepdims=True)
    return rstd * (gy - first - xhat * second)


def gelu_both(z):
    k0 = np.float32(np.sqrt(2.0 / np.pi))
    k1 = np.float32(0.044715)
    square = z * z
    t = jnp.tanh(k0 * z * (1.0 + k1 * square))
    half = 0.5 * (1.0 + t)
    slope = half + 0.5 * z * (1.0 - t * t) * (k0 * (1.0 + 3.0 * k1 * square))
    return z * half, slope


def col_sum(x):
    return jnp.sum(x.astype(F32), axis=0, keepdims=True)


def spread_heads(x, heads_ref):
    return jnp.concatenate([x * heads_ref[h : h + 1, :] for h in range(HEADS)], axis=0)


def gather_heads(x, headsf_ref, rows):
    total = x[:rows] * headsf_ref[0:1, :]
    for h in range(1, HEADS):
        total = total + x[h * rows : (h + 1) * rows] * headsf_ref[h : h + 1, :]
    return total


def time_forward(
    lvars, b, tok_ref, off_ref, fac_ref, wi_ref, wo_ref, ab_ref, win_ref, bin_ref, wout_ref, bout_ref,
    gain_ref, shift_ref, heads_ref, headsf_ref, kept,
):
    q_ref, k_ref, v_ref, p_ref, tc_ref, x1_ref, r1_ref, f1_ref, s1_ref, x2_ref, r2_ref = kept
    segs, width = tok_ref.shape[2:]
    rows = lvars * segs
    scale = np.float32((width // HEADS) ** (-0.5))
    tok = tok_ref[0].reshape(rows, width).astype(F32)
    start = (tok - off_ref[0]) * fac_ref[0]
    low = start.astype(LOW)
    q_ref[b] = (mm(low, wi_ref[0, 0]) + ab_ref[0, 0:1, :]).astype(LOW)
    k_ref[b] = mm(low, wi_ref[0, 1]).astype(LOW)
    v_ref[b] = (mm(low, wi_ref[0, 2]) + ab_ref[0, 1:2, :]).astype(LOW)
    for v in range(lvars):
        part = slice(v * segs, (v + 1) * segs)
        spread = spread_heads(q_ref[b, part, :], heads_ref)
        scores = mm_nt(k_ref[b, part, :], spread)
        top = jnp.max(scores, axis=0, keepdims=True)
        expo = jnp.exp((scores - top) * scale)
        prob = (expo / jnp.sum(expo, axis=0, keepdims=True)).astype(LOW)
        p_ref[b, part, :] = prob
        tc_ref[b, part, :] = gather_heads(mm_tn(prob, v_ref[b, part, :]), headsf_ref, segs).astype(LOW)
    a1 = start + mm(tc_ref[b], wo_ref[0]) + ab_ref[0, 2:3, :]
    x1, r1 = ln_stats(a1)
    x1_ref[b] = x1.astype(LOW)
    r1_ref[b] = jnp.broadcast_to(r1, (rows, 128))
    t1 = x1 * gain_ref[0:1, :] + shift_ref[0:1, :]
    act, slope = gelu_both(mm(t1.astype(LOW), win_ref[0]) + bin_ref[0:1, :])
    f1_ref[b] = act.astype(LOW)
    s1_ref[b] = slope.astype(LOW)
    a2 = t1 + mm(f1_ref[b], wout_ref[0]) + bout_ref[0:1, :]
    x2, r2 = ln_stats(a2)
    x2_ref[b] = x2.astype(LOW)
    r2_ref[b] = jnp.broadcast_to(r2, (rows, 128))
    return (x2 * gain_ref[1:2, :] + shift_ref[1:2, :]).astype(LOW)


B_SQ, B_SK, B_SV, B_RQ, B_RK, B_RV, B_O1, B_O2, B_IN, B_OUT, B_SMALL = [256 * i for i in (0, 1, 2, 3, 4, 5, 6, 7, 8, 10, 12)]
B_ROWS = B_SMALL + 16
C_Q, C_K, C_V, C_O, C_IN, C_OUT, C_SMALL = [256 * i for i in (0, 1, 2, 3, 4, 6, 8)]
C_ROWS = C_SMALL + 16


def router_part(
    lsegs, nvars, routers, steps, b, arrived, leaving,
    lim_ref, router_ref, wi1_ref, wi2_ref, wo_ref, ab_ref, win_ref, bin_ref, wout_ref, bout_ref,
    gain_ref, shift_ref, mask_ref, grow_ref, shrink_ref, sumr_ref, perm_ref, back_ref,
    grads_ref, groute_ref, qx_ref, kq_ref,
):
    rows, width = perm_ref.shape[0], wo_ref.shape[1]
    lanes = SLOTS * HEADS
    scale = np.float32((width // HEADS) ** (-0.5))

    def expand(x):
        return (mm(grow_ref[...], x).astype(LOW).reshape(-1, 16, width) * mask_ref[...][None]).reshape(-1, width)

    def contract(x):
        return mm(shrink_ref[...], (x.astype(LOW).reshape(-1, 16, width) * mask_ref[...][None]).reshape(-1, width))

    @pl.when(b == 0)
    def _():
        grads_ref[...] = jnp.zeros_like(grads_ref)
        kq_ref[...] = jnp.zeros_like(kq_ref)
        sq = (mm(router_ref[...], wi1_ref[0, 0]) + ab_ref[1, 0:1, :]).astype(LOW)
        qx_ref[...] = expand(sq)

    def per_segment(f):
        return [f(slice(s * nvars, (s + 1) * nvars), slice(s * lanes, (s + 1) * lanes)) for s in range(lsegs)]

    t2 = mm(perm_ref[...], arrived(0).reshape(rows, width)).astype(LOW)
    sk = mm(t2, wi1_ref[0, 1]).astype(LOW)
    sv = (mm(t2, wi1_ref[0, 2]) + ab_ref[1, 1:2, :]).astype(LOW)
    rq = (mm(t2, wi2_ref[0, 0]) + ab_ref[2, 0:1, :]).astype(LOW)
    valid = lax.broadcasted_iota(jnp.int32, (nvars, lanes), 0).astype(F32) < lim_ref[b]

    def send_prob(n, l):
        scores = jnp.where(valid, mm_nt(sk[n], qx_ref[l, :]), MASKED)
        top = jnp.max(scores, axis=0, keepdims=True)
        expo = jnp.where(valid, jnp.exp((scores - top) * scale), 0.0)
        return expo / jnp.sum(expo, axis=0, keepdims=True)

    sp = per_segment(send_prob)
    sp_low = [x.astype(LOW) for x in sp]
    pre = contract(jnp.concatenate([mm_tn(sp_low[s], sv[s * nvars : (s + 1) * nvars]) for s in range(lsegs)], axis=0))
    pre_low = pre.astype(LOW)
    buffer = (mm(pre_low, wo_ref[1]) + ab_ref[1, 2:3, :]).astype(LOW)
    rkx = expand(mm(buffer, wi2_ref[0, 1]).astype(LOW))
    rvx = expand((mm(buffer, wi2_ref[0, 2]) + ab_ref[2, 1:2, :]).astype(LOW))
    scores = jnp.concatenate(per_segment(lambda n, l: mm_nt(rq[n], rkx[l])), axis=0)
    real = lax.broadcasted_iota(jnp.int32, (rows, lanes), 1) < routers * HEADS
    scores = jnp.where(real, scores, MASKED)
    top = scores
    shift = lanes // 2
    while shift >= HEADS:
        top = jnp.maximum(top, pltpu.roll(top, shift, 1))
        shift //= 2
    expo = jnp.where(real, jnp.exp((scores - top) * scale), 0.0)
    rp = expo / mm(expo.astype(LOW), sumr_ref[...])
    rp_low = rp.astype(LOW)
    rc = jnp.concatenate(per_segment(lambda n, l: mm(rp_low[n], rvx[l])), axis=0).astype(LOW)
    a3 = t2.astype(F32) + mm(rc, wo_ref[2]) + ab_ref[2, 2:3, :]
    x3, r3 = ln_stats(a3)
    t3 = x3 * gain_ref[2:3, :] + shift_ref[2:3, :]
    t3_low = t3.astype(LOW)
    act, slope = gelu_both(mm(t3_low, win_ref[0]) + bin_ref[1:2, :])
    f2 = act.astype(LOW)
    a4 = t3 + mm(f2, wout_ref[0]) + bout_ref[1:2, :]
    x4, r4 = ln_stats(a4)
    out = (x4 * gain_ref[3:4, :] + shift_ref[3:4, :]).astype(LOW)
    leaving(3, mm(back_ref[...], out).astype(LOW))

    def add(row, value):
        grads_ref[row : row + value.shape[0], :] += value

    small = {}
    cot = mm(perm_ref[...], arrived(1).reshape(rows, width))
    small[10] = col_sum(cot * x4)
    small[12] = col_sum(cot)
    g4 = ln_back(cot, x4, r4, gain_ref[3:4, :])
    e4 = g4.astype(LOW)
    add(B_OUT, mm_tn(f2, e4))
    small[8] = col_sum(e4)
    e3 = (slope * mm_nt(e4, wout_ref[0])).astype(LOW)
    add(B_IN, mm_tn(t3_low, e3[:, :width]))
    add(B_IN + width, mm_tn(t3_low, e3[:, width:]))
    e3_sum = col_sum(e3)
    small[6] = e3_sum[:, :width]
    small[7] = e3_sum[:, width:]
    g3 = g4 + mm_nt(e3, win_ref[0])
    small[9] = col_sum(g3 * x3)
    small[11] = col_sum(g3)
    g3 = ln_back(g3, x3, r3, gain_ref[2:3, :])
    eo = g3.astype(LOW)
    add(B_O2, mm_tn(rc, eo))
    small[5] = col_sum(eo)
    ec = mm_nt(eo, wo_ref[2]).astype(LOW)
    dp = jnp.concatenate(per_segment(lambda n, l: mm_nt(ec[n], rvx[l])), axis=0)
    ds = (scale * rp * (dp - mm((rp * dp).astype(LOW), sumr_ref[...]))).astype(LOW)
    erq = jnp.concatenate(per_segment(lambda n, l: mm(ds[n], rkx[l])), axis=0).astype(LOW)
    erk = contract(jnp.concatenate(per_segment(lambda n, l: mm_tn(ds[n], rq[n])), axis=0)).astype(LOW)
    erv = contract(jnp.concatenate(per_segment(lambda n, l: mm_tn(rp_low[n], ec[n])), axis=0)).astype(LOW)
    add(B_RQ, mm_tn(t2, erq))
    small[3] = col_sum(erq)
    add(B_RK, mm_tn(buffer, erk))
    add(B_RV, mm_tn(buffer, erv))
    small[4] = col_sum(erv)
    eb = (mm_nt(erk, wi2_ref[0, 1]) + mm_nt(erv, wi2_ref[0, 2])).astype(LOW)
    add(B_O1, mm_tn(pre_low, eb))
    small[2] = col_sum(eb)
    epx = expand(mm_nt(eb, wo_ref[1]).astype(LOW))
    dss = []
    for s in range(lsegs):
        dps = mm_nt(sv[s * nvars : (s + 1) * nvars], epx[s * lanes : (s + 1) * lanes])
        weighted = sp[s] * dps
        center = jnp.sum(weighted, axis=0, keepdims=True)
        dss.append((scale * (weighted - sp[s] * center)).astype(LOW))
    esv = jnp.concatenate([mm(sp_low[s], epx[s * lanes : (s + 1) * lanes]) for s in range(lsegs)], axis=0).astype(LOW)
    esk = jnp.concatenate([mm(dss[s], qx_ref[s * lanes : (s + 1) * lanes, :]) for s in range(lsegs)], axis=0).astype(LOW)
    for s in range(lsegs):
        kq_ref[s * lanes : (s + 1) * lanes, :] += mm_tn(dss[s], sk[s * nvars : (s + 1) * nvars])
    add(B_SK, mm_tn(t2, esk))
    add(B_SV, mm_tn(t2, esv))
    small[1] = col_sum(esv)
    g2 = g3 + mm_nt(erq, wi2_ref[0, 0]) + mm_nt(esk, wi1_ref[0, 1]) + mm_nt(esv, wi1_ref[0, 2])
    leaving(2, mm(back_ref[...], g2.astype(LOW)).astype(LOW))
    for row in range(1, 13):
        add(B_SMALL + row, small[row])

    @pl.when(b == steps - 1)
    def _():
        kq = contract(kq_ref[...])
        kq_low = kq.astype(LOW)
        grads_ref[B_SQ : B_SQ + width, :] = mm_tn(router_ref[...], kq_low)
        grads_ref[B_SMALL : B_SMALL + 1, :] = col_sum(kq)
        groute_ref[...] = mm_nt(kq_low, wi1_ref[0, 0])


def time_backward(
    lvars, b, arrived, tok_ref, off_ref, fac_ref, wi_ref, wo_ref, win_ref, wout_ref, gain_ref, shift_ref,
    heads_ref, headsf_ref, perm_ref, kept, gin_ref, grads_ref, gq_ref, gk_ref, gv_ref,
):
    q_ref, k_ref, v_ref, p_ref, tc_ref, x1_ref, r1_ref, f1_ref, s1_ref, x2_ref, r2_ref = kept
    segs, width = tok_ref.shape[2:]
    rows = lvars * segs
    scale = np.float32((width // HEADS) ** (-0.5))

    @pl.when(b == 0)
    def _():
        grads_ref[...] = jnp.zeros_like(grads_ref)

    def add(row, value):
        grads_ref[row : row + value.shape[0], :] += value

    def wide(ref):
        return jnp.concatenate([ref[b]] * (width // 128), axis=1)

    g2 = mm(perm_ref[...], arrived(2).reshape(rows, width))
    x2 = x2_ref[b].astype(F32)
    add(C_SMALL + 7, col_sum(g2 * x2))
    add(C_SMALL + 9, col_sum(g2))
    g2 = ln_back(g2, x2, wide(r2_ref), gain_ref[1:2, :])
    e2 = g2.astype(LOW)
    add(C_OUT, mm_tn(f1_ref[b], e2))
    add(C_SMALL + 5, col_sum(e2))
    e1 = (s1_ref[b].astype(F32) * mm_nt(e2, wout_ref[0])).astype(LOW)
    x1 = x1_ref[b].astype(F32)
    t1 = (x1 * gain_ref[0:1, :] + shift_ref[0:1, :]).astype(LOW)
    add(C_IN, mm_tn(t1, e1[:, :width]))
    add(C_IN + width, mm_tn(t1, e1[:, width:]))
    e1_sum = col_sum(e1)
    add(C_SMALL + 3, e1_sum[:, :width])
    add(C_SMALL + 4, e1_sum[:, width:])
    g1 = g2 + mm_nt(e1, win_ref[0])
    add(C_SMALL + 6, col_sum(g1 * x1))
    add(C_SMALL + 8, col_sum(g1))
    g1 = ln_back(g1, x1, wide(r1_ref), gain_ref[0:1, :])
    et = g1.astype(LOW)
    add(C_O, mm_tn(tc_ref[b], et))
    add(C_SMALL + 2, col_sum(et))
    etc = mm_nt(et, wo_ref[0]).astype(LOW)
    for v in range(lvars):
        part = slice(v * segs, (v + 1) * segs)
        ex = spread_heads(etc[part], heads_ref)
        prob_low = p_ref[b, part, :]
        prob = prob_low.astype(F32)
        weighted = prob * mm_nt(v_ref[b, part, :], ex)
        ets = (weighted - prob * jnp.sum(weighted, axis=0, keepdims=True)).astype(LOW)
        gv_ref[part, :] = mm(prob_low, ex).astype(LOW)
        gk_ref[part, :] = (scale * mm(ets, spread_heads(q_ref[b, part, :], heads_ref))).astype(LOW)
        gq_ref[part, :] = (scale * gather_heads(mm_tn(ets, k_ref[b, part, :]), headsf_ref, segs)).astype(LOW)
    factor = fac_ref[0]
    low = ((tok_ref[0].reshape(rows, width).astype(F32) - off_ref[0]) * factor).astype(LOW)
    gq = gq_ref[...]
    gk = gk_ref[...]
    gv = gv_ref[...]
    add(C_Q, mm_tn(low, gq))
    add(C_K, mm_tn(low, gk))
    add(C_V, mm_tn(low, gv))
    add(C_SMALL, col_sum(gq))
    add(C_SMALL + 1, col_sum(gv))
    gs = g1 + mm_nt(gq, wi_ref[0, 0]) + mm_nt(gk, wi_ref[0, 1]) + mm_nt(gv, wi_ref[0, 2])
    gin_ref[0] = (gs * factor).reshape(lvars, segs, width)


def layer_kernel(
    lvars, lsegs, nvars, routers, steps, var_size,
    tok_ref, cot_ref, off_ref, fac_ref, lim_ref, router_ref, wi0_ref, wi1_ref, wi2_ref, wo_ref, ab_ref,
    win0_ref, win1_ref, bin_ref, wout0_ref, wout1_ref, bout_ref, gain_ref, shift_ref,
    heads_ref, headsf_ref, split_ref, join_ref, mask_ref, grow_ref, shrink_ref, sumr_ref, swap_ref, back_ref,
    out_ref, gin_ref, gradsb_ref, gradsc_ref, groute_ref,
    sent_ref, came_ref, qx_ref, kq_ref, gq_ref, gk_ref, gv_ref, send_sem, recv_sem, *kept,
):
    step = pl.program_id(0)
    me = lax.axis_index("var")
    width = tok_ref.shape[3]
    rows = lvars * tok_ref.shape[2]
    block = rows // var_size

    def place(kind, b, u):
        return came_ref.at[kind, b, u]

    def copy(kind, b, k):
        target = lax.rem(me + k, var_size)
        return pltpu.make_async_remote_copy(
            src_ref=sent_ref.at[kind, b, target],
            dst_ref=place(kind, b, me),
            send_sem=send_sem.at[kind, b],
            recv_sem=recv_sem.at[kind, b],
            device_id={"var": target},
            device_id_type=MESH,
        )

    def whole(kind, b):
        others = pl.ds(0, var_size - 1)
        return pltpu.make_async_remote_copy(
            src_ref=sent_ref.at[kind, b, others],
            dst_ref=came_ref.at[kind, b, others],
            send_sem=send_sem.at[kind, b],
            recv_sem=recv_sem.at[kind, b],
            device_id={"var": lax.rem(me + 1, var_size)},
            device_id_type=MESH,
        )

    def store(kind, b, value):
        value = value.reshape(var_size, block, width)
        sent_ref[kind, b] = value
        place(kind, b, me)[...] = sent_ref[kind, b, me]

    def send(kind, b):
        for k in range(1, var_size):
            copy(kind, b, k).start()

    @pl.when(step < steps)
    def _():
        b = step

        @pl.when(b == 0)
        def _():
            barrier = pltpu.get_barrier_semaphore()
            for k in range(1, var_size):
                pl.semaphore_signal(barrier, inc=1, device_id={"var": lax.rem(me + k, var_size)}, device_id_type=MESH)

        store(1, b, mm(split_ref[...], cot_ref[0].reshape(rows, width)).astype(LOW))
        t2 = time_forward(
            lvars, b, tok_ref, off_ref, fac_ref, wi0_ref, wo_ref, ab_ref, win0_ref, bin_ref, wout0_ref, bout_ref,
            gain_ref, shift_ref, heads_ref, headsf_ref, kept,
        )
        store(0, b, mm(split_ref[...], t2).astype(LOW))

        @pl.when(b == 0)
        def _():
            pl.semaphore_wait(pltpu.get_barrier_semaphore(), var_size - 1)

        send(0, b)
        send(1, b)

    @pl.when((step >= steps) & (step < 2 * steps))
    def _():
        b = step - steps

        def arrived(kind):
            whole(kind, b).wait_recv()
            return came_ref[kind, b]

        def leaving(kind, value):
            store(kind, b, value)
            if kind == 2:
                send(kind, b)

        router_part(
            lsegs, nvars, routers, steps, b, arrived, leaving,
            lim_ref, router_ref, wi1_ref, wi2_ref, wo_ref, ab_ref, win1_ref, bin_ref, wout1_ref, bout_ref,
            gain_ref, shift_ref, mask_ref, grow_ref, shrink_ref, sumr_ref, swap_ref, back_ref,
            gradsb_ref, groute_ref, qx_ref, kq_ref,
        )

    @pl.when(step >= 2 * steps)
    def _():
        b = step - 2 * steps
        send(3, b)

        def arrived(kind):
            whole(kind, b).wait_recv()
            return came_ref[kind, b]

        time_backward(
            lvars, b, arrived, tok_ref, off_ref, fac_ref, wi0_ref, wo_ref, win0_ref, wout0_ref, gain_ref, shift_ref,
            heads_ref, headsf_ref, join_ref, kept, gin_ref, gradsc_ref, gq_ref, gk_ref, gv_ref,
        )

    @pl.when(step == 3 * steps - 1)
    def _():
        for b in range(steps):
            whole(3, b).wait_recv()
            for kind in range(4):
                whole(kind, b).wait_send()
        out_ref[...] = came_ref[3]


def reduce_kernel(axes, x_ref, o_ref, acc_ref, send_ref, *scratch):
    recv_refs, sems = scratch[:-4], scratch[-4:]
    scatter_send, scatter_recv, gather_send, gather_recv = sems
    position = {name: index for name, (index, _, _) in axes.items()}
    members = {name: count for name, (_, count, _) in axes.items()}
    total = x_ref.shape[0]
    half = total // 2
    barrier = pltpu.get_barrier_semaphore()
    greeted = 0
    for name, (index, count, target) in axes.items():
        for k in range(1, count):
            pl.semaphore_signal(barrier, inc=1, device_id=target(lax.rem(index + k, count)), device_id_type=MESH)
            greeted += 1
    pl.semaphore_wait(barrier, greeted)
    acc_ref[...] = x_ref[...]
    names = [name for name in axes if members[name] > 1]
    orders = [names, names[:1] + [names[2], names[1]] + names[3:]] if len(names) == 4 else [names, names]
    starts = [jnp.int32(0), jnp.int32(half)]
    sizes = [half, half]
    slot = 0
    plan = [[], []]
    counter = 0
    for level in range(len(names)):
        waits = [[], []]
        for part in range(2):
            name = orders[part][level]
            index, count, target = axes[name]
            size = sizes[part] // count
            recv = recv_refs[part * len(names) + level]
            for k in range(1, count):
                peer = lax.rem(index + k, count)
                begin = pl.multiple_of(starts[part] + peer * size, 16)
                send_ref[pl.ds(begin, size), :] = acc_ref[pl.ds(begin, size), :].astype(LOW)
                copy = pltpu.make_async_remote_copy(
                    src_ref=send_ref.at[pl.ds(begin, size), :],
                    dst_ref=recv.at[k - 1],
                    send_sem=scatter_send.at[counter],
                    recv_sem=scatter_recv.at[counter],
                    device_id=target(peer),
                    device_id_type=MESH,
                )
                copy.start()
                waits[part].append(copy)
                counter += 1
        for part in range(2):
            name = orders[part][level]
            index, count, target = axes[name]
            size = sizes[part] // count
            recv = recv_refs[part * len(names) + level]
            mine = pl.multiple_of(starts[part] + index * size, 16)
            for copy in waits[part]:
                copy.wait()
            value = acc_ref[pl.ds(mine, size), :]
            for k in range(1, count):
                value = value + recv[k - 1].astype(F32)
            acc_ref[pl.ds(mine, size), :] = value
            plan[part].append((name, starts[part], size))
            starts[part] = mine
            sizes[part] = size
    for part in range(2):
        own = pl.ds(pl.multiple_of(starts[part], 16), sizes[part])
        o_ref[own, :] = acc_ref[own, :].astype(LOW)
    counter = 0
    for level in reversed(range(len(names))):
        copies = []
        for part in range(2):
            name, base, size = plan[part][level]
            index, count, target = axes[name]
            own = pl.ds(pl.multiple_of(base + index * size, 16), size)
            for k in range(1, count):
                copy = pltpu.make_async_remote_copy(
                    src_ref=o_ref.at[own, :],
                    dst_ref=o_ref.at[own, :],
                    send_sem=gather_send.at[counter],
                    recv_sem=gather_recv.at[counter],
                    device_id=target(lax.rem(index + k, count)),
                    device_id_type=MESH,
                )
                copy.start()
                copies.append(copy)
                counter += 1
        for copy in copies:
            copy.wait()


def all_reduce(x, var_size, seg_size, collective_id):
    cores = 2 if seg_size % 2 == 0 else 1
    xs = seg_size // cores
    ys = xs if var_size % xs == 0 else 1
    zs = var_size // ys
    devices = var_size * seg_size
    rows, width = x.shape
    quantum = 2 * 16 * devices
    padded = -(-rows // quantum) * quantum
    x = jnp.pad(x, ((0, padded - rows), (0, 0)))
    counts = {"core": cores, "x": xs, "y": ys, "z": zs}

    def kernel(*refs):
        var = lax.axis_index("var")
        seg = lax.axis_index("seg")
        core, xi = lax.rem(seg, cores), lax.div(seg, cores)
        yi, zi = lax.rem(var, ys), lax.div(var, ys)
        axes = {
            "core": (core, cores, lambda i: {"seg": xi * cores + i}),
            "x": (xi, xs, lambda i: {"seg": i * cores + core}),
            "y": (yi, ys, lambda i: {"var": zi * ys + i}),
            "z": (zi, zs, lambda i: {"var": i * ys + yi}),
        }
        reduce_kernel(axes, *refs)

    names = [name for name in counts if counts[name] > 1]
    orders = [names, names[:1] + [names[2], names[1]] + names[3:]] if len(names) == 4 else [names, names]
    recv = []
    for part in range(2):
        size = padded // 2
        for name in orders[part]:
            size //= counts[name]
            recv.append(pltpu.VMEM((counts[name] - 1, size, width), LOW))
    copies = 2 * sum(counts[name] - 1 for name in names)
    out = pl.pallas_call(
        kernel,
        out_shape=jax.ShapeDtypeStruct((padded, width), LOW),
        in_specs=[pl.BlockSpec(memory_space=pltpu.VMEM)],
        out_specs=pl.BlockSpec(memory_space=pltpu.VMEM),
        scratch_shapes=[pltpu.VMEM((padded, width), F32), pltpu.VMEM((padded, width), LOW)]
        + recv
        + [pltpu.SemaphoreType.DMA((copies,))] * 4,
        compiler_params=pltpu.CompilerParams(
            collective_id=collective_id, has_side_effects=True, vmem_limit_bytes=VMEM_LIMIT
        ),
        name="reduce",
    )(x)
    return out[:rows]


def fixed(shape, index=None):
    index = (0,) * len(shape) if index is None else index
    return pl.BlockSpec(shape, lambda b: index)


def on_device(
    var_size, seg_size,
    tokens, domain, counts, domain_mean, domain_scale, attn_inner, attn_outer, attn_bias,
    mlp_in, mlp_in_bias, mlp_out, mlp_out_bias, norm_gain, norm_bias, router, cotangent,
):
    batch, lvars, segs, width = tokens.shape
    routers = router.shape[1]
    hidden = mlp_in.shape[2]
    lsegs = segs // var_size
    nvars = lvars * var_size
    rows = lvars * segs
    lanes = SLOTS * HEADS
    domains = counts.shape[0]
    me = lax.axis_index("var")

    picks = domain[:, None] == jnp.arange(domains, dtype=jnp.int32)[None, :]
    offset = jnp.sum(jnp.where(picks[:, :, None], domain_mean[None], 0.0), axis=1)[:, None, :]
    factor = jnp.sum(jnp.where(picks[:, :, None], domain_scale[None], 0.0), axis=1)[:, None, :]
    limit = jnp.sum(jnp.where(picks, counts[None, :], 0), axis=1).astype(F32)
    limit = jnp.broadcast_to(limit[:, None, None], (batch, 1, lanes))

    heads = (np.arange(width)[None, :] // (width // HEADS) == np.arange(HEADS)[:, None]).astype(np.float32)
    heads_low = jnp.asarray(heads, LOW)
    heads_f = jnp.asarray(heads, F32)
    mask = jnp.asarray(np.concatenate([heads, heads], axis=0), LOW)
    order = np.arange(rows).reshape(lvars, var_size, lsegs).transpose(1, 0, 2).reshape(-1)
    split = np.eye(rows, dtype=np.float32)[order]
    order = np.arange(rows).reshape(nvars, lsegs).transpose(1, 0).reshape(-1)
    swap = np.eye(rows, dtype=np.float32)[order]
    group = np.arange(lsegs * lanes) // HEADS
    grow = (group[:, None] == np.arange(lsegs * SLOTS)[None, :]).astype(np.float32)
    sumr = (np.arange(lanes)[:, None] % HEADS == np.arange(lanes)[None, :] % HEADS).astype(np.float32)

    kept = [
        ((rows, width), LOW), ((rows, width), LOW), ((rows, width), LOW), ((rows, HEADS * segs), LOW),
        ((rows, width), LOW), ((rows, width), LOW), ((rows, 128), F32), ((rows, hidden), LOW),
        ((rows, hidden), LOW), ((rows, width), LOW), ((rows, 128), F32),
    ]
    mine = lax.dynamic_slice_in_dim(router, me * lsegs, lsegs, 0)
    mine = jnp.pad(mine, ((0, 0), (0, SLOTS - routers), (0, 0))).reshape(lsegs * SLOTS, width)
    inner = [fixed((1,) + attn_inner.shape[1:], (i, 0, 0, 0)) for i in range(3)]
    up0, up1 = [fixed((1,) + mlp_in.shape[1:], (i, 0, 0)) for i in range(2)]
    down0, down1 = [fixed((1,) + mlp_out.shape[1:], (i, 0, 0)) for i in range(2)]
    consts = [jnp.asarray(x, LOW) for x in (split, split.T)] + [mask]
    consts += [jnp.asarray(x, LOW) for x in (grow, grow.T, sumr, swap, swap.T)]

    def first_last(i):
        return jnp.where(i < batch, i, jnp.maximum(i - 2 * batch, 0))

    def first(i):
        return jnp.minimum(i, batch - 1)

    def last(i):
        return jnp.maximum(i - 2 * batch, 0)

    whole = lambda x: fixed(x.shape)
    block = (1, lvars, segs, width)
    row_spec = pl.BlockSpec((1, 1, width), lambda i: (first_last(i), 0, 0))
    arrived, input_grad, grads_b, grads_c, groute = pl.pallas_call(
        functools.partial(layer_kernel, lvars, lsegs, nvars, routers, batch, var_size),
        grid=(3 * batch,),
        in_specs=[
            pl.BlockSpec(block, lambda i: (first_last(i), 0, 0, 0)),
            pl.BlockSpec(block, lambda i: (first(i), 0, 0, 0)),
            row_spec, row_spec, whole(limit), whole(mine), *inner, whole(attn_outer), whole(attn_bias),
            up0, up1, whole(mlp_in_bias), down0, down1, whole(mlp_out_bias), whole(norm_gain), whole(norm_bias),
            whole(heads_low), whole(heads_f),
        ]
        + [whole(c) for c in consts],
        out_specs=[
            fixed((batch, var_size, rows // var_size, width)),
            pl.BlockSpec(block, lambda i: (last(i), 0, 0, 0)),
            fixed((B_ROWS, width)), fixed((C_ROWS, width)), fixed((lsegs * SLOTS, width)),
        ],
        out_shape=[
            jax.ShapeDtypeStruct((batch, var_size, rows // var_size, width), LOW),
            jax.ShapeDtypeStruct(tokens.shape, F32),
            jax.ShapeDtypeStruct((B_ROWS, width), F32),
            jax.ShapeDtypeStruct((C_ROWS, width), F32),
            jax.ShapeDtypeStruct((lsegs * SLOTS, width), F32),
        ],
        scratch_shapes=[
            pltpu.VMEM((4, batch, var_size, rows // var_size, width), LOW),
            pltpu.VMEM((4, batch, var_size, rows // var_size, width), LOW),
            pltpu.VMEM((lsegs * lanes, width), LOW),
            pltpu.VMEM((lsegs * lanes, width), F32),
            *[pltpu.VMEM((rows, width), LOW)] * 3,
            pltpu.SemaphoreType.DMA((4, batch)),
            pltpu.SemaphoreType.DMA((4, batch)),
        ]
        + [pltpu.VMEM((batch,) + shape, dtype) for shape, dtype in kept],
        compiler_params=pltpu.CompilerParams(
            dimension_semantics=("arbitrary",), vmem_limit_bytes=VMEM_LIMIT, collective_id=0, has_side_effects=True
        ),
        name="layer",
    )(
        tokens, cotangent, offset, factor, limit, mine, attn_inner, attn_inner, attn_inner, attn_outer, attn_bias,
        mlp_in, mlp_in, mlp_in_bias, mlp_out, mlp_out, mlp_out_bias, norm_gain, norm_bias, heads_low, heads_f, *consts,
    )
    output = arrived.reshape(batch, var_size, lvars, lsegs, width).transpose(0, 2, 1, 3, 4).reshape(tokens.shape).astype(F32)

    groute = groute.reshape(lsegs, SLOTS, width)[:, :routers]
    routes = lax.dynamic_update_slice_in_dim(jnp.zeros(router.shape, F32), groute, me * lsegs, 0)
    routes = routes.reshape(-1, width)
    sums = all_reduce(jnp.concatenate([grads_b, grads_c, routes], axis=0), var_size, seg_size, 1).astype(F32)
    gb, gc, gr = sums[:B_ROWS], sums[B_ROWS : B_ROWS + C_ROWS], sums[B_ROWS + C_ROWS :]
    grad_inner = jnp.concatenate([gc[: 3 * width], gb[: 6 * width]], axis=0).reshape(attn_inner.shape)
    grad_outer = jnp.concatenate([gc[C_O : C_O + width], gb[B_O1 : B_O1 + 2 * width]], axis=0).reshape(attn_outer.shape)
    bs, cs = gb[B_SMALL:], gc[C_SMALL:]
    grad_bias = jnp.concatenate([cs[0:3], bs[0:6]], axis=0).reshape(attn_bias.shape)

    def up(x):
        return jnp.concatenate([x[:width], x[width : 2 * width]], axis=1)

    grad_up = jnp.stack([up(gc[C_IN:]), up(gb[B_IN:])])
    grad_up_bias = jnp.stack([cs[3:5].reshape(-1), bs[6:8].reshape(-1)])
    grad_down = jnp.stack([gc[C_OUT : C_OUT + hidden], gb[B_OUT : B_OUT + hidden]])
    grad_down_bias = jnp.stack([cs[5], bs[8]])
    grad_gain = jnp.concatenate([cs[6:8], bs[9:11]], axis=0)
    grad_shift = jnp.concatenate([cs[8:10], bs[11:13]], axis=0)
    return (
        output, input_grad, grad_inner, grad_outer, grad_bias, grad_up, grad_up_bias, grad_down, grad_down_bias,
        grad_gain, grad_shift, gr.reshape(router.shape),
    )


def solution(mesh):
    split = P("seg", "var", None, None)
    in_specs = (split, P("seg")) + (P(),) * 13 + (split,)
    out_specs = (split, split) + (P(),) * 10
    var_size, seg_size = mesh.shape["var"], mesh.shape["seg"]
    return jax.shard_map(
        functools.partial(on_device, var_size, seg_size),
        mesh=mesh, in_specs=in_specs, out_specs=out_specs, check_vma=False,
    )
```

```python
import functools

import jax
import jax.numpy as jnp
import numpy as np
from jax import lax
from jax.experimental import pallas as pl
from jax.experimental.pallas import tpu as pltpu
from jax.sharding import PartitionSpec as P

HEADS = 8
SLOTS = 16
EPS = 1e-05
MASKED = -1e30
MESH = pl.DeviceIdType.MESH
F32 = jnp.float32
LOW = jnp.bfloat16
VMEM_LIMIT = 56 * 1024 * 1024


def mm(a, b):
    return jnp.dot(a, b, preferred_element_type=F32)


def mm_nt(a, b):
    return lax.dot_general(a, b, (((1,), (1,)), ((), ())), preferred_element_type=F32)


def mm_tn(a, b):
    return lax.dot_general(a, b, (((0,), (0,)), ((), ())), preferred_element_type=F32)


def ln_stats(a):
    mean = jnp.mean(a, axis=1, keepdims=True)
    center = a - mean
    var = jnp.mean(center * center, axis=1, keepdims=True)
    rstd = lax.rsqrt(var + EPS)
    return center * rstd, rstd


def ln_back(g, xhat, rstd, gain):
    gy = g * gain
    first = jnp.mean(gy, axis=1, keepdims=True)
    second = jnp.mean(gy * xhat, axis=1, keepdims=True)
    return rstd * (gy - first - xhat * second)


def gelu_both(z):
    k0 = np.float32(np.sqrt(2.0 / np.pi))
    k1 = np.float32(0.044715)
    square = z * z
    t = jnp.tanh(k0 * z * (1.0 + k1 * square))
    half = 0.5 * (1.0 + t)
    slope = half + 0.5 * z * (1.0 - t * t) * (k0 * (1.0 + 3.0 * k1 * square))
    return z * half, slope


def col_sum(x):
    return jnp.sum(x.astype(F32), axis=0, keepdims=True)


def spread_heads(x, heads_ref):
    return jnp.concatenate([x * heads_ref[h : h + 1, :] for h in range(HEADS)], axis=0)


def gather_heads(x, headsf_ref, rows):
    total = x[:rows] * headsf_ref[0:1, :]
    for h in range(1, HEADS):
        total = total + x[h * rows : (h + 1) * rows] * headsf_ref[h : h + 1, :]
    return total


def time_forward(
    lvars, b, tok_ref, offset, factor, wi_ref, wo_ref, ab_ref, win_ref, bin_ref, wout_ref, bout_ref,
    gain_ref, shift_ref, heads_ref, headsf_ref, kept,
):
    q_ref, k_ref, v_ref, p_ref, tc_ref, x1_ref, r1_ref, f1_ref, s1_ref, x2_ref, r2_ref = kept
    segs, width = tok_ref.shape[2:]
    rows = lvars * segs
    scale = np.float32((width // HEADS) ** (-0.5))
    tok = tok_ref[0].reshape(rows, width).astype(F32)
    start = (tok - offset) * factor
    low = start.astype(LOW)
    q_ref[b] = (mm(low, wi_ref[0, 0]) + ab_ref[0, 0:1, :]).astype(LOW)
    k_ref[b] = mm(low, wi_ref[0, 1]).astype(LOW)
    v_ref[b] = (mm(low, wi_ref[0, 2]) + ab_ref[0, 1:2, :]).astype(LOW)
    for v in range(lvars):
        part = slice(v * segs, (v + 1) * segs)
        spread = spread_heads(q_ref[b, part, :], heads_ref)
        scores = mm_nt(k_ref[b, part, :], spread)
        top = jnp.max(scores, axis=0, keepdims=True)
        expo = jnp.exp((scores - top) * scale)
        prob = (expo / jnp.sum(expo, axis=0, keepdims=True)).astype(LOW)
        p_ref[b, part, :] = prob
        tc_ref[b, part, :] = gather_heads(mm_tn(prob, v_ref[b, part, :]), headsf_ref, segs).astype(LOW)
    a1 = start + mm(tc_ref[b], wo_ref[0]) + ab_ref[0, 2:3, :]
    x1, r1 = ln_stats(a1)
    x1_ref[b] = x1.astype(LOW)
    r1_ref[b] = jnp.broadcast_to(r1, (rows, 128))
    t1 = x1 * gain_ref[0:1, :] + shift_ref[0:1, :]
    act, slope = gelu_both(mm(t1.astype(LOW), win_ref[0]) + bin_ref[0:1, :])
    f1_ref[b] = act.astype(LOW)
    s1_ref[b] = slope.astype(LOW)
    a2 = t1 + mm(f1_ref[b], wout_ref[0]) + bout_ref[0:1, :]
    x2, r2 = ln_stats(a2)
    x2_ref[b] = x2.astype(LOW)
    r2_ref[b] = jnp.broadcast_to(r2, (rows, 128))
    return (x2 * gain_ref[1:2, :] + shift_ref[1:2, :]).astype(LOW)


B_SQ, B_SK, B_SV, B_RQ, B_RK, B_RV, B_O1, B_O2, B_IN, B_OUT, B_ROUTE = [256 * i for i in (0, 1, 2, 3, 4, 5, 6, 7, 8, 10, 12)]
M_IN, M_OUT, M_ROWS = [256 * i for i in (0, 2, 4)]
T_Q, T_K, T_V, T_O, T_ROWS = [256 * i for i in (0, 1, 2, 3, 4)]
S_BIAS, S_IN, S_OUT, S_GAIN, S_SHIFT, S_ROWS = 0, 9, 13, 15, 19, 32


def router_part(
    lsegs, nvars, routers, steps, b, arrived, leaving,
    limit, router_ref, wi1_ref, wi2_ref, wo_ref, ab_ref, win_ref, bin_ref, wout_ref, bout_ref,
    gain_ref, shift_ref, mask_ref, grow_ref, shrink_ref, sumr_ref, perm_ref, back_ref,
    grads_ref, small_ref, qx_ref, kq_ref, first_route,
):
    rows, width = perm_ref.shape[0], wo_ref.shape[1]
    lanes = SLOTS * HEADS
    scale = np.float32((width // HEADS) ** (-0.5))

    def expand(x):
        return (mm(grow_ref[...], x).astype(LOW).reshape(-1, 16, width) * mask_ref[...][None]).reshape(-1, width)

    def contract(x):
        return mm(shrink_ref[...], (x.astype(LOW).reshape(-1, 16, width) * mask_ref[...][None]).reshape(-1, width))

    @pl.when(b == 0)
    def _():
        grads_ref[...] = jnp.zeros_like(grads_ref)
        kq_ref[...] = jnp.zeros_like(kq_ref)
        sq = (mm(router_ref[...], wi1_ref[0, 0]) + ab_ref[1, 0:1, :]).astype(LOW)
        qx_ref[...] = expand(sq)

    def per_segment(f):
        return [f(slice(s * nvars, (s + 1) * nvars), slice(s * lanes, (s + 1) * lanes)) for s in range(lsegs)]

    t2 = mm(perm_ref[...], arrived(0).reshape(rows, width)).astype(LOW)
    sk = mm(t2, wi1_ref[0, 1]).astype(LOW)
    sv = (mm(t2, wi1_ref[0, 2]) + ab_ref[1, 1:2, :]).astype(LOW)
    rq = (mm(t2, wi2_ref[0, 0]) + ab_ref[2, 0:1, :]).astype(LOW)
    valid = lax.broadcasted_iota(jnp.int32, (nvars, lanes), 0).astype(F32) < limit

    def send_prob(n, l):
        scores = jnp.where(valid, mm_nt(sk[n], qx_ref[l, :]), MASKED)
        top = jnp.max(scores, axis=0, keepdims=True)
        expo = jnp.where(valid, jnp.exp((scores - top) * scale), 0.0)
        return expo / jnp.sum(expo, axis=0, keepdims=True)

    sp = per_segment(send_prob)
    sp_low = [x.astype(LOW) for x in sp]
    pre = contract(jnp.concatenate([mm_tn(sp_low[s], sv[s * nvars : (s + 1) * nvars]) for s in range(lsegs)], axis=0))
    pre_low = pre.astype(LOW)
    buffer = (mm(pre_low, wo_ref[1]) + ab_ref[1, 2:3, :]).astype(LOW)
    rkx = expand(mm(buffer, wi2_ref[0, 1]).astype(LOW))
    rvx = expand((mm(buffer, wi2_ref[0, 2]) + ab_ref[2, 1:2, :]).astype(LOW))
    scores = jnp.concatenate(per_segment(lambda n, l: mm_nt(rq[n], rkx[l])), axis=0)
    real = lax.broadcasted_iota(jnp.int32, (rows, lanes), 1) < routers * HEADS
    scores = jnp.where(real, scores, MASKED)
    top = scores
    shift = lanes // 2
    while shift >= HEADS:
        top = jnp.maximum(top, pltpu.roll(top, shift, 1))
        shift //= 2
    expo = jnp.where(real, jnp.exp((scores - top) * scale), 0.0)
    rp = expo / mm(expo.astype(LOW), sumr_ref[...])
    rp_low = rp.astype(LOW)
    rc = jnp.concatenate(per_segment(lambda n, l: mm(rp_low[n], rvx[l])), axis=0).astype(LOW)
    a3 = t2.astype(F32) + mm(rc, wo_ref[2]) + ab_ref[2, 2:3, :]
    x3, r3 = ln_stats(a3)
    t3 = x3 * gain_ref[2:3, :] + shift_ref[2:3, :]
    t3_low = t3.astype(LOW)
    act, slope = gelu_both(mm(t3_low, win_ref[0]) + bin_ref[1:2, :])
    f2 = act.astype(LOW)
    a4 = t3 + mm(f2, wout_ref[0]) + bout_ref[1:2, :]
    x4, r4 = ln_stats(a4)
    out = (x4 * gain_ref[3:4, :] + shift_ref[3:4, :]).astype(LOW)
    leaving(3, mm(back_ref[...], out).astype(LOW))

    def add(row, value):
        grads_ref[row : row + value.shape[0], :] += value

    def add_small(row, value):
        small_ref[row : row + 1, :] += value

    cot = mm(perm_ref[...], arrived(1).reshape(rows, width))
    add_small(S_GAIN + 3, col_sum(cot * x4))
    add_small(S_SHIFT + 3, col_sum(cot))
    g4 = ln_back(cot, x4, r4, gain_ref[3:4, :])
    e4 = g4.astype(LOW)
    add(B_OUT, mm_tn(f2, e4))
    add_small(S_OUT + 1, col_sum(e4))
    e3 = (slope * mm_nt(e4, wout_ref[0])).astype(LOW)
    add(B_IN, mm_tn(t3_low, e3[:, :width]))
    add(B_IN + width, mm_tn(t3_low, e3[:, width:]))
    e3_sum = col_sum(e3)
    add_small(S_IN + 2, e3_sum[:, :width])
    add_small(S_IN + 3, e3_sum[:, width:])
    g3 = g4 + mm_nt(e3, win_ref[0])
    add_small(S_GAIN + 2, col_sum(g3 * x3))
    add_small(S_SHIFT + 2, col_sum(g3))
    g3 = ln_back(g3, x3, r3, gain_ref[2:3, :])
    eo = g3.astype(LOW)
    add(B_O2, mm_tn(rc, eo))
    add_small(S_BIAS + 8, col_sum(eo))
    ec = mm_nt(eo, wo_ref[2]).astype(LOW)
    dp = jnp.concatenate(per_segment(lambda n, l: mm_nt(ec[n], rvx[l])), axis=0)
    ds = (scale * rp * (dp - mm((rp * dp).astype(LOW), sumr_ref[...]))).astype(LOW)
    erq = jnp.concatenate(per_segment(lambda n, l: mm(ds[n], rkx[l])), axis=0).astype(LOW)
    erk = contract(jnp.concatenate(per_segment(lambda n, l: mm_tn(ds[n], rq[n])), axis=0)).astype(LOW)
    erv = contract(jnp.concatenate(per_segment(lambda n, l: mm_tn(rp_low[n], ec[n])), axis=0)).astype(LOW)
    add(B_RQ, mm_tn(t2, erq))
    add_small(S_BIAS + 6, col_sum(erq))
    add(B_RK, mm_tn(buffer, erk))
    add(B_RV, mm_tn(buffer, erv))
    add_small(S_BIAS + 7, col_sum(erv))
    eb = (mm_nt(erk, wi2_ref[0, 1]) + mm_nt(erv, wi2_ref[0, 2])).astype(LOW)
    add(B_O1, mm_tn(pre_low, eb))
    add_small(S_BIAS + 5, col_sum(eb))
    epx = expand(mm_nt(eb, wo_ref[1]).astype(LOW))
    dss = []
    for s in range(lsegs):
        dps = mm_nt(sv[s * nvars : (s + 1) * nvars], epx[s * lanes : (s + 1) * lanes])
        weighted = sp[s] * dps
        center = jnp.sum(weighted, axis=0, keepdims=True)
        dss.append((scale * (weighted - sp[s] * center)).astype(LOW))
    esv = jnp.concatenate([mm(sp_low[s], epx[s * lanes : (s + 1) * lanes]) for s in range(lsegs)], axis=0).astype(LOW)
    esk = jnp.concatenate([mm(dss[s], qx_ref[s * lanes : (s + 1) * lanes, :]) for s in range(lsegs)], axis=0).astype(LOW)
    for s in range(lsegs):
        kq_ref[s * lanes : (s + 1) * lanes, :] += mm_tn(dss[s], sk[s * nvars : (s + 1) * nvars])
    add(B_SK, mm_tn(t2, esk))
    add(B_SV, mm_tn(t2, esv))
    add_small(S_BIAS + 4, col_sum(esv))
    g2 = g3 + mm_nt(erq, wi2_ref[0, 0]) + mm_nt(esk, wi1_ref[0, 1]) + mm_nt(esv, wi1_ref[0, 2])
    leaving(2, mm(back_ref[...], g2.astype(LOW)).astype(LOW))

    @pl.when(b == steps - 1)
    def _():
        kq = contract(kq_ref[...])
        kq_low = kq.astype(LOW)
        grads_ref[B_SQ : B_SQ + width, :] = mm_tn(router_ref[...], kq_low)
        add_small(S_BIAS + 3, col_sum(kq))
        grads_ref[pl.ds(first_route, lsegs * SLOTS), :] = mm_nt(kq_low, wi1_ref[0, 0])


def feed_backward(
    rows, b, arrived, wo_ref, win_ref, wout_ref, gain_ref, shift_ref, perm_ref, kept, feeds_ref, times_ref, small_ref,
    etc_ref, g1_ref,
):
    q_ref, k_ref, v_ref, p_ref, tc_ref, x1_ref, r1_ref, f1_ref, s1_ref, x2_ref, r2_ref = kept
    width = wo_ref.shape[1]

    @pl.when(b == 0)
    def _():
        feeds_ref[...] = jnp.zeros_like(feeds_ref)
        times_ref[...] = jnp.zeros_like(times_ref)

    def add(ref, row, value):
        ref[row : row + value.shape[0], :] += value

    def wide(ref):
        return jnp.concatenate([ref[b]] * (width // 128), axis=1)

    g2 = mm(perm_ref[...], arrived(2).reshape(rows, width))
    x2 = x2_ref[b].astype(F32)
    add(small_ref, S_GAIN + 1, col_sum(g2 * x2))
    add(small_ref, S_SHIFT + 1, col_sum(g2))
    g2 = ln_back(g2, x2, wide(r2_ref), gain_ref[1:2, :])
    e2 = g2.astype(LOW)
    add(feeds_ref, M_OUT, mm_tn(f1_ref[b], e2))
    add(small_ref, S_OUT, col_sum(e2))
    e1 = (s1_ref[b].astype(F32) * mm_nt(e2, wout_ref[0])).astype(LOW)
    x1 = x1_ref[b].astype(F32)
    t1 = (x1 * gain_ref[0:1, :] + shift_ref[0:1, :]).astype(LOW)
    add(feeds_ref, M_IN, mm_tn(t1, e1[:, :width]))
    add(feeds_ref, M_IN + width, mm_tn(t1, e1[:, width:]))
    e1_sum = col_sum(e1)
    add(small_ref, S_IN, e1_sum[:, :width])
    add(small_ref, S_IN + 1, e1_sum[:, width:])
    g1 = g2 + mm_nt(e1, win_ref[0])
    add(small_ref, S_GAIN, col_sum(g1 * x1))
    add(small_ref, S_SHIFT, col_sum(g1))
    g1 = ln_back(g1, x1, wide(r1_ref), gain_ref[0:1, :])
    g1_ref[b] = g1
    et = g1.astype(LOW)
    add(times_ref, T_O, mm_tn(tc_ref[b], et))
    add(small_ref, S_BIAS + 2, col_sum(et))
    etc_ref[b] = mm_nt(et, wo_ref[0]).astype(LOW)


def time_backward(lvars, b, tok_ref, offset, factor, heads_ref, headsf_ref, kept, times_ref, small_ref, etc_ref):
    q_ref, k_ref, v_ref, p_ref = kept[:4]
    segs, width = tok_ref.shape[2:]
    rows = lvars * segs
    scale = np.float32((width // HEADS) ** (-0.5))

    def add(ref, row, value):
        ref[row : row + value.shape[0], :] += value

    for v in range(lvars):
        part = slice(v * segs, (v + 1) * segs)
        ex = spread_heads(etc_ref[b, part, :], heads_ref)
        prob_low = p_ref[b, part, :]
        prob = prob_low.astype(F32)
        weighted = prob * mm_nt(v_ref[b, part, :], ex)
        ets = (weighted - prob * jnp.sum(weighted, axis=0, keepdims=True)).astype(LOW)
        v_ref[b, part, :] = mm(prob_low, ex).astype(LOW)
        gk = (scale * mm(ets, spread_heads(q_ref[b, part, :], heads_ref))).astype(LOW)
        q_ref[b, part, :] = (scale * gather_heads(mm_tn(ets, k_ref[b, part, :]), headsf_ref, segs)).astype(LOW)
        k_ref[b, part, :] = gk
    low = ((tok_ref[0].reshape(rows, width).astype(F32) - offset) * factor).astype(LOW)
    add(times_ref, T_Q, mm_tn(low, q_ref[b]))
    add(times_ref, T_K, mm_tn(low, k_ref[b]))
    add(times_ref, T_V, mm_tn(low, v_ref[b]))
    add(small_ref, S_BIAS, col_sum(q_ref[b]))
    add(small_ref, S_BIAS + 1, col_sum(v_ref[b]))


class Sum:
    def __init__(self, axes, direct, acc, send, total, recv, sems):
        self.axes, self.acc, self.send, self.total, self.recv, self.sems = axes, acc, send, total, recv, sems
        self.direct = direct
        self.plan = []
        half = acc.shape[0] // 2
        for part, order in enumerate(self.orders({name: axis[1] for name, axis in axes.items()})):
            start, size, levels = part * half, half, []
            for depth, name in enumerate(order):
                index, count, _ = axes[name]
                whole = direct and depth == len(order) - 1
                size = size if whole else size // count
                levels.append((name, start, size))
                start = start if whole else start + index * size
            self.plan.append(levels)
        self.levels = len(self.plan[0])
        self.last = 2 * self.levels - (1 if direct else 0)

    @staticmethod
    def orders(counts):
        names = [name for name in counts if counts[name] > 1]
        if len(names) < 4:
            return [names, names]
        return [names, [names[0], names[2], names[1], names[3]]]

    @classmethod
    def scratch(cls, rows, width, counts, direct):
        recv, copies = [], 0
        for order in cls.orders(counts):
            size = rows // 2
            for depth, name in enumerate(order):
                whole = direct and depth == len(order) - 1
                size = size if whole else size // counts[name]
                recv.append(pltpu.VMEM((counts[name] if whole else counts[name] - 1, size, width), LOW))
                copies += counts[name] - 1
        return [
            pltpu.VMEM((rows, width), F32), pltpu.VMEM((rows, width), LOW), pltpu.VMEM((rows, width), LOW),
            *[pltpu.SemaphoreType.DMA((copies,))] * 4, *recv,
        ]

    def rows(self, start, size):
        return pl.ds(start if isinstance(start, int) else pl.multiple_of(start, 16), size)

    def whole(self, level):
        return self.direct and level == self.levels - 1

    def copies(self, level, gather):
        send_sem, recv_sem = self.sems[2:] if gather else self.sems[:2]
        found, counter = [], 0
        for part, levels in enumerate(self.plan):
            for depth, (name, start, size) in enumerate(levels):
                index, count, target = self.axes[name]
                for k in range(1, count):
                    if depth == level:
                        peer = lax.rem(index + k, count)
                        recv = self.recv[part * self.levels + level]
                        if self.whole(level):
                            rows, where = self.rows(start, size), recv.at[index]
                        else:
                            rows = self.rows(start + (index if gather else peer) * size, size)
                            where = self.total.at[rows, :] if gather else recv.at[k - 1]
                        source = self.total if gather else self.send
                        copy = pltpu.make_async_remote_copy(
                            src_ref=source.at[rows, :],
                            dst_ref=where,
                            send_sem=send_sem.at[counter],
                            recv_sem=recv_sem.at[counter],
                            device_id=target(peer),
                            device_id_type=MESH,
                        )
                        found.append((copy, rows))
                    counter += 1
        return found

    def advance(self, turn):
        levels = self.levels
        if 0 < turn <= levels:
            for copy, _ in self.copies(turn - 1, False):
                copy.wait()
            for part, plan in enumerate(self.plan):
                name, start, size = plan[turn - 1]
                index, count, _ = self.axes[name]
                recv = self.recv[part * levels + turn - 1]
                if self.whole(turn - 1):
                    mine = self.rows(start, size)
                    value = recv[0].astype(F32)
                    others = range(1, count)
                else:
                    mine = self.rows(start + index * size, size)
                    value = self.acc[mine, :]
                    others = range(count - 1)
                for k in others:
                    value = value + recv[k].astype(F32)
                if turn < levels:
                    self.acc[mine, :] = value
                else:
                    self.total[mine, :] = value.astype(LOW)
        elif turn > levels:
            for copy, _ in self.copies(self.last - turn, True):
                copy.wait()
        if turn < levels:
            if self.whole(turn):
                for part, plan in enumerate(self.plan):
                    name, start, size = plan[turn]
                    mine = self.rows(start, size)
                    value = self.acc[mine, :].astype(LOW)
                    self.send[mine, :] = value
                    self.recv[part * levels + turn][self.axes[name][0]] = value
            for copy, rows in self.copies(turn, False):
                if not self.whole(turn):
                    self.send[rows, :] = self.acc[rows, :].astype(LOW)
                copy.start()
        elif turn < self.last:
            for copy, _ in self.copies(self.last - 1 - turn, True):
                copy.start()

    @property
    def turns(self):
        return self.last + 1


class SmallSum:
    def __init__(self, acc, sent, recvs, sems, places):
        self.acc, self.sent, self.recvs, self.sems, self.places = acc, sent, recvs, sems, places

    @staticmethod
    def scratch(rows, width, sizes):
        return [
            pltpu.VMEM((rows, width), F32), pltpu.VMEM((len(sizes), rows, width), LOW),
            *[pltpu.VMEM((size, rows, width), LOW) for size in sizes],
            *[pltpu.SemaphoreType.DMA((size,)) for size in sizes for _ in range(2)],
        ]

    def copies(self, stage):
        name, me, size = self.places[stage]
        send_sem, recv_sem = self.sems[2 * stage : 2 * stage + 2]
        return [
            pltpu.make_async_remote_copy(
                src_ref=self.sent.at[stage],
                dst_ref=self.recvs[stage].at[me],
                send_sem=send_sem.at[k],
                recv_sem=recv_sem.at[k],
                device_id={name: lax.rem(me + k, size)},
                device_id_type=MESH,
            )
            for k in range(1, size)
        ]

    def start(self, stage):
        value = self.acc[...].astype(LOW)
        self.sent[stage] = value
        self.recvs[stage][self.places[stage][1]] = value
        for copy in self.copies(stage):
            copy.start()

    def finish(self, stage):
        for copy in self.copies(stage):
            copy.wait()
        value = self.recvs[stage][0].astype(F32)
        for k in range(1, self.places[stage][2]):
            value = value + self.recvs[stage][k].astype(F32)
        self.acc[...] = value


def layer_kernel(
    lvars, lsegs, nvars, routers, steps, var_size, seg_size, counts, directs,
    dom_ref, cnt_ref, tok_ref, cot_ref, mean_ref, scale_ref, router_ref, wi0_ref, wi1_ref, wi2_ref, wo_ref, ab_ref,
    win0_ref, win1_ref, bin_ref, wout0_ref, wout1_ref, bout_ref, gain_ref, shift_ref,
    heads_ref, headsf_ref, split_ref, join_ref, mask_ref, grow_ref, shrink_ref, sumr_ref, swap_ref, back_ref,
    out_ref, gin_ref, small_out_ref, inner_ref, outer_ref, up_ref, down_ref, route_ref,
    sent_ref, came_ref, qx_ref, kq_ref, etc_ref, g1_ref, send_sem, recv_sem, out_sem, *scratch,
):
    step = pl.program_id(0)
    me = lax.axis_index("var")
    seg = lax.axis_index("seg")
    width = tok_ref.shape[3]
    rows = lvars * tok_ref.shape[2]
    block = rows // var_size
    kept, scratch = scratch[:11], scratch[11:]
    cores, xs, ys = counts["core"], counts["x"], counts["y"]
    core, xi = lax.rem(seg, cores), lax.div(seg, cores)
    yi, zi = lax.rem(me, ys), lax.div(me, ys)
    axes = {
        "core": (core, cores, lambda i: {"seg": xi * cores + i}),
        "x": (xi, xs, lambda i: {"seg": i * cores + core}),
        "y": (yi, ys, lambda i: {"var": zi * ys + i}),
        "z": (zi, counts["z"], lambda i: {"var": i * ys + yi}),
    }
    sums = []
    for direct in directs:
        used = 7 + 2 * len([name for name in counts if counts[name] > 1])
        group, scratch = scratch[:used], scratch[used:]
        sums.append(Sum(axes, direct, group[0], group[1], group[2], group[7:], group[3:7]))
    routes, feeds, times = sums
    small = SmallSum(scratch[0], scratch[1], scratch[2:4], scratch[4:8], [("seg", seg, seg_size), ("var", me, var_size)])

    def copy(kind, b, k):
        target = lax.rem(me + k, var_size)
        return pltpu.make_async_remote_copy(
            src_ref=sent_ref.at[kind, b, target],
            dst_ref=came_ref.at[kind, b, me],
            send_sem=send_sem.at[kind, b],
            recv_sem=recv_sem.at[kind, b],
            device_id={"var": target},
            device_id_type=MESH,
        )

    def whole(kind, b):
        others = pl.ds(0, var_size - 1)
        return pltpu.make_async_remote_copy(
            src_ref=sent_ref.at[kind, b, others],
            dst_ref=came_ref.at[kind, b, others],
            send_sem=send_sem.at[kind, b],
            recv_sem=recv_sem.at[kind, b],
            device_id={"var": lax.rem(me + 1, var_size)},
            device_id_type=MESH,
        )

    def store(kind, b, value):
        value = value.reshape(var_size, block, width)
        sent_ref[kind, b] = value
        came_ref[kind, b, me] = sent_ref[kind, b, me]

    def send(kind, b):
        for k in range(1, var_size):
            copy(kind, b, k).start()

    def pick(b, ref):
        total = jnp.zeros((1, width), F32)
        for d in range(ref.shape[0]):
            total = total + jnp.where(dom_ref[b] == d, ref[d : d + 1, :], 0.0)
        return total

    def arrived(kind, b):
        whole(kind, b).wait_recv()
        return came_ref[kind, b]

    pieces = [
        (times, T_Q, 3 * width, inner_ref, 0), (routes, B_SQ, 6 * width, inner_ref, 3 * width),
        (times, T_O, width, outer_ref, 0), (routes, B_O1, 2 * width, outer_ref, width),
        (feeds, M_IN, 2 * width, up_ref, 0), (routes, B_IN, 2 * width, up_ref, 2 * width),
        (feeds, M_OUT, 2 * width, down_ref, 0), (routes, B_OUT, 2 * width, down_ref, 2 * width),
        (routes, B_ROUTE, route_ref.shape[0], route_ref, 0),
    ]

    def deliver(which):
        return [
            pltpu.make_async_copy(
                total.total.at[pl.ds(row, count), :], ref.at[pl.ds(there, count), :], out_sem.at[index]
            )
            for index, (total, row, count, ref, there) in enumerate(pieces)
            if total is which
        ]

    @pl.when(step < steps)
    def _():
        b = step

        @pl.when(b == 0)
        def _():
            barrier = pltpu.get_barrier_semaphore()
            for k in range(1, var_size):
                pl.semaphore_signal(barrier, inc=1, device_id={"var": lax.rem(me + k, var_size)}, device_id_type=MESH)
            for k in range(1, seg_size):
                pl.semaphore_signal(barrier, inc=1, device_id={"seg": lax.rem(seg + k, seg_size)}, device_id_type=MESH)
            small.acc[...] = jnp.zeros_like(small.acc)

        store(1, b, mm(split_ref[...], cot_ref[0].reshape(rows, width)).astype(LOW))
        t2 = time_forward(
            lvars, b, tok_ref, pick(b, mean_ref), pick(b, scale_ref), wi0_ref, wo_ref, ab_ref, win0_ref, bin_ref,
            wout0_ref, bout_ref, gain_ref, shift_ref, heads_ref, headsf_ref, kept,
        )
        store(0, b, mm(split_ref[...], t2).astype(LOW))

        @pl.when(b == 0)
        def _():
            pl.semaphore_wait(pltpu.get_barrier_semaphore(), var_size + seg_size - 2)

        send(0, b)
        send(1, b)

    @pl.when((step >= steps) & (step < 2 * steps))
    def _():
        b = step - steps

        def leaving(kind, value):
            store(kind, b, value)
            if kind == 2:
                send(kind, b)

        limit = jnp.int32(0)
        for d in range(cnt_ref.shape[0]):
            limit = limit + jnp.where(dom_ref[b] == d, cnt_ref[d], 0)
        router_part(
            lsegs, nvars, routers, steps, b, lambda kind: arrived(kind, b), leaving,
            limit, router_ref, wi1_ref, wi2_ref, wo_ref, ab_ref, win1_ref, bin_ref, wout1_ref, bout_ref,
            gain_ref, shift_ref, mask_ref, grow_ref, shrink_ref, sumr_ref, swap_ref, back_ref,
            routes.acc, small.acc, qx_ref, kq_ref, B_ROUTE + me * (lsegs * SLOTS),
        )

    @pl.when((step >= 2 * steps) & (step < 3 * steps))
    def _():
        b = step - 2 * steps
        send(3, b)
        feed_backward(
            rows, b, lambda kind: arrived(kind, b), wo_ref, win0_ref, wout0_ref, gain_ref, shift_ref, join_ref, kept,
            feeds.acc, times.acc, small.acc, etc_ref, g1_ref,
        )

    @pl.when((step >= 3 * steps) & (step < 4 * steps))
    def _():
        b = step - 3 * steps
        time_backward(
            lvars, b, tok_ref, pick(b, mean_ref), pick(b, scale_ref), heads_ref, headsf_ref, kept, times.acc, small.acc,
            etc_ref,
        )

    def at(turn_step, run):
        pl.when(step == turn_step)(run)

    for total, first_step, last_step in ((routes, 2 * steps, 4 * steps), (feeds, 3 * steps, 4 * steps)):
        for turn in range(total.turns):
            at(first_step + (last_step - first_step) * turn // (total.turns - 1), functools.partial(total.advance, turn))
    spread = [min(turn * steps // (times.turns - 1), steps - 1) for turn in range(times.turns)]

    @pl.when(step >= 4 * steps)
    def _():
        b = step - 4 * steps

        @pl.when(b == 0)
        def _():
            small.start(0)
            for total in (routes, feeds):
                for copy in deliver(total):
                    copy.start()

        for turn in range(times.turns - 1):
            pl.when(b == spread[turn])(functools.partial(times.advance, turn))

        @pl.when(b == steps // 2)
        def _():
            small.finish(0)
            small.start(1)

        grad = g1_ref[b] + mm_nt(kept[0][b], wi0_ref[0, 0]) + mm_nt(kept[1][b], wi0_ref[0, 1])
        grad = (grad + mm_nt(kept[2][b], wi0_ref[0, 2])) * pick(b, scale_ref)
        gin_ref[0] = grad.reshape(gin_ref.shape[1:])

    @pl.when(step == 5 * steps - 1)
    def _():
        small.finish(1)
        small_out_ref[...] = small.acc[...]
        for b in range(steps):
            whole(3, b).wait_recv()
            for kind in range(4):
                whole(kind, b).wait_send()
        out_ref[...] = came_ref[3]
        times.advance(times.turns - 1)
        for copy in deliver(times):
            copy.start()
        for total in sums:
            for copy in deliver(total):
                copy.wait()


def finish_kernel(
    width, segs, lvars, out_ref, inner_ref, outer_ref, up_ref, down_ref, route_ref, join_ref,
    output_ref, ginner_ref, gouter_ref, gup_ref, gdown_ref, groute_ref,
):
    routers = groute_ref.shape[1]
    output_ref[0] = mm(join_ref[...], out_ref[0].reshape(lvars * segs, width)).reshape(lvars, segs, width)
    ginner_ref[...] = inner_ref[...].astype(F32)
    gouter_ref[...] = outer_ref[...].astype(F32)
    gup_ref[0, :, :width] = up_ref[0, 0].astype(F32)
    gup_ref[0, :, width:] = up_ref[0, 1].astype(F32)
    gdown_ref[...] = down_ref[...].astype(F32)
    groute_ref[...] = route_ref[...].astype(F32)[:, :routers, :]


def fixed(shape, index=None):
    index = (0,) * len(shape) if index is None else index
    return pl.BlockSpec(shape, lambda b: index)


def on_device(
    var_size, seg_size,
    tokens, domain, counts, domain_mean, domain_scale, attn_inner, attn_outer, attn_bias,
    mlp_in, mlp_in_bias, mlp_out, mlp_out_bias, norm_gain, norm_bias, router, cotangent,
):
    batch, lvars, segs, width = tokens.shape
    routers = router.shape[1]
    hidden = mlp_in.shape[2]
    lsegs = segs // var_size
    nvars = lvars * var_size
    rows = lvars * segs
    lanes = SLOTS * HEADS
    me = lax.axis_index("var")

    heads = (np.arange(width)[None, :] // (width // HEADS) == np.arange(HEADS)[:, None]).astype(np.float32)
    heads_low = jnp.asarray(heads, LOW)
    heads_f = jnp.asarray(heads, F32)
    mask = jnp.asarray(np.concatenate([heads, heads], axis=0), LOW)
    order = np.arange(rows).reshape(lvars, var_size, lsegs).transpose(1, 0, 2).reshape(-1)
    split = np.eye(rows, dtype=np.float32)[order]
    order = np.arange(rows).reshape(nvars, lsegs).transpose(1, 0).reshape(-1)
    swap = np.eye(rows, dtype=np.float32)[order]
    group = np.arange(lsegs * lanes) // HEADS
    grow = (group[:, None] == np.arange(lsegs * SLOTS)[None, :]).astype(np.float32)
    sumr = (np.arange(lanes)[:, None] % HEADS == np.arange(lanes)[None, :] % HEADS).astype(np.float32)

    kept = [
        ((rows, width), LOW), ((rows, width), LOW), ((rows, width), LOW), ((rows, HEADS * segs), LOW),
        ((rows, width), LOW), ((rows, width), LOW), ((rows, 128), F32), ((rows, hidden), LOW),
        ((rows, hidden), LOW), ((rows, width), LOW), ((rows, 128), F32),
    ]
    mine = lax.dynamic_slice_in_dim(router, me * lsegs, lsegs, 0)
    mine = jnp.pad(mine, ((0, 0), (0, SLOTS - routers), (0, 0))).reshape(lsegs * SLOTS, width)
    inner = [fixed((1,) + attn_inner.shape[1:], (i, 0, 0, 0)) for i in range(3)]
    up0, up1 = [fixed((1,) + mlp_in.shape[1:], (i, 0, 0)) for i in range(2)]
    down0, down1 = [fixed((1,) + mlp_out.shape[1:], (i, 0, 0)) for i in range(2)]
    consts = [jnp.asarray(x, LOW) for x in (split, split.T)] + [mask]
    consts += [jnp.asarray(x, LOW) for x in (grow, grow.T, sumr, swap, swap.T)]

    def first_third(i):
        return jnp.where(i < batch, i, jnp.clip(i - 3 * batch, 0, batch - 1))

    def first(i):
        return jnp.minimum(i, batch - 1)

    def last(i):
        return jnp.clip(i - 4 * batch, 0, batch - 1)

    cores = 2 if seg_size % 2 == 0 else 1
    xs = seg_size // cores
    ys = xs if var_size % xs == 0 else 1
    sizes = {"core": cores, "x": xs, "y": ys, "z": var_size // ys}
    directs = [var_size * seg_size > 32] * 3
    quantum = 32 * var_size * seg_size
    sum_rows = []
    for count, direct in zip((B_ROUTE + segs * SLOTS, M_ROWS, T_ROWS), directs):
        unit = quantum // sizes["z"] if direct else quantum
        sum_rows.append(-(-count // unit) * unit)
    whole = lambda x: fixed(x.shape)
    scalars = pl.BlockSpec(memory_space=pltpu.SMEM)
    anywhere = pl.BlockSpec(memory_space=pl.ANY)
    block = (1, lvars, segs, width)
    out_shapes = [
        jax.ShapeDtypeStruct((batch, var_size, rows // var_size, width), LOW),
        jax.ShapeDtypeStruct(tokens.shape, F32),
        jax.ShapeDtypeStruct((S_ROWS, width), F32),
        jax.ShapeDtypeStruct((9 * width, width), LOW),
        jax.ShapeDtypeStruct((3 * width, width), LOW),
        jax.ShapeDtypeStruct((4 * width, width), LOW),
        jax.ShapeDtypeStruct((2 * hidden, width), LOW),
        jax.ShapeDtypeStruct((segs * SLOTS, width), LOW),
    ]
    arrived, input_grad, small, inner_low, outer_low, up_low, down_low, route_low = pl.pallas_call(
        functools.partial(layer_kernel, lvars, lsegs, nvars, routers, batch, var_size, seg_size, sizes, directs),
        grid=(5 * batch,),
        in_specs=[
            scalars, scalars,
            pl.BlockSpec(block, lambda i: (first_third(i), 0, 0, 0)),
            pl.BlockSpec(block, lambda i: (first(i), 0, 0, 0)),
            whole(domain_mean), whole(domain_scale), whole(mine), *inner, whole(attn_outer), whole(attn_bias),
            up0, up1, whole(mlp_in_bias), down0, down1, whole(mlp_out_bias), whole(norm_gain), whole(norm_bias),
            whole(heads_low), whole(heads_f),
        ]
        + [whole(c) for c in consts],
        out_specs=[
            whole(out_shapes[0]),
            pl.BlockSpec(block, lambda i: (last(i), 0, 0, 0)),
            whole(out_shapes[2]),
            *[anywhere] * 5,
        ],
        out_shape=out_shapes,
        scratch_shapes=[
            pltpu.VMEM((4, batch, var_size, rows // var_size, width), LOW),
            pltpu.VMEM((4, batch, var_size, rows // var_size, width), LOW),
            pltpu.VMEM((lsegs * lanes, width), LOW),
            pltpu.VMEM((lsegs * lanes, width), F32),
            pltpu.VMEM((batch, rows, width), LOW),
            pltpu.VMEM((batch, rows, width), F32),
            pltpu.SemaphoreType.DMA((4, batch)),
            pltpu.SemaphoreType.DMA((4, batch)),
            pltpu.SemaphoreType.DMA((9,)),
            *[pltpu.VMEM((batch,) + shape, dtype) for shape, dtype in kept],
            *[x for count, direct in zip(sum_rows, directs) for x in Sum.scratch(count, width, sizes, direct)],
            *SmallSum.scratch(S_ROWS, width, (seg_size, var_size)),
        ],
        compiler_params=pltpu.CompilerParams(
            dimension_semantics=("arbitrary",), vmem_limit_bytes=VMEM_LIMIT, collective_id=0, has_side_effects=True
        ),
        name="layer",
    )(
        domain, counts, tokens, cotangent, domain_mean, domain_scale, mine, attn_inner, attn_inner, attn_inner,
        attn_outer, attn_bias, mlp_in, mlp_in, mlp_in_bias, mlp_out, mlp_out, mlp_out_bias, norm_gain, norm_bias,
        heads_low, heads_f, *consts,
    )

    def shares(*shape):
        shape = (shape[0] // batch,) + shape[1:]
        return pl.BlockSpec(shape, lambda i: (i,) + (0,) * (len(shape) - 1))

    quarter = width * 2 // batch
    per = batch // 2
    output, grad_inner, grad_outer, grad_up, grad_down, grad_router = pl.pallas_call(
        functools.partial(finish_kernel, width, segs, lvars),
        grid=(batch,),
        in_specs=[
            shares(batch, var_size, rows // var_size, width),
            shares(*inner_low.shape), shares(*outer_low.shape),
            pl.BlockSpec((1, 2, quarter, width), lambda i: (i // per, 0, i % per, 0)),
            shares(*down_low.shape), shares(segs, SLOTS, width), whole(consts[1]),
        ],
        out_specs=[
            pl.BlockSpec(block, lambda i: (i, 0, 0, 0)),
            shares(*inner_low.shape), shares(*outer_low.shape),
            pl.BlockSpec((1, quarter, hidden), lambda i: (i // per, i % per, 0)),
            shares(*down_low.shape), shares(*router.shape),
        ],
        out_shape=[
            jax.ShapeDtypeStruct(tokens.shape, F32),
            jax.ShapeDtypeStruct(inner_low.shape, F32),
            jax.ShapeDtypeStruct(outer_low.shape, F32),
            jax.ShapeDtypeStruct(mlp_in.shape, F32),
            jax.ShapeDtypeStruct(down_low.shape, F32),
            jax.ShapeDtypeStruct(router.shape, F32),
        ],
        compiler_params=pltpu.CompilerParams(dimension_semantics=("arbitrary",), vmem_limit_bytes=VMEM_LIMIT),
        name="finish",
    )(
        arrived, inner_low, outer_low, up_low.reshape(2, 2, width, width), down_low,
        route_low.reshape(segs, SLOTS, width), consts[1],
    )
    return (
        output, input_grad, grad_inner.reshape(attn_inner.shape), grad_outer.reshape(attn_outer.shape),
        small[S_BIAS : S_BIAS + 9].reshape(attn_bias.shape), grad_up, small[S_IN : S_IN + 4].reshape(mlp_in_bias.shape),
        grad_down.reshape(mlp_out.shape), small[S_OUT : S_OUT + 2], small[S_GAIN : S_GAIN + 4],
        small[S_SHIFT : S_SHIFT + 4], grad_router,
    )


def solution(mesh):
    split = P("seg", "var", None, None)
    in_specs = (split, P("seg")) + (P(),) * 13 + (split,)
    out_specs = (split, split) + (P(),) * 10
    var_size, seg_size = mesh.shape["var"], mesh.shape["seg"]
    return jax.shard_map(
        functools.partial(on_device, var_size, seg_size),
        mesh=mesh, in_specs=in_specs, out_specs=out_specs, check_vma=False,
    )
```

```python
import functools

import jax
import jax.numpy as jnp
import numpy as np
from jax import lax
from jax.experimental import pallas as pl
from jax.experimental.pallas import tpu as pltpu
from jax.sharding import PartitionSpec as P

HEADS = 8
SLOTS = 16
EPS = 1e-05
MASKED = -1e30
MESH = pl.DeviceIdType.MESH
F32 = jnp.float32
LOW = jnp.bfloat16
VMEM_LIMIT = 60 * 1024 * 1024


OUT_ROUNDS = (-7, -6, -5, -4, -3, -2, -1, 0)
ATTN_ROUNDS = (0, 2, 9, 14, 17, 19, 21)
ROUTE_ROUNDS = (1, 3, 12, 16, 18, 20, 22)
FEED_ROUNDS = (9, 11, 16, 18, 20, 22, 24)
TIME_ROUNDS = (16, 17, 19, 22, 23)


def mm(a, b):
    return jnp.dot(a, b, preferred_element_type=F32)


def mm_nt(a, b):
    return lax.dot_general(a, b, (((1,), (1,)), ((), ())), preferred_element_type=F32)


def mm_tn(a, b):
    return lax.dot_general(a, b, (((0,), (0,)), ((), ())), preferred_element_type=F32)


def ln_stats(a):
    mean = jnp.mean(a, axis=1, keepdims=True)
    center = a - mean
    var = jnp.mean(center * center, axis=1, keepdims=True)
    rstd = lax.rsqrt(var + EPS)
    return center * rstd, rstd


def ln_back(g, xhat, rstd, gain):
    gy = g * gain
    first = jnp.mean(gy, axis=1, keepdims=True)
    second = jnp.mean(gy * xhat, axis=1, keepdims=True)
    return rstd * (gy - first - xhat * second)


def gelu_both(z):
    k0 = np.float32(np.sqrt(2.0 / np.pi))
    k1 = np.float32(0.044715)
    square = z * z
    t = jnp.tanh(k0 * z * (1.0 + k1 * square))
    half = 0.5 * (1.0 + t)
    slope = half + 0.5 * z * (1.0 - t * t) * (k0 * (1.0 + 3.0 * k1 * square))
    return z * half, slope


def col_sum(x):
    return jnp.sum(x.astype(F32), axis=0, keepdims=True)


def spread_heads(x, heads_ref):
    return jnp.concatenate([x * heads_ref[h : h + 1, :] for h in range(HEADS)], axis=0)


def gather_heads(x, headsf_ref, rows):
    total = x[:rows] * headsf_ref[0:1, :]
    for h in range(1, HEADS):
        total = total + x[h * rows : (h + 1) * rows] * headsf_ref[h : h + 1, :]
    return total


def time_forward(
    lvars, b, tok_ref, offset, factor, wi_ref, wo_ref, ab_ref, win_ref, bin_ref, wout_ref, bout_ref,
    gain_ref, shift_ref, heads_ref, headsf_ref, kept,
):
    q_ref, k_ref, v_ref, p_ref, tc_ref, x1_ref, r1_ref, f1_ref, s1_ref, x2_ref, r2_ref = kept
    segs, width = tok_ref.shape[2:]
    rows = lvars * segs
    scale = np.float32((width // HEADS) ** (-0.5))
    tok = tok_ref[b].reshape(rows, width).astype(F32)
    start = (tok - offset) * factor
    low = start.astype(LOW)
    q_ref[b] = (mm(low, wi_ref[0, 0]) + ab_ref[0, 0:1, :]).astype(LOW)
    k_ref[b] = mm(low, wi_ref[0, 1]).astype(LOW)
    v_ref[b] = (mm(low, wi_ref[0, 2]) + ab_ref[0, 1:2, :]).astype(LOW)
    for v in range(lvars):
        part = slice(v * segs, (v + 1) * segs)
        spread = spread_heads(q_ref[b, part, :], heads_ref)
        scores = mm_nt(k_ref[b, part, :], spread)
        top = jnp.max(scores, axis=0, keepdims=True)
        expo = jnp.exp((scores - top) * scale)
        prob = (expo / jnp.sum(expo, axis=0, keepdims=True)).astype(LOW)
        p_ref[b, part, :] = prob
        tc_ref[b, part, :] = gather_heads(mm_tn(prob, v_ref[b, part, :]), headsf_ref, segs).astype(LOW)
    a1 = start + mm(tc_ref[b], wo_ref[0]) + ab_ref[0, 2:3, :]
    x1, r1 = ln_stats(a1)
    x1_ref[b] = x1.astype(LOW)
    r1_ref[b] = jnp.broadcast_to(r1, (rows, 128))
    t1 = x1 * gain_ref[0:1, :] + shift_ref[0:1, :]
    act, slope = gelu_both(mm(t1.astype(LOW), win_ref[0]) + bin_ref[0:1, :])
    f1_ref[b] = act.astype(LOW)
    s1_ref[b] = slope.astype(LOW)
    a2 = t1 + mm(f1_ref[b], wout_ref[0]) + bout_ref[0:1, :]
    x2, r2 = ln_stats(a2)
    x2_ref[b] = x2.astype(LOW)
    r2_ref[b] = jnp.broadcast_to(r2, (rows, 128))
    return (x2 * gain_ref[1:2, :] + shift_ref[1:2, :]).astype(LOW)


B_SQ, B_SK, B_SV, B_RQ, B_RK, B_RV, B_O1, B_O2, B_ROWS = [256 * i for i in range(9)]
R_IN, R_OUT, R_ROUTE = [256 * i for i in (0, 2, 4)]
M_IN, M_OUT, M_V, M_O, M_ROWS = [256 * i for i in (0, 2, 4, 5, 6)]
T_Q, T_K, T_ROWS = [256 * i for i in (0, 1, 2)]
S_BIAS, S_IN, S_OUT, S_GAIN, S_SHIFT, S_ROWS = 0, 9, 13, 15, 19, 32


def router_part(
    lsegs, nvars, routers, steps, b, arrived, leaving,
    limit, router_ref, wi_ref, wo_ref, ab_ref, win_ref, bin_ref, wout_ref, bout_ref,
    gain_ref, shift_ref, mask_ref, grow_ref, shrink_ref, sumr_ref, perm_ref, back_ref,
    attn_ref, rest_ref, small_ref, qx_ref, kq_ref, first_seg, var_size,
):
    rows, width = perm_ref.shape[0], wo_ref.shape[1]
    lanes = SLOTS * HEADS
    scale = np.float32((width // HEADS) ** (-0.5))

    def expand(x):
        return (mm(grow_ref[...], x).astype(LOW).reshape(-1, 16, width) * mask_ref[...][None]).reshape(-1, width)

    def contract(x):
        return mm(shrink_ref[...], (x.astype(LOW).reshape(-1, 16, width) * mask_ref[...][None]).reshape(-1, width))

    @pl.when(b == 0)
    def _():
        attn_ref[...] = jnp.zeros(attn_ref.shape, F32)
        rest_ref[...] = jnp.zeros(rest_ref.shape, F32)
        kq_ref[...] = jnp.zeros_like(kq_ref)
        sq = (mm(router_ref[...], wi_ref[1, 0]) + ab_ref[1, 0:1, :]).astype(LOW)
        qx_ref[...] = expand(sq)

    def per_segment(f):
        return [f(slice(s * nvars, (s + 1) * nvars), slice(s * lanes, (s + 1) * lanes)) for s in range(lsegs)]

    t2 = mm(perm_ref[...], arrived(0).reshape(rows, width)).astype(LOW)
    sk = mm(t2, wi_ref[1, 1]).astype(LOW)
    sv = (mm(t2, wi_ref[1, 2]) + ab_ref[1, 1:2, :]).astype(LOW)
    rq = (mm(t2, wi_ref[2, 0]) + ab_ref[2, 0:1, :]).astype(LOW)
    valid = lax.broadcasted_iota(jnp.int32, (nvars, lanes), 0).astype(F32) < limit

    def send_prob(n, l):
        scores = jnp.where(valid, mm_nt(sk[n], qx_ref[l, :]), MASKED)
        top = jnp.max(scores, axis=0, keepdims=True)
        expo = jnp.where(valid, jnp.exp((scores - top) * scale), 0.0)
        return expo / jnp.sum(expo, axis=0, keepdims=True)

    sp = per_segment(send_prob)
    sp_low = [x.astype(LOW) for x in sp]
    pre = contract(jnp.concatenate([mm_tn(sp_low[s], sv[s * nvars : (s + 1) * nvars]) for s in range(lsegs)], axis=0))
    pre_low = pre.astype(LOW)
    buffer = (mm(pre_low, wo_ref[1]) + ab_ref[1, 2:3, :]).astype(LOW)
    rkx = expand(mm(buffer, wi_ref[2, 1]).astype(LOW))
    rvx = expand((mm(buffer, wi_ref[2, 2]) + ab_ref[2, 1:2, :]).astype(LOW))
    scores = jnp.concatenate(per_segment(lambda n, l: mm_nt(rq[n], rkx[l])), axis=0)
    real = lax.broadcasted_iota(jnp.int32, (rows, lanes), 1) < routers * HEADS
    scores = jnp.where(real, scores, MASKED)
    top = scores
    shift = lanes // 2
    while shift >= HEADS:
        top = jnp.maximum(top, pltpu.roll(top, shift, 1))
        shift //= 2
    expo = jnp.where(real, jnp.exp((scores - top) * scale), 0.0)
    rp = expo / mm(expo.astype(LOW), sumr_ref[...])
    rp_low = rp.astype(LOW)
    rc = jnp.concatenate(per_segment(lambda n, l: mm(rp_low[n], rvx[l])), axis=0).astype(LOW)
    a3 = t2.astype(F32) + mm(rc, wo_ref[2]) + ab_ref[2, 2:3, :]
    x3, r3 = ln_stats(a3)
    t3 = x3 * gain_ref[2:3, :] + shift_ref[2:3, :]
    t3_low = t3.astype(LOW)
    act, slope = gelu_both(mm(t3_low, win_ref[1]) + bin_ref[1:2, :])
    f2 = act.astype(LOW)
    a4 = t3 + mm(f2, wout_ref[1]) + bout_ref[1:2, :]
    x4, r4 = ln_stats(a4)
    out = (x4 * gain_ref[3:4, :] + shift_ref[3:4, :]).astype(LOW)
    leaving(3, mm(back_ref[...], out).astype(LOW))

    def add(row, value, ref=attn_ref):
        ref[row : row + value.shape[0], :] += value

    def add_small(row, value):
        small_ref[row : row + 1, :] += value

    cot = mm(perm_ref[...], arrived(1).reshape(rows, width))
    add_small(S_GAIN + 3, col_sum(cot * x4))
    add_small(S_SHIFT + 3, col_sum(cot))
    g4 = ln_back(cot, x4, r4, gain_ref[3:4, :])
    e4 = g4.astype(LOW)
    add(R_OUT, mm_tn(f2, e4), rest_ref)
    add_small(S_OUT + 1, col_sum(e4))
    e3 = (slope * mm_nt(e4, wout_ref[1])).astype(LOW)
    add(R_IN, mm_tn(t3_low, e3[:, :width]), rest_ref)
    add(R_IN + width, mm_tn(t3_low, e3[:, width:]), rest_ref)
    e3_sum = col_sum(e3)
    add_small(S_IN + 2, e3_sum[:, :width])
    add_small(S_IN + 3, e3_sum[:, width:])
    g3 = g4 + mm_nt(e3, win_ref[1])
    add_small(S_GAIN + 2, col_sum(g3 * x3))
    add_small(S_SHIFT + 2, col_sum(g3))
    g3 = ln_back(g3, x3, r3, gain_ref[2:3, :])
    eo = g3.astype(LOW)
    add(B_O2, mm_tn(rc, eo))
    add_small(S_BIAS + 8, col_sum(eo))
    ec = mm_nt(eo, wo_ref[2]).astype(LOW)
    dp = jnp.concatenate(per_segment(lambda n, l: mm_nt(ec[n], rvx[l])), axis=0)
    ds = (scale * rp * (dp - mm((rp * dp).astype(LOW), sumr_ref[...]))).astype(LOW)
    erq = jnp.concatenate(per_segment(lambda n, l: mm(ds[n], rkx[l])), axis=0).astype(LOW)
    erk = contract(jnp.concatenate(per_segment(lambda n, l: mm_tn(ds[n], rq[n])), axis=0)).astype(LOW)
    erv = contract(jnp.concatenate(per_segment(lambda n, l: mm_tn(rp_low[n], ec[n])), axis=0)).astype(LOW)
    add(B_RQ, mm_tn(t2, erq))
    add_small(S_BIAS + 6, col_sum(erq))
    add(B_RK, mm_tn(buffer, erk))
    add(B_RV, mm_tn(buffer, erv))
    add_small(S_BIAS + 7, col_sum(erv))
    eb = (mm_nt(erk, wi_ref[2, 1]) + mm_nt(erv, wi_ref[2, 2])).astype(LOW)
    add(B_O1, mm_tn(pre_low, eb))
    add_small(S_BIAS + 5, col_sum(eb))
    epx = expand(mm_nt(eb, wo_ref[1]).astype(LOW))
    dss = []
    for s in range(lsegs):
        dps = mm_nt(sv[s * nvars : (s + 1) * nvars], epx[s * lanes : (s + 1) * lanes])
        weighted = sp[s] * dps
        center = jnp.sum(weighted, axis=0, keepdims=True)
        dss.append((scale * (weighted - sp[s] * center)).astype(LOW))
    esv = jnp.concatenate([mm(sp_low[s], epx[s * lanes : (s + 1) * lanes]) for s in range(lsegs)], axis=0).astype(LOW)
    esk = jnp.concatenate([mm(dss[s], qx_ref[s * lanes : (s + 1) * lanes, :]) for s in range(lsegs)], axis=0).astype(LOW)
    for s in range(lsegs):
        kq_ref[s * lanes : (s + 1) * lanes, :] += mm_tn(dss[s], sk[s * nvars : (s + 1) * nvars])
    add(B_SK, mm_tn(t2, esk))
    add(B_SV, mm_tn(t2, esv))
    add_small(S_BIAS + 4, col_sum(esv))
    g2 = g3 + mm_nt(erq, wi_ref[2, 0]) + mm_nt(esk, wi_ref[1, 1]) + mm_nt(esv, wi_ref[1, 2])
    leaving(2, mm(back_ref[...], g2.astype(LOW)).astype(LOW))

    @pl.when(b == steps - 1)
    def _():
        kq = contract(kq_ref[...])
        kq_low = kq.astype(LOW)
        attn_ref[B_SQ : B_SQ + width, :] = mm_tn(router_ref[...], kq_low)
        add_small(S_BIAS + 3, col_sum(kq))
        places = routers * lsegs * var_size
        there = lax.broadcasted_iota(jnp.int32, (places, lsegs * SLOTS), 0)
        here = lax.broadcasted_iota(jnp.int32, (places, lsegs * SLOTS), 1)
        here = lax.div(here, lsegs) * (lsegs * var_size) + lax.rem(here, lsegs) + first_seg
        here = jnp.where(there == here, 1.0, 0.0).astype(LOW)
        rest_ref[R_ROUTE : R_ROUTE + places, :] = mm(here, mm_nt(kq_low, wi_ref[1, 0]).astype(LOW))


def feed_backward(
    lvars, b, arrived, tok_ref, offset, factor, wo_ref, win_ref, wout_ref, gain_ref, shift_ref, heads_ref, perm_ref, kept,
    feeds_ref, small_ref, etc_ref, g1_ref,
):

    q_ref, k_ref, v_ref, p_ref, tc_ref, x1_ref, r1_ref, f1_ref, s1_ref, x2_ref, r2_ref = kept
    segs, width = tok_ref.shape[2:]
    rows = lvars * segs

    @pl.when(b == 0)
    def _():
        feeds_ref[...] = jnp.zeros(feeds_ref.shape, F32)

    def add(ref, row, value):
        ref[row : row + value.shape[0], :] += value

    def wide(ref):
        return jnp.concatenate([ref[b]] * (width // 128), axis=1)

    g2 = mm(perm_ref[...], arrived(2).reshape(rows, width))
    x2 = x2_ref[b].astype(F32)
    add(small_ref, S_GAIN + 1, col_sum(g2 * x2))
    add(small_ref, S_SHIFT + 1, col_sum(g2))
    g2 = ln_back(g2, x2, wide(r2_ref), gain_ref[1:2, :])
    e2 = g2.astype(LOW)
    add(feeds_ref, M_OUT, mm_tn(f1_ref[b], e2))
    add(small_ref, S_OUT, col_sum(e2))
    e1 = (s1_ref[b].astype(F32) * mm_nt(e2, wout_ref[0])).astype(LOW)
    x1 = x1_ref[b].astype(F32)
    t1 = (x1 * gain_ref[0:1, :] + shift_ref[0:1, :]).astype(LOW)
    add(feeds_ref, M_IN, mm_tn(t1, e1[:, :width]))
    add(feeds_ref, M_IN + width, mm_tn(t1, e1[:, width:]))
    e1_sum = col_sum(e1)
    add(small_ref, S_IN, e1_sum[:, :width])
    add(small_ref, S_IN + 1, e1_sum[:, width:])
    g1 = g2 + mm_nt(e1, win_ref[0])
    add(small_ref, S_GAIN, col_sum(g1 * x1))
    add(small_ref, S_SHIFT, col_sum(g1))
    g1 = ln_back(g1, x1, wide(r1_ref), gain_ref[0:1, :])
    g1_ref[b] = g1
    et = g1.astype(LOW)
    add(feeds_ref, M_O, mm_tn(tc_ref[b], et))
    add(small_ref, S_BIAS + 2, col_sum(et))
    etc_ref[b] = mm_nt(et, wo_ref[0]).astype(LOW)
    for v in range(lvars):
        part = slice(v * segs, (v + 1) * segs)
        tc_ref[b, part, :] = mm(p_ref[b, part, :], spread_heads(etc_ref[b, part, :], heads_ref)).astype(LOW)
    low = ((tok_ref[b].reshape(rows, width).astype(F32) - offset) * factor).astype(LOW)
    add(feeds_ref, M_V, mm_tn(low, tc_ref[b]))
    add(small_ref, S_BIAS + 1, col_sum(tc_ref[b]))


def time_backward(lvars, b, tok_ref, offset, factor, heads_ref, headsf_ref, kept, times_ref, small_ref, etc_ref):
    q_ref, k_ref, v_ref, p_ref = kept[:4]
    segs, width = tok_ref.shape[2:]
    rows = lvars * segs
    scale = np.float32((width // HEADS) ** (-0.5))

    @pl.when(b == 0)
    def _():
        times_ref[...] = jnp.zeros(times_ref.shape, F32)

    def add(ref, row, value):
        ref[row : row + value.shape[0], :] += value

    for v in range(lvars):
        part = slice(v * segs, (v + 1) * segs)
        ex = spread_heads(etc_ref[b, part, :], heads_ref)
        prob = p_ref[b, part, :].astype(F32)
        weighted = prob * mm_nt(v_ref[b, part, :], ex)
        ets = (weighted - prob * jnp.sum(weighted, axis=0, keepdims=True)).astype(LOW)
        gk = (scale * mm(ets, spread_heads(q_ref[b, part, :], heads_ref))).astype(LOW)
        q_ref[b, part, :] = (scale * gather_heads(mm_tn(ets, k_ref[b, part, :]), headsf_ref, segs)).astype(LOW)
        k_ref[b, part, :] = gk
    low = ((tok_ref[b].reshape(rows, width).astype(F32) - offset) * factor).astype(LOW)
    add(times_ref, T_Q, mm_tn(low, q_ref[b]))
    add(times_ref, T_K, mm_tn(low, k_ref[b]))
    add(small_ref, S_BIAS, col_sum(q_ref[b]))


class Sum:
    def __init__(self, axes, acc, send, total, recv, sems):
        self.acc, self.send, self.total, self.recv, self.sems = acc, send, total, recv, sems
        self.plan = []
        start, size = 0, acc.shape[0]
        for index, count, target in axes:
            size //= count
            self.plan.append((index, count, target, start, size))
            start = start + index * size
        self.levels = len(self.plan)
        self.last = 2 * self.levels

    @staticmethod
    def scratch(rows, width, counts):
        recv, size = [], rows
        for count in counts:
            size //= count
            recv.append(pltpu.VMEM((count - 1, size, width), LOW))
        copies = sum(counts) - len(counts)
        return [
            pltpu.VMEM((rows, width), F32), pltpu.VMEM((rows, width), LOW), pltpu.VMEM((rows, width), LOW),
            *[pltpu.SemaphoreType.DMA((copies,))] * 4, *recv,
        ]

    def rows(self, start, size):
        return pl.ds(start if isinstance(start, int) else pl.multiple_of(start, 16), size)

    def copies(self, level, gather):
        send_sem, recv_sem = self.sems[2:] if gather else self.sems[:2]
        index, count, target, start, size = self.plan[level]
        first = sum(entry[1] - 1 for entry in self.plan[:level])
        found = []
        for k in range(1, count):
            peer = lax.rem(index + k, count)
            rows = self.rows(start + (index if gather else peer) * size, size)
            copy = pltpu.make_async_remote_copy(
                src_ref=(self.total if gather else self.send).at[rows, :],
                dst_ref=self.total.at[rows, :] if gather else self.recv[level].at[k - 1],
                send_sem=send_sem.at[first + k - 1],
                recv_sem=recv_sem.at[first + k - 1],
                device_id=target(peer),
                device_id_type=MESH,
            )
            found.append((copy, rows))
        return found

    def advance(self, turn):
        levels = self.levels
        if 0 < turn <= levels:
            for copy, _ in self.copies(turn - 1, False):
                copy.wait()
            index, count, _, start, size = self.plan[turn - 1]
            mine = self.rows(start + index * size, size)
            value = self.acc[mine, :]
            for k in range(count - 1):
                value = value + self.recv[turn - 1][k].astype(F32)
            if turn < levels:
                self.acc[mine, :] = value
            else:
                self.total[mine, :] = value.astype(LOW)
        elif turn > levels:
            for copy, _ in self.copies(self.last - turn, True):
                copy.wait()
        if turn < levels:
            for copy, rows in self.copies(turn, False):
                self.send[rows, :] = self.acc[rows, :].astype(LOW)
                copy.start()
        elif turn < self.last:
            for copy, _ in self.copies(self.last - 1 - turn, True):
                copy.start()

    @property
    def turns(self):
        return self.last + 1


class SmallSum:
    def __init__(self, acc, sent, recvs, sems, places):
        self.acc, self.sent, self.recvs, self.sems, self.places = acc, sent, recvs, sems, places

    @staticmethod
    def scratch(rows, width, sizes):
        return [
            pltpu.VMEM((rows, width), F32), pltpu.VMEM((len(sizes), rows, width), LOW),
            *[pltpu.VMEM((size, rows, width), LOW) for size in sizes],
            *[pltpu.SemaphoreType.DMA((size,)) for size in sizes for _ in range(2)],
        ]

    def copies(self, stage):
        name, me, size = self.places[stage]
        send_sem, recv_sem = self.sems[2 * stage : 2 * stage + 2]
        return [
            pltpu.make_async_remote_copy(
                src_ref=self.sent.at[stage],
                dst_ref=self.recvs[stage].at[me],
                send_sem=send_sem.at[k],
                recv_sem=recv_sem.at[k],
                device_id={name: lax.rem(me + k, size)},
                device_id_type=MESH,
            )
            for k in range(1, size)
        ]

    def start(self, stage):
        value = self.acc[...].astype(LOW)
        self.sent[stage] = value
        self.recvs[stage][self.places[stage][1]] = value
        for copy in self.copies(stage):
            copy.start()

    def finish(self, stage):
        for copy in self.copies(stage):
            copy.wait()
        value = self.recvs[stage][0].astype(F32)
        for k in range(1, self.places[stage][2]):
            value = value + self.recvs[stage][k].astype(F32)
        self.acc[...] = value


def layer_kernel(
    lvars, lsegs, nvars, routers, steps, var_size, seg_size, sizes, groups, shares,
    dom_ref, cnt_ref, tok_ref, cot_ref, mean_ref, scale_ref, router_ref, wi_ref, wo_ref, ab_ref,
    win_ref, bin_ref, wout_ref, bout_ref, gain_ref, shift_ref, heads_ref, headsf_ref, split_ref, join_ref, mask_ref, grow_ref, shrink_ref, sumr_ref, swap_ref, back_ref,
    small_out_ref, out_ref, gin_ref, inner_ref, outer_ref, up_ref, down_ref, route_ref,
    sent_ref, came_ref, qx_ref, kq_ref, etc_ref, g1_ref, send_sem, recv_sem, out_sem, *scratch,
):
    me = lax.axis_index("var")
    seg = lax.axis_index("seg")
    width = tok_ref.shape[3]
    rows = lvars * tok_ref.shape[2]
    block = rows // var_size
    kept, scratch = scratch[:11], scratch[11:]
    cores, xs, ys, zs = sizes
    core, xi = lax.rem(seg, cores), lax.div(seg, cores)
    yi, zi = lax.rem(me, ys), lax.div(me, ys)

    def space(i):
        return {"seg": lax.rem(i, xs) * cores + core, "var": lax.div(i, xs)}

    axes = {
        "core": (core, cores, lambda i: {"seg": xi * cores + i}),
        "plane": (yi * xs + xi, xs * ys, lambda i: space(zi * (xs * ys) + i)),
        "z": (zi, zs, lambda i: {"var": i * ys + yi}),
        "space": (me * xs + xi, var_size * xs, space),
    }
    sums = []
    for _, names in groups:
        used = 7 + len(names)
        group, scratch = scratch[:used], scratch[used:]
        sums.append(Sum([axes[name] for name in names], group[0], group[1], group[2], group[7:], group[3:7]))
    parts = []
    for index, base, count in shares:
        parts.append((sums[index], base, sums[index].acc.at[pl.ds(base, count), :]))
    attns, routes, feeds, times = parts
    small = SmallSum(scratch[0], scratch[1], scratch[2:4], scratch[4:8], [("seg", seg, seg_size), ("var", me, var_size)])

    def copy(kind, b, k):
        target = lax.rem(me + k, var_size)
        return pltpu.make_async_remote_copy(
            src_ref=sent_ref.at[kind, b, target],
            dst_ref=came_ref.at[kind, b, me],
            send_sem=send_sem.at[kind, b],
            recv_sem=recv_sem.at[kind, b],
            device_id={"var": target},
            device_id_type=MESH,
        )

    def whole(kind, b):
        others = pl.ds(0, var_size - 1)
        return pltpu.make_async_remote_copy(
            src_ref=sent_ref.at[kind, b, others],
            dst_ref=came_ref.at[kind, b, others],
            send_sem=send_sem.at[kind, b],
            recv_sem=recv_sem.at[kind, b],
            device_id={"var": lax.rem(me + 1, var_size)},
            device_id_type=MESH,
        )

    def store(kind, b, value):
        value = value.reshape(var_size, block, width)
        sent_ref[kind, b] = value
        came_ref[kind, b, me] = sent_ref[kind, b, me]

    def send(kind, b):
        for k in range(1, var_size):
            copy(kind, b, k).start()

    def pick(b, ref):
        total = jnp.zeros((1, width), F32)
        for d in range(ref.shape[0]):
            total = total + jnp.where(dom_ref[b] == d, ref[d : d + 1, :], 0.0)
        return total

    def arrived(kind, b):
        whole(kind, b).wait_recv()
        return came_ref[kind, b]

    pieces = [
        (times, T_Q, 2 * width, inner_ref, 0), (feeds, M_V, width, inner_ref, 2 * width), (attns, B_SQ, 6 * width, inner_ref, 3 * width),
        (feeds, M_O, width, outer_ref, 0), (attns, B_O1, 2 * width, outer_ref, width),
        (feeds, M_IN, 2 * width, up_ref, 0), (routes, R_IN, 2 * width, up_ref, 2 * width),
        (feeds, M_OUT, 2 * width, down_ref, 0), (routes, R_OUT, 2 * width, down_ref, 2 * width),
        (routes, R_ROUTE, route_ref.shape[0], route_ref, 0),
    ]

    def deliver(which):
        return [
            pltpu.make_async_copy(
                which.total.at[pl.ds(base + row, count), :], ref.at[pl.ds(there, count), :], out_sem.at[index]
            )
            for index, ((total, base, _), row, count, ref, there) in enumerate(pieces)
            if total is which
        ]

    def series_out(kind, b):
        source, ref = ((came_ref.at[3, b], out_ref), (g1_ref.at[b], gin_ref))[kind]
        return pltpu.make_async_copy(source, ref.at[b], out_sem.at[len(pieces) + kind * steps + b])

    barrier = pltpu.get_barrier_semaphore()
    _, spaces, _ = axes["space"]
    for k in range(1, spaces):
        pl.semaphore_signal(barrier, inc=1, device_id=space(lax.rem(axes["space"][0] + k, spaces)), device_id_type=MESH)
    for k in range(1, cores):
        for i in range(xs):
            peer = {"seg": i * cores + lax.rem(core + k, cores)}
            pl.semaphore_signal(barrier, inc=1, device_id=peer, device_id_type=MESH)
    small.acc[...] = jnp.zeros_like(small.acc)

    def forward(b):
        store(1, b, mm(split_ref[...], cot_ref[b].reshape(rows, width)).astype(LOW))
        t2 = time_forward(
            lvars, b, tok_ref, pick(b, mean_ref), pick(b, scale_ref), wi_ref, wo_ref, ab_ref, win_ref, bin_ref,
            wout_ref, bout_ref, gain_ref, shift_ref, heads_ref, headsf_ref, kept,
        )
        store(0, b, mm(split_ref[...], t2).astype(LOW))

        @pl.when(b == 0)
        def _():
            pl.semaphore_wait(barrier, spaces - 1 + (cores - 1) * xs)

        send(0, b)
        send(1, b)

    def middle(b):
        def leaving(kind, value):
            store(kind, b, value)
            if kind == 2:
                send(2, b)

        limit = jnp.int32(0)
        for d in range(cnt_ref.shape[0]):
            limit = limit + jnp.where(dom_ref[b] == d, cnt_ref[d], 0)
        router_part(
            lsegs, nvars, routers, steps, b, lambda kind: arrived(kind, b), leaving,
            limit, router_ref, wi_ref, wo_ref, ab_ref, win_ref, bin_ref, wout_ref, bout_ref,
            gain_ref, shift_ref, mask_ref, grow_ref, shrink_ref, sumr_ref, swap_ref, back_ref,
            attns[2], routes[2], small.acc, qx_ref, kq_ref, me * lsegs, var_size,
        )

    def back_feed(b):
        feed_backward(
            lvars, b, lambda kind: arrived(kind, b), tok_ref, pick(b, mean_ref), pick(b, scale_ref), wo_ref, win_ref,
            wout_ref, gain_ref, shift_ref, heads_ref, join_ref, kept, feeds[2], small.acc, etc_ref, g1_ref,
        )

    def back_time(b):
        time_backward(
            lvars, b, tok_ref, pick(b, mean_ref), pick(b, scale_ref), heads_ref, headsf_ref, kept, times[2], small.acc,
            etc_ref,
        )

    def back_input(b):
        grad = g1_ref[b] + mm_nt(kept[0][b], wi_ref[0, 0]) + mm_nt(kept[1][b], wi_ref[0, 1])
        g1_ref[b] = (grad + mm_nt(kept[4][b], wi_ref[0, 2])) * pick(b, scale_ref)
        series_out(1, b).start()

    todo = {}

    def plan(total, *rounds):
        for turn in range(total.turns):
            todo.setdefault(rounds[min(turn, len(rounds) - 1)], []).append(functools.partial(total.advance, turn))

    for b, round_ in enumerate(OUT_ROUNDS):
        todo.setdefault(round_, []).append(functools.partial(send, 3, b))
    rounds_of = (ATTN_ROUNDS, ROUTE_ROUNDS, FEED_ROUNDS, TIME_ROUNDS) if len(sums) > 1 else ((2 * steps, 3 * steps),)
    for total, rounds in zip(sums, rounds_of):
        plan(total, *rounds)
    todo.setdefault(2 * steps, []).append(functools.partial(small.start, 0))
    todo.setdefault(2 * steps + steps // 2, []).append(lambda: (small.finish(0), small.start(1)))

    def sweep(run, first):
        def body(b, carry):
            for round_, acts in sorted(todo.items()):
                if first <= round_ < first + steps:

                    @pl.when(b == round_ - first)
                    def _(acts=acts):
                        for act in acts:
                            act()

            run(b)
            return carry

        lax.fori_loop(0, steps, body, 0)

    sweep(forward, -2 * steps)
    sweep(middle, -steps)
    sweep(back_feed, 0)
    sweep(back_time, steps)
    sweep(back_input, 2 * steps)
    last = [max(rounds[: total.turns]) for total, rounds in zip(sums, rounds_of)]
    for round_ in range(3 * steps, max(max(todo), *last) + 1):
        for act in todo.get(round_, []):
            act()
        for total, end in zip(sums, last):
            if round_ == max(end, 3 * steps):
                for copy in deliver(total):
                    copy.start()
    small.finish(1)
    small_out_ref[...] = small.acc[...]
    for b in range(steps):
        whole(3, b).wait_recv()
        series_out(0, b).start()
    for b in range(steps):
        for kind in range(4):
            whole(kind, b).wait_send()
    for total in sums:
        for copy in deliver(total):
            copy.wait()
    for b in range(steps):
        series_out(0, b).wait()
        series_out(1, b).wait()


def finish_kernel(
    segs, lvars, out_ref, gin_ref, small_ref, inner_ref, outer_ref, up_ref, down_ref, route_ref, join_ref,
    output_ref, gin_out_ref, ginner_ref, gouter_ref, gbias_ref, gup_ref, gupb_ref, gdown_ref, gdownb_ref, ggain_ref,
    gshift_ref, groute_ref,
):
    width = inner_ref.shape[1]

    @pl.when(pl.program_id(0) == 0)
    def _():
        for i in range(3):
            gbias_ref[i] = small_ref[S_BIAS + 3 * i : S_BIAS + 3 * i + 3, :]
        for i in range(2):
            for j in range(2):
                row = S_IN + 2 * i + j
                gupb_ref[i : i + 1, j * width : (j + 1) * width] = small_ref[row : row + 1, :]
        gdownb_ref[...] = small_ref[S_OUT : S_OUT + 2, :]
        ggain_ref[...] = small_ref[S_GAIN : S_GAIN + 4, :]
        gshift_ref[...] = small_ref[S_SHIFT : S_SHIFT + 4, :]

    for i in range(out_ref.shape[0]):
        output_ref[i] = mm(join_ref[...], out_ref[i].reshape(lvars * segs, width)).reshape(lvars, segs, width)
    gin_out_ref[...] = gin_ref[...]
    ginner_ref[...] = inner_ref[...].astype(F32)
    gouter_ref[...] = outer_ref[...].astype(F32)
    gup_ref[0, :, :width] = up_ref[0, 0].astype(F32)
    gup_ref[0, :, width:] = up_ref[0, 1].astype(F32)
    gdown_ref[...] = down_ref[...].astype(F32)
    groute_ref[...] = route_ref[...].astype(F32)


def fixed(shape, index=None):
    index = (0,) * len(shape) if index is None else index
    return pl.BlockSpec(shape, lambda b: index)


def on_device(
    var_size, seg_size,
    tokens, domain, counts, domain_mean, domain_scale, attn_inner, attn_outer, attn_bias,
    mlp_in, mlp_in_bias, mlp_out, mlp_out_bias, norm_gain, norm_bias, router, cotangent,
):
    batch, lvars, segs, width = tokens.shape
    routers = router.shape[1]
    hidden = mlp_in.shape[2]
    lsegs = segs // var_size
    nvars = lvars * var_size
    rows = lvars * segs
    lanes = SLOTS * HEADS
    me = lax.axis_index("var")

    heads = (np.arange(width)[None, :] // (width // HEADS) == np.arange(HEADS)[:, None]).astype(np.float32)
    heads_low = jnp.asarray(heads, LOW)
    heads_f = jnp.asarray(heads, F32)
    mask = jnp.asarray(np.concatenate([heads, heads], axis=0), LOW)
    order = np.arange(rows).reshape(lvars, var_size, lsegs).transpose(1, 0, 2).reshape(-1)
    split = np.eye(rows, dtype=np.float32)[order]
    order = np.arange(rows).reshape(nvars, lsegs).transpose(1, 0).reshape(-1)
    swap = np.eye(rows, dtype=np.float32)[order]
    group = np.arange(lsegs * lanes) // HEADS
    group = group % SLOTS * lsegs + group // SLOTS
    grow = (group[:, None] == np.arange(lsegs * SLOTS)[None, :]).astype(np.float32)
    sumr = (np.arange(lanes)[:, None] % HEADS == np.arange(lanes)[None, :] % HEADS).astype(np.float32)

    kept = [
        ((rows, width), LOW), ((rows, width), LOW), ((rows, width), LOW), ((rows, HEADS * segs), LOW),
        ((rows, width), LOW), ((rows, width), LOW), ((rows, 128), F32), ((rows, hidden), LOW),
        ((rows, hidden), LOW), ((rows, width), LOW), ((rows, 128), F32),
    ]
    mine = lax.dynamic_slice_in_dim(router.transpose(1, 0, 2), me * lsegs, lsegs, 1)
    mine = jnp.pad(mine, ((0, SLOTS - routers), (0, 0), (0, 0))).reshape(SLOTS * lsegs, width)
    consts = [jnp.asarray(x, LOW) for x in (split, split.T)] + [mask]
    consts += [jnp.asarray(x, LOW) for x in (grow, grow.T, sumr, swap, swap.T)]

    cores = 2 if seg_size % 2 == 0 else 1
    xs = seg_size // cores
    ys = xs if var_size % xs == 0 else 1
    zs = var_size // ys
    sizes = (cores, xs, ys, zs)
    counts_of = {"core": cores, "plane": xs * ys, "z": zs, "space": var_size * xs}
    far = ("core", "plane", "z")
    near = ("core", "space") if var_size * xs <= 16 else far
    unit = 16 * var_size * seg_size
    wanted = [(B_ROWS, far), (R_ROUTE + segs * routers, far), (M_ROWS, far), (T_ROWS, near)]
    if unit > 1024:
        starts = np.cumsum([0] + [count for count, _ in wanted])
        parts = [(0, int(start), count) for start, (count, _) in zip(starts, wanted)]
        wanted = [(int(starts[-1]), far)]
    else:
        parts = [(index, 0, count) for index, (count, _) in enumerate(wanted)]
    groups = []
    for count, names in wanted:
        groups.append((-(-count // unit) * unit, [name for name in names if counts_of[name] > 1]))
    scalars = pl.BlockSpec(memory_space=pltpu.SMEM)
    anywhere = pl.BlockSpec(memory_space=pl.ANY)
    out_shapes = [
        jax.ShapeDtypeStruct((S_ROWS, width), F32),
        jax.ShapeDtypeStruct((batch, var_size, rows // var_size, width), LOW),
        jax.ShapeDtypeStruct((batch, rows, width), F32),
        jax.ShapeDtypeStruct((9 * width, width), LOW),
        jax.ShapeDtypeStruct((3 * width, width), LOW),
        jax.ShapeDtypeStruct((4 * width, width), LOW),
        jax.ShapeDtypeStruct((2 * hidden, width), LOW),
        jax.ShapeDtypeStruct((routers * segs, width), LOW),
    ]
    in_vmem = pl.BlockSpec(memory_space=pltpu.VMEM)
    small, arrived, input_grad, inner_low, outer_low, up_low, down_low, route_low = pl.pallas_call(
        functools.partial(layer_kernel, lvars, lsegs, nvars, routers, batch, var_size, seg_size, sizes, groups, parts),
        in_specs=[scalars] * 2 + [in_vmem] * (16 + len(consts)),
        out_specs=[in_vmem] + [anywhere] * 7,
        out_shape=out_shapes,
        scratch_shapes=[
            pltpu.VMEM((4, batch, var_size, rows // var_size, width), LOW),
            pltpu.VMEM((4, batch, var_size, rows // var_size, width), LOW),
            pltpu.VMEM((lsegs * lanes, width), LOW),
            pltpu.VMEM((lsegs * lanes, width), F32),
            pltpu.VMEM((batch, rows, width), LOW),
            pltpu.VMEM((batch, rows, width), F32),
            pltpu.SemaphoreType.DMA((4, batch)),
            pltpu.SemaphoreType.DMA((4, batch)),
            pltpu.SemaphoreType.DMA((10 + 2 * batch,)),
            *[pltpu.VMEM((batch,) + shape, dtype) for shape, dtype in kept],
            *[x for count, names in groups for x in Sum.scratch(count, width, [counts_of[name] for name in names])],
            *SmallSum.scratch(S_ROWS, width, (seg_size, var_size)),
        ],
        compiler_params=pltpu.CompilerParams(
            vmem_limit_bytes=VMEM_LIMIT, collective_id=0, has_side_effects=True
        ),
        name="layer",
    )(
        domain, counts, tokens, cotangent, domain_mean, domain_scale, mine, attn_inner, attn_outer, attn_bias, mlp_in,
        mlp_in_bias, mlp_out, mlp_out_bias, norm_gain, norm_bias, heads_low, heads_f, *consts,
    )

    turns = 4

    def shares(*shape):
        shape = (shape[0] // turns,) + shape[1:]
        return pl.BlockSpec(shape, lambda i: (i,) + (0,) * (len(shape) - 1))

    piece = width * 2 // turns
    per = turns // 2
    whole = lambda x: fixed(x.shape)
    f32 = lambda x: jax.ShapeDtypeStruct(x.shape, F32)
    output, input_grad, grad_inner, grad_outer, grad_bias, grad_up, grad_up_bias, grad_down, *rest = pl.pallas_call(
        functools.partial(finish_kernel, segs, lvars),
        grid=(turns,),
        in_specs=[
            shares(*arrived.shape), shares(*input_grad.shape), whole(small),
            shares(*inner_low.shape), shares(*outer_low.shape),
            pl.BlockSpec((1, 2, piece, width), lambda i: (i // per, 0, i % per, 0)),
            shares(*down_low.shape), shares(*route_low.shape), whole(consts[1]),
        ],
        out_specs=[
            shares(*tokens.shape), shares(*input_grad.shape), shares(*inner_low.shape), shares(*outer_low.shape), whole(attn_bias),
            pl.BlockSpec((1, piece, hidden), lambda i: (i // per, i % per, 0)), whole(mlp_in_bias),
            shares(*down_low.shape), whole(mlp_out_bias), whole(norm_gain), whole(norm_bias), shares(*route_low.shape),
        ],
        out_shape=[
            f32(tokens), f32(input_grad), f32(inner_low), f32(outer_low), f32(attn_bias), f32(mlp_in), f32(mlp_in_bias),
            f32(down_low), f32(mlp_out_bias), f32(norm_gain), f32(norm_bias), f32(route_low),
        ],
        compiler_params=pltpu.CompilerParams(dimension_semantics=("arbitrary",), vmem_limit_bytes=VMEM_LIMIT),
        name="finish",
    )(
        arrived, input_grad, small, inner_low, outer_low, up_low.reshape(2, 2, width, width), down_low,
        route_low, consts[1],
    )
    grad_down_bias, grad_gain, grad_shift, grad_router = rest
    return (
        output, input_grad.reshape(tokens.shape), grad_inner.reshape(attn_inner.shape),
        grad_outer.reshape(attn_outer.shape), grad_bias, grad_up, grad_up_bias, grad_down.reshape(mlp_out.shape),
        grad_down_bias, grad_gain, grad_shift, grad_router.reshape(routers, segs, width).transpose(1, 0, 2),
    )


def solution(mesh):
    split = P("seg", "var", None, None)
    in_specs = (split, P("seg")) + (P(),) * 13 + (split,)
    out_specs = (split, split) + (P(),) * 10
    var_size, seg_size = mesh.shape["var"], mesh.shape["seg"]
    return jax.shard_map(
        functools.partial(on_device, var_size, seg_size),
        mesh=mesh, in_specs=in_specs, out_specs=out_specs, check_vma=False,
    )
```

```python
import functools

import jax
import jax.numpy as jnp
import numpy as np
from jax import lax
from jax.experimental import pallas as pl
from jax.experimental.pallas import tpu as pltpu
from jax.sharding import PartitionSpec as P

HEADS = 8
SLOTS = 16
EPS = 1e-05
MASKED = -1e30
MESH = pl.DeviceIdType.MESH
F32 = jnp.float32
LOW = jnp.bfloat16
VMEM_LIMIT = 60 * 1024 * 1024


OUT_ROUNDS = (-2, -2, 0, 2, 4, 8, 12, 14)
ATTN_ROUNDS = (0, 2, 9, 14, 17, 19, 21)
ROUTE_ROUNDS = (1, 3, 12, 16, 18, 20, 22)
FEED_ROUNDS = (12, 14, 16, 18, 20, 22, 24)
TIME_ROUNDS = (16, 17, 19, 22, 23)
TOGETHER = (2, 2, 2, 2, 2)
AHEAD = 1


def mm(a, b):
    return jnp.dot(a, b, preferred_element_type=F32)


def mm_nt(a, b):
    return lax.dot_general(a, b, (((1,), (1,)), ((), ())), preferred_element_type=F32)


def mm_tn(a, b):
    return lax.dot_general(a, b, (((0,), (0,)), ((), ())), preferred_element_type=F32)


def ln_stats(a):
    mean = jnp.mean(a, axis=1, keepdims=True)
    center = a - mean
    var = jnp.mean(center * center, axis=1, keepdims=True)
    rstd = lax.rsqrt(var + EPS)
    return center * rstd, rstd


def ln_back(g, xhat, rstd, gain):
    gy = g * gain
    first = jnp.mean(gy, axis=1, keepdims=True)
    second = jnp.mean(gy * xhat, axis=1, keepdims=True)
    return rstd * (gy - first - xhat * second)


def gelu_both(z):
    k0 = np.float32(np.sqrt(2.0 / np.pi))
    k1 = np.float32(0.044715)
    square = z * z
    t = jnp.tanh(k0 * z * (1.0 + k1 * square))
    half = 0.5 * (1.0 + t)
    slope = half + 0.5 * z * (1.0 - t * t) * (k0 * (1.0 + 3.0 * k1 * square))
    return z * half, slope


def col_sum(x):
    return jnp.sum(x.astype(F32), axis=0, keepdims=True)


def spread_heads(x, heads_ref):
    return jnp.concatenate([x * heads_ref[h : h + 1, :] for h in range(HEADS)], axis=0)


def gather_heads(x, headsf_ref, rows):
    total = x[:rows] * headsf_ref[0:1, :]
    for h in range(1, HEADS):
        total = total + x[h * rows : (h + 1) * rows] * headsf_ref[h : h + 1, :]
    return total


def time_forward(
    lvars, b, several, tok_ref, offsets, factors, wi_ref, wo_ref, ab_ref, win_ref, bin_ref, wout_ref, bout_ref,
    gain_ref, shift_ref, heads_ref, headsf_ref, kept,
):
    q_ref, k_ref, v_ref, p_ref, tc_ref, x1_ref, r1_ref, f1_ref, s1_ref, x2_ref, r2_ref = kept
    segs, width = tok_ref.shape[2:]
    rows = lvars * segs
    scale = np.float32((width // HEADS) ** (-0.5))

    def keep(ref, value):
        ref[pl.ds(b, several)] = value.reshape(several, rows, value.shape[1])

    start = jnp.concatenate(
        [(tok_ref[b + i].reshape(rows, width).astype(F32) - offsets[i]) * factors[i] for i in range(several)], axis=0
    )
    low = start.astype(LOW)
    query = (mm(low, wi_ref[0, 0]) + ab_ref[0, 0:1, :]).astype(LOW)
    key = mm(low, wi_ref[0, 1]).astype(LOW)
    value = (mm(low, wi_ref[0, 2]) + ab_ref[0, 1:2, :]).astype(LOW)
    keep(q_ref, query)
    keep(k_ref, key)
    keep(v_ref, value)
    probs, contexts = [], []
    for v in range(several * lvars):
        part = slice(v * segs, (v + 1) * segs)
        scores = mm_nt(key[part], spread_heads(query[part], heads_ref))
        top = jnp.max(scores, axis=0, keepdims=True)
        expo = jnp.exp((scores - top) * scale)
        prob = (expo / jnp.sum(expo, axis=0, keepdims=True)).astype(LOW)
        probs.append(prob)
        contexts.append(gather_heads(mm_tn(prob, value[part]), headsf_ref, segs).astype(LOW))
    keep(p_ref, jnp.concatenate(probs, axis=0))
    context = jnp.concatenate(contexts, axis=0)
    keep(tc_ref, context)
    a1 = start + mm(context, wo_ref[0]) + ab_ref[0, 2:3, :]
    x1, r1 = ln_stats(a1)
    keep(x1_ref, x1.astype(LOW))
    keep(r1_ref, jnp.broadcast_to(r1, (several * rows, 128)))
    t1 = x1 * gain_ref[0:1, :] + shift_ref[0:1, :]
    act, slope = gelu_both(mm(t1.astype(LOW), win_ref[0]) + bin_ref[0:1, :])
    f1 = act.astype(LOW)
    keep(f1_ref, f1)
    keep(s1_ref, slope.astype(LOW))
    a2 = t1 + mm(f1, wout_ref[0]) + bout_ref[0:1, :]
    x2, r2 = ln_stats(a2)
    keep(x2_ref, x2.astype(LOW))
    keep(r2_ref, jnp.broadcast_to(r2, (several * rows, 128)))
    return (x2 * gain_ref[1:2, :] + shift_ref[1:2, :]).astype(LOW)


B_SQ, B_SK, B_SV, B_RQ, B_RK, B_RV, B_O1, B_O2, B_ROWS = [256 * i for i in range(9)]
R_IN, R_OUT, R_ROUTE = [256 * i for i in (0, 2, 4)]
M_IN, M_OUT, M_V, M_O, M_ROWS = [256 * i for i in (0, 2, 4, 5, 6)]
T_Q, T_K, T_ROWS = [256 * i for i in (0, 1, 2)]
S_BIAS, S_IN, S_OUT, S_GAIN, S_SHIFT, S_ROWS = 0, 9, 13, 15, 19, 32


def router_start(router_ref, wi_ref, ab_ref, grow_ref, mask_ref, attn_ref, rest_ref, qx_ref, kq_ref):
    attn_ref[...] = jnp.zeros(attn_ref.shape, F32)
    rest_ref[...] = jnp.zeros(rest_ref.shape, F32)
    kq_ref[...] = jnp.zeros(kq_ref.shape, F32)
    sq = (mm(router_ref[...], wi_ref[1, 0]) + ab_ref[1, 0:1, :]).astype(LOW)
    qx_ref[...] = expand(sq, grow_ref, mask_ref)


def router_end(lsegs, routers, var_size, first_seg, router_ref, wi_ref, shrink_ref, mask_ref, attn_ref, rest_ref, small_ref, kq_ref):
    width = router_ref.shape[1]
    kq = contract(kq_ref[...], shrink_ref, mask_ref)
    kq_low = kq.astype(LOW)
    attn_ref[B_SQ : B_SQ + width, :] = mm_tn(router_ref[...], kq_low)
    small_ref[S_BIAS + 3 : S_BIAS + 4, :] = col_sum(kq)
    places = routers * lsegs * var_size
    there = lax.broadcasted_iota(jnp.int32, (places, lsegs * SLOTS), 0)
    here = lax.broadcasted_iota(jnp.int32, (places, lsegs * SLOTS), 1)
    here = lax.div(here, lsegs) * (lsegs * var_size) + lax.rem(here, lsegs) + first_seg
    here = jnp.where(there == here, 1.0, 0.0).astype(LOW)
    rest_ref[R_ROUTE : R_ROUTE + places, :] = mm(here, mm_nt(kq_low, wi_ref[1, 0]).astype(LOW))


def expand(x, grow_ref, mask_ref):
    width = x.shape[1]
    return (mm(grow_ref[...], x).astype(LOW).reshape(-1, 16, width) * mask_ref[...][None]).reshape(-1, width)


def contract(x, shrink_ref, mask_ref):
    width = x.shape[1]
    return mm(shrink_ref[...], (x.astype(LOW).reshape(-1, 16, width) * mask_ref[...][None]).reshape(-1, width))


def router_part(
    lsegs, nvars, routers, several, arrived, leaving,
    limits, wi_ref, wo_ref, ab_ref, win_ref, bin_ref, wout_ref, bout_ref,
    gain_ref, shift_ref, mask_ref, grow_ref, shrink_ref, sumr_ref, perm_ref, back_ref,
    attn_ref, rest_ref, small_ref, qx_ref, kq_ref,
):
    series, width = perm_ref.shape[0], wo_ref.shape[1]
    rows = several * series
    lanes = SLOTS * HEADS
    scale = np.float32((width // HEADS) ** (-0.5))
    parts = range(several * lsegs)
    ns = [slice(j * nvars, (j + 1) * nvars) for j in parts]
    ls = [slice(j * lanes, (j + 1) * lanes) for j in parts]
    qs = [slice(j % lsegs * lanes, (j % lsegs + 1) * lanes) for j in parts]

    def cat(blocks):
        return jnp.concatenate(list(blocks), axis=0)

    def each(f, x):
        size = x.shape[0] // several
        return cat(f(x[i * size : (i + 1) * size]) for i in range(several))

    def grown(x):
        return each(lambda y: expand(y, grow_ref, mask_ref), x)

    def shrunk(blocks):
        return cat(contract(cat(blocks[i * lsegs : (i + 1) * lsegs]), shrink_ref, mask_ref) for i in range(several))

    def permuted(ref, x):
        return each(lambda y: mm(ref[...], y), x)

    t2 = permuted(perm_ref, arrived(0)).astype(LOW)
    sk = mm(t2, wi_ref[1, 1]).astype(LOW)
    sv = (mm(t2, wi_ref[1, 2]) + ab_ref[1, 1:2, :]).astype(LOW)
    rq = (mm(t2, wi_ref[2, 0]) + ab_ref[2, 0:1, :]).astype(LOW)
    var = lax.broadcasted_iota(jnp.int32, (nvars, lanes), 0)
    valid = [var < limit for limit in limits]

    def send_prob(j):
        real = valid[j // lsegs]
        scores = jnp.where(real, mm_nt(sk[ns[j]], qx_ref[qs[j], :]), MASKED)
        top = jnp.max(scores, axis=0, keepdims=True)
        expo = jnp.where(real, jnp.exp((scores - top) * scale), 0.0)
        return expo / jnp.sum(expo, axis=0, keepdims=True)

    sp = [send_prob(j) for j in parts]
    sp_low = [x.astype(LOW) for x in sp]
    pre_low = shrunk([mm_tn(sp_low[j], sv[ns[j]]) for j in parts]).astype(LOW)
    buffer = (mm(pre_low, wo_ref[1]) + ab_ref[1, 2:3, :]).astype(LOW)
    rkx = grown(mm(buffer, wi_ref[2, 1]).astype(LOW))
    rvx = grown((mm(buffer, wi_ref[2, 2]) + ab_ref[2, 1:2, :]).astype(LOW))
    scores = cat(mm_nt(rq[ns[j]], rkx[ls[j]]) for j in parts)
    real = lax.broadcasted_iota(jnp.int32, (rows, lanes), 1) < routers * HEADS
    scores = jnp.where(real, scores, MASKED)
    top = scores
    shift = lanes // 2
    while shift >= HEADS:
        top = jnp.maximum(top, pltpu.roll(top, shift, 1))
        shift //= 2
    expo = jnp.where(real, jnp.exp((scores - top) * scale), 0.0)
    rp = expo / mm(expo.astype(LOW), sumr_ref[...])
    rp_low = rp.astype(LOW)
    rc = cat(mm(rp_low[ns[j]], rvx[ls[j]]) for j in parts).astype(LOW)
    a3 = t2.astype(F32) + mm(rc, wo_ref[2]) + ab_ref[2, 2:3, :]
    x3, r3 = ln_stats(a3)
    t3 = x3 * gain_ref[2:3, :] + shift_ref[2:3, :]
    t3_low = t3.astype(LOW)
    act, slope = gelu_both(mm(t3_low, win_ref[1]) + bin_ref[1:2, :])
    f2 = act.astype(LOW)
    a4 = t3 + mm(f2, wout_ref[1]) + bout_ref[1:2, :]
    x4, r4 = ln_stats(a4)
    out = (x4 * gain_ref[3:4, :] + shift_ref[3:4, :]).astype(LOW)
    leaving(3, permuted(back_ref, out).astype(LOW))

    def add(row, value, ref=attn_ref):
        ref[row : row + value.shape[0], :] += value

    def add_small(row, value):
        small_ref[row : row + 1, :] += value

    cot = permuted(perm_ref, arrived(1))
    add_small(S_GAIN + 3, col_sum(cot * x4))
    add_small(S_SHIFT + 3, col_sum(cot))
    g4 = ln_back(cot, x4, r4, gain_ref[3:4, :])
    e4 = g4.astype(LOW)
    add(R_OUT, mm_tn(f2, e4), rest_ref)
    add_small(S_OUT + 1, col_sum(e4))
    e3 = (slope * mm_nt(e4, wout_ref[1])).astype(LOW)
    add(R_IN, mm_tn(t3_low, e3[:, :width]), rest_ref)
    add(R_IN + width, mm_tn(t3_low, e3[:, width:]), rest_ref)
    e3_sum = col_sum(e3)
    add_small(S_IN + 2, e3_sum[:, :width])
    add_small(S_IN + 3, e3_sum[:, width:])
    g3 = g4 + mm_nt(e3, win_ref[1])
    add_small(S_GAIN + 2, col_sum(g3 * x3))
    add_small(S_SHIFT + 2, col_sum(g3))
    g3 = ln_back(g3, x3, r3, gain_ref[2:3, :])
    eo = g3.astype(LOW)
    add(B_O2, mm_tn(rc, eo))
    add_small(S_BIAS + 8, col_sum(eo))
    ec = mm_nt(eo, wo_ref[2]).astype(LOW)
    dp = cat(mm_nt(ec[ns[j]], rvx[ls[j]]) for j in parts)
    ds = (scale * rp * (dp - mm((rp * dp).astype(LOW), sumr_ref[...]))).astype(LOW)
    erk = shrunk([mm_tn(ds[ns[j]], rq[ns[j]]) for j in parts]).astype(LOW)
    erv = shrunk([mm_tn(rp_low[ns[j]], ec[ns[j]]) for j in parts]).astype(LOW)
    erq = cat(mm(ds[ns[j]], rkx[ls[j]]) for j in parts).astype(LOW)
    eb = (mm_nt(erk, wi_ref[2, 1]) + mm_nt(erv, wi_ref[2, 2])).astype(LOW)
    epx = grown(mm_nt(eb, wo_ref[1]).astype(LOW))
    add(B_RQ, mm_tn(t2, erq))
    add_small(S_BIAS + 6, col_sum(erq))
    add(B_RK, mm_tn(buffer, erk))
    add(B_RV, mm_tn(buffer, erv))
    add_small(S_BIAS + 7, col_sum(erv))
    add(B_O1, mm_tn(pre_low, eb))
    add_small(S_BIAS + 5, col_sum(eb))
    dss = []
    for j in parts:
        weighted = sp[j] * mm_nt(sv[ns[j]], epx[ls[j]])
        center = jnp.sum(weighted, axis=0, keepdims=True)
        dss.append((scale * (weighted - sp[j] * center)).astype(LOW))
    esv = cat(mm(sp_low[j], epx[ls[j]]) for j in parts).astype(LOW)
    esk = cat(mm(dss[j], qx_ref[qs[j], :]) for j in parts).astype(LOW)
    g2 = g3 + mm_nt(erq, wi_ref[2, 0]) + mm_nt(esk, wi_ref[1, 1]) + mm_nt(esv, wi_ref[1, 2])
    leaving(2, permuted(back_ref, g2.astype(LOW)).astype(LOW))
    for s in range(lsegs):
        total = mm_tn(dss[s], sk[ns[s]])
        for i in range(1, several):
            total = total + mm_tn(dss[i * lsegs + s], sk[ns[i * lsegs + s]])
        kq_ref[qs[s], :] += total
    add(B_SK, mm_tn(t2, esk))
    add(B_SV, mm_tn(t2, esv))
    add_small(S_BIAS + 4, col_sum(esv))


def feed_backward(
    lvars, b, several, arrived, tok_ref, offsets, factors, wo_ref, win_ref, wout_ref, gain_ref, shift_ref, heads_ref,
    perm_ref, kept, feeds_ref, small_ref, etc_ref, g1_ref,
):
    q_ref, k_ref, v_ref, p_ref, tc_ref, x1_ref, r1_ref, f1_ref, s1_ref, x2_ref, r2_ref = kept
    segs, width = tok_ref.shape[2:]
    rows = lvars * segs

    def add(ref, row, value):
        ref[row : row + value.shape[0], :] += value

    def held(ref):
        return ref[pl.ds(b, several)].reshape(several * rows, ref.shape[2])

    def keep(ref, value):
        ref[pl.ds(b, several)] = value.reshape(several, rows, value.shape[1])

    def wide(ref):
        return jnp.concatenate([held(ref)] * (width // 128), axis=1)

    g2 = arrived(2)
    g2 = jnp.concatenate([mm(perm_ref[...], g2[i * rows : (i + 1) * rows]) for i in range(several)], axis=0)
    x2 = held(x2_ref).astype(F32)
    add(small_ref, S_GAIN + 1, col_sum(g2 * x2))
    add(small_ref, S_SHIFT + 1, col_sum(g2))
    g2 = ln_back(g2, x2, wide(r2_ref), gain_ref[1:2, :])
    e2 = g2.astype(LOW)
    add(feeds_ref, M_OUT, mm_tn(held(f1_ref), e2))
    add(small_ref, S_OUT, col_sum(e2))
    e1 = (held(s1_ref).astype(F32) * mm_nt(e2, wout_ref[0])).astype(LOW)
    x1 = held(x1_ref).astype(F32)
    t1 = (x1 * gain_ref[0:1, :] + shift_ref[0:1, :]).astype(LOW)
    add(feeds_ref, M_IN, mm_tn(t1, e1[:, :width]))
    add(feeds_ref, M_IN + width, mm_tn(t1, e1[:, width:]))
    e1_sum = col_sum(e1)
    add(small_ref, S_IN, e1_sum[:, :width])
    add(small_ref, S_IN + 1, e1_sum[:, width:])
    g1 = g2 + mm_nt(e1, win_ref[0])
    add(small_ref, S_GAIN, col_sum(g1 * x1))
    add(small_ref, S_SHIFT, col_sum(g1))
    g1 = ln_back(g1, x1, wide(r1_ref), gain_ref[0:1, :])
    keep(g1_ref, g1)
    et = g1.astype(LOW)
    add(feeds_ref, M_O, mm_tn(held(tc_ref), et))
    add(small_ref, S_BIAS + 2, col_sum(et))
    etc = mm_nt(et, wo_ref[0]).astype(LOW)
    keep(etc_ref, etc)
    prob = held(p_ref)
    grads = []
    for v in range(several * lvars):
        part = slice(v * segs, (v + 1) * segs)
        grads.append(mm(prob[part], spread_heads(etc[part], heads_ref)).astype(LOW))
    gv = jnp.concatenate(grads, axis=0)
    keep(tc_ref, gv)
    low = start_low(lvars, b, several, tok_ref, offsets, factors)
    add(feeds_ref, M_V, mm_tn(low, gv))
    add(small_ref, S_BIAS + 1, col_sum(gv))


def start_low(lvars, b, several, tok_ref, offsets, factors):
    segs, width = tok_ref.shape[2:]
    tok = [tok_ref[b + i].reshape(lvars * segs, width).astype(F32) for i in range(several)]
    return jnp.concatenate([((tok[i] - offsets[i]) * factors[i]).astype(LOW) for i in range(several)], axis=0)


def time_backward(
    lvars, b, several, tok_ref, offsets, factors, heads_ref, headsf_ref, kept, times_ref, small_ref, etc_ref
):
    q_ref, k_ref, v_ref, p_ref = kept[:4]
    segs, width = tok_ref.shape[2:]
    rows = lvars * segs
    scale = np.float32((width // HEADS) ** (-0.5))

    def add(ref, row, value):
        ref[row : row + value.shape[0], :] += value

    def held(ref):
        return ref[pl.ds(b, several)].reshape(several * rows, ref.shape[2])

    def keep(ref, value):
        ref[pl.ds(b, several)] = value.reshape(several, rows, value.shape[1])

    etc, query, key, value, probs = held(etc_ref), held(q_ref), held(k_ref), held(v_ref), held(p_ref)
    grads_q, grads_k = [], []
    for v in range(several * lvars):
        part = slice(v * segs, (v + 1) * segs)
        prob = probs[part].astype(F32)
        weighted = prob * mm_nt(value[part], spread_heads(etc[part], heads_ref))
        ets = (weighted - prob * jnp.sum(weighted, axis=0, keepdims=True)).astype(LOW)
        grads_k.append((scale * mm(ets, spread_heads(query[part], heads_ref))).astype(LOW))
        grads_q.append((scale * gather_heads(mm_tn(ets, key[part]), headsf_ref, segs)).astype(LOW))
    gq = jnp.concatenate(grads_q, axis=0)
    gk = jnp.concatenate(grads_k, axis=0)
    keep(q_ref, gq)
    keep(k_ref, gk)
    low = start_low(lvars, b, several, tok_ref, offsets, factors)
    add(times_ref, T_Q, mm_tn(low, gq))
    add(times_ref, T_K, mm_tn(low, gk))
    add(small_ref, S_BIAS, col_sum(gq))


class Sum:
    def __init__(self, axes, acc, send, total, recv, sems):
        self.acc, self.send, self.total, self.recv, self.sems = acc, send, total, recv, sems
        self.plan = []
        start, size = 0, acc.shape[0]
        for index, count, target in axes:
            size //= count
            self.plan.append((index, count, target, start, size))
            start = start + index * size
        self.levels = len(self.plan)
        self.last = 2 * self.levels

    @staticmethod
    def scratch(rows, width, counts):
        recv, size = [], rows
        for count in counts:
            size //= count
            recv.append(pltpu.VMEM((count - 1, size, width), LOW))
        copies = sum(counts) - len(counts)
        return [
            pltpu.VMEM((rows, width), F32), pltpu.VMEM((rows, width), LOW), pltpu.VMEM((rows, width), LOW),
            *[pltpu.SemaphoreType.DMA((copies,))] * 4, *recv,
        ]

    def rows(self, start, size):
        return pl.ds(start if isinstance(start, int) else pl.multiple_of(start, 16), size)

    def copies(self, level, gather):
        send_sem, recv_sem = self.sems[2:] if gather else self.sems[:2]
        index, count, target, start, size = self.plan[level]
        first = sum(entry[1] - 1 for entry in self.plan[:level])
        found = []
        for k in range(1, count):
            peer = lax.rem(index + k, count)
            rows = self.rows(start + (index if gather else peer) * size, size)
            copy = pltpu.make_async_remote_copy(
                src_ref=(self.total if gather else self.send).at[rows, :],
                dst_ref=self.total.at[rows, :] if gather else self.recv[level].at[k - 1],
                send_sem=send_sem.at[first + k - 1],
                recv_sem=recv_sem.at[first + k - 1],
                device_id=target(peer),
                device_id_type=MESH,
            )
            found.append((copy, rows))
        return found

    def advance(self, turn):
        levels = self.levels
        if 0 < turn <= levels:
            for copy, _ in self.copies(turn - 1, False):
                copy.wait()
            index, count, _, start, size = self.plan[turn - 1]
            mine = self.rows(start + index * size, size)
            value = self.acc[mine, :]
            for k in range(count - 1):
                value = value + self.recv[turn - 1][k].astype(F32)
            if turn < levels:
                self.acc[mine, :] = value
            else:
                self.total[mine, :] = value.astype(LOW)
        elif turn > levels:
            for copy, _ in self.copies(self.last - turn, True):
                copy.wait()
        if turn < levels:
            for copy, rows in self.copies(turn, False):
                self.send[rows, :] = self.acc[rows, :].astype(LOW)
                copy.start()
        elif turn < self.last:
            for copy, _ in self.copies(self.last - 1 - turn, True):
                copy.start()

    @property
    def turns(self):
        return self.last + 1


class SmallSum:
    def __init__(self, acc, sent, recvs, sems, places):
        self.acc, self.sent, self.recvs, self.sems, self.places = acc, sent, recvs, sems, places

    @staticmethod
    def scratch(rows, width, sizes):
        return [
            pltpu.VMEM((rows, width), F32), pltpu.VMEM((len(sizes), rows, width), LOW),
            *[pltpu.VMEM((size, rows, width), LOW) for size in sizes],
            *[pltpu.SemaphoreType.DMA((size,)) for size in sizes for _ in range(2)],
        ]

    def copies(self, stage):
        name, me, size = self.places[stage]
        send_sem, recv_sem = self.sems[2 * stage : 2 * stage + 2]
        return [
            pltpu.make_async_remote_copy(
                src_ref=self.sent.at[stage],
                dst_ref=self.recvs[stage].at[me],
                send_sem=send_sem.at[k],
                recv_sem=recv_sem.at[k],
                device_id={name: lax.rem(me + k, size)},
                device_id_type=MESH,
            )
            for k in range(1, size)
        ]

    def start(self, stage):
        value = self.acc[...].astype(LOW)
        self.sent[stage] = value
        self.recvs[stage][self.places[stage][1]] = value
        for copy in self.copies(stage):
            copy.start()

    def finish(self, stage):
        for copy in self.copies(stage):
            copy.wait()
        value = self.recvs[stage][0].astype(F32)
        for k in range(1, self.places[stage][2]):
            value = value + self.recvs[stage][k].astype(F32)
        self.acc[...] = value


def layer_kernel(
    lvars, lsegs, nvars, routers, steps, var_size, seg_size, sizes, groups, shares,
    dom_ref, cnt_ref, tok_ref, cot_ref, mean_ref, scale_ref, router_ref, wi_ref, wo_ref, ab_ref,
    win_ref, bin_ref, wout_ref, bout_ref, gain_ref, shift_ref, heads_ref, headsf_ref, split_ref, join_ref, mask_ref, grow_ref, shrink_ref, sumr_ref, swap_ref, back_ref,
    small_out_ref, out_ref, gin_ref, inner_ref, outer_ref, up_ref, down_ref, route_ref,
    sent_ref, came_ref, qx_ref, kq_ref, etc_ref, g1_ref, send_sem, recv_sem, out_sem, *scratch,
):
    me = lax.axis_index("var")
    seg = lax.axis_index("seg")
    width = tok_ref.shape[3]
    rows = lvars * tok_ref.shape[2]
    block = rows // var_size
    kept, scratch = scratch[:11], scratch[11:]
    cores, xs, ys, zs = sizes
    core, xi = lax.rem(seg, cores), lax.div(seg, cores)
    yi, zi = lax.rem(me, ys), lax.div(me, ys)

    def space(i):
        return {"seg": lax.rem(i, xs) * cores + core, "var": lax.div(i, xs)}

    axes = {
        "core": (core, cores, lambda i: {"seg": xi * cores + i}),
        "plane": (yi * xs + xi, xs * ys, lambda i: space(zi * (xs * ys) + i)),
        "z": (zi, zs, lambda i: {"var": i * ys + yi}),
        "space": (me * xs + xi, var_size * xs, space),
    }
    sums = []
    for _, names in groups:
        used = 7 + len(names)
        group, scratch = scratch[:used], scratch[used:]
        sums.append(Sum([axes[name] for name in names], group[0], group[1], group[2], group[7:], group[3:7]))
    parts = []
    for index, base, count in shares:
        parts.append((sums[index], base, sums[index].acc.at[pl.ds(base, count), :]))
    attns, routes, feeds, times = parts
    small = SmallSum(scratch[0], scratch[1], scratch[2:4], scratch[4:8], [("seg", seg, seg_size), ("var", me, var_size)])

    def copy(kind, b, k):
        target = lax.rem(me + k, var_size)
        return pltpu.make_async_remote_copy(
            src_ref=sent_ref.at[kind, b, target],
            dst_ref=came_ref.at[kind, b, me],
            send_sem=send_sem.at[kind, b],
            recv_sem=recv_sem.at[kind, b],
            device_id={"var": target},
            device_id_type=MESH,
        )

    def whole(kind, b):
        others = pl.ds(0, var_size - 1)
        return pltpu.make_async_remote_copy(
            src_ref=sent_ref.at[kind, b, others],
            dst_ref=came_ref.at[kind, b, others],
            send_sem=send_sem.at[kind, b],
            recv_sem=recv_sem.at[kind, b],
            device_id={"var": lax.rem(me + 1, var_size)},
            device_id_type=MESH,
        )

    def store(kind, b, several, value):
        value = value.reshape(several, var_size, block, width)
        sent_ref[kind, pl.ds(b, several)] = value
        for i in range(several):
            came_ref[kind, b + i, me] = sent_ref[kind, b + i, me]

    def send(kind, b, several=1):
        for i in range(several):
            for k in range(1, var_size):
                copy(kind, b + i, k).start()

    def pick(b, ref):
        total = jnp.zeros((1, width), F32)
        for d in range(ref.shape[0]):
            total = total + jnp.where(dom_ref[b] == d, ref[d : d + 1, :], 0.0)
        return total

    def picks(b, several, ref):
        return [pick(b + i, ref) for i in range(several)]

    def arrived(kind, b, several):
        for i in range(several):
            whole(kind, b + i).wait_recv()
        return came_ref[kind, pl.ds(b, several)].reshape(several * rows, width)

    pieces = [
        (times, T_Q, 2 * width, inner_ref, 0), (feeds, M_V, width, inner_ref, 2 * width), (attns, B_SQ, 6 * width, inner_ref, 3 * width),
        (feeds, M_O, width, outer_ref, 0), (attns, B_O1, 2 * width, outer_ref, width),
        (feeds, M_IN, 2 * width, up_ref, 0), (routes, R_IN, 2 * width, up_ref, 2 * width),
        (feeds, M_OUT, 2 * width, down_ref, 0), (routes, R_OUT, 2 * width, down_ref, 2 * width),
        (routes, R_ROUTE, route_ref.shape[0], route_ref, 0),
    ]

    def deliver(which):
        return [
            pltpu.make_async_copy(
                which.total.at[pl.ds(base + row, count), :], ref.at[pl.ds(there, count), :], out_sem.at[index]
            )
            for index, ((total, base, _), row, count, ref, there) in enumerate(pieces)
            if total is which
        ]

    def series_out(kind, b):
        source, ref = ((came_ref.at[3, b], out_ref), (g1_ref.at[b], gin_ref))[kind]
        return pltpu.make_async_copy(source, ref.at[b], out_sem.at[len(pieces) + kind * steps + b])

    barrier = pltpu.get_barrier_semaphore()
    _, spaces, _ = axes["space"]
    for k in range(1, spaces):
        pl.semaphore_signal(barrier, inc=1, device_id=space(lax.rem(axes["space"][0] + k, spaces)), device_id_type=MESH)
    for k in range(1, cores):
        for i in range(xs):
            peer = {"seg": i * cores + lax.rem(core + k, cores)}
            pl.semaphore_signal(barrier, inc=1, device_id=peer, device_id_type=MESH)
    small.acc[...] = jnp.zeros_like(small.acc)
    router_start(
        router_ref, wi_ref, ab_ref, grow_ref, mask_ref, attns[2], routes[2], qx_ref, kq_ref
    )
    feeds[2][...] = jnp.zeros(feeds[2].shape, F32)
    times[2][...] = jnp.zeros(times[2].shape, F32)
    pl.semaphore_wait(barrier, spaces - 1 + (cores - 1) * xs)

    def forward(b, several):
        for i in range(several):
            store(1, b + i, 1, mm(split_ref[...], cot_ref[b + i].reshape(rows, width)).astype(LOW))
        send(1, b, several)
        t2 = time_forward(
            lvars, b, several, tok_ref, picks(b, several, mean_ref), picks(b, several, scale_ref), wi_ref, wo_ref,
            ab_ref, win_ref, bin_ref, wout_ref, bout_ref, gain_ref, shift_ref, heads_ref, headsf_ref, kept,
        )
        for i in range(several):
            store(0, b + i, 1, mm(split_ref[...], t2[i * rows : (i + 1) * rows]).astype(LOW))
        send(0, b, several)

    def middle(b, several):
        def leaving(kind, value):
            store(kind, b, several, value)
            if kind == 2:
                send(2, b, several)

        limits = []
        for i in range(several):
            limit = jnp.int32(0)
            for d in range(cnt_ref.shape[0]):
                limit = limit + jnp.where(dom_ref[b + i] == d, cnt_ref[d], 0)
            limits.append(limit)
        router_part(
            lsegs, nvars, routers, several, lambda kind: arrived(kind, b, several), leaving,
            limits, wi_ref, wo_ref, ab_ref, win_ref, bin_ref, wout_ref, bout_ref,
            gain_ref, shift_ref, mask_ref, grow_ref, shrink_ref, sumr_ref, swap_ref, back_ref,
            attns[2], routes[2], small.acc, qx_ref, kq_ref,
        )

    def back_feed(b, several):
        feed_backward(
            lvars, b, several, lambda kind: arrived(kind, b, several), tok_ref, picks(b, several, mean_ref),
            picks(b, several, scale_ref), wo_ref, win_ref, wout_ref, gain_ref, shift_ref, heads_ref, join_ref, kept,
            feeds[2], small.acc, etc_ref, g1_ref,
        )

    def back_time(b, several):
        time_backward(
            lvars, b, several, tok_ref, picks(b, several, mean_ref), picks(b, several, scale_ref), heads_ref, headsf_ref,
            kept, times[2], small.acc, etc_ref,
        )

    def back_input(b, several):
        def held(ref):
            return ref[pl.ds(b, several)].reshape(several * rows, width)

        grad = held(g1_ref) + mm_nt(held(kept[0]), wi_ref[0, 0]) + mm_nt(held(kept[1]), wi_ref[0, 1])
        grad = grad + mm_nt(held(kept[4]), wi_ref[0, 2])
        for i in range(several):
            g1_ref[b + i] = grad[i * rows : (i + 1) * rows] * pick(b + i, scale_ref)
            series_out(1, b + i).start()

    todo = {}

    def plan(total, *rounds):
        for turn in range(total.turns):
            todo.setdefault(rounds[min(turn, len(rounds) - 1)], []).append(functools.partial(total.advance, turn))

    for b, round_ in enumerate(OUT_ROUNDS):
        todo.setdefault(round_, []).append(functools.partial(send, 3, b))
    rounds_of = (ATTN_ROUNDS, ROUTE_ROUNDS, FEED_ROUNDS, TIME_ROUNDS) if len(sums) > 1 else ((2 * steps, 3 * steps),)
    for total, rounds in zip(sums, rounds_of):
        plan(total, *rounds)
    todo.setdefault(2 * steps, []).append(functools.partial(small.start, 0))
    todo.setdefault(2 * steps + steps // 2, []).append(lambda: (small.finish(0), small.start(1)))

    def sweep(run, first, several):
        def body(i, carry):
            b = i * several
            for round_, acts in sorted(todo.items()):
                if first <= round_ < first + steps:

                    @pl.when(i == (round_ - first) // several)
                    def _(acts=acts):
                        for act in acts:
                            act()

            run(b, several)
            return carry

        lax.fori_loop(0, steps // several, body, 0)

    together = TOGETHER if len(sums) > 1 else (1,) * 5
    sweep(forward, -2 * steps, together[0])
    sweep(middle, -steps, together[1])
    router_end(
        lsegs, routers, var_size, me * lsegs, router_ref, wi_ref, shrink_ref, mask_ref, attns[2], routes[2], small.acc,
        kq_ref,
    )
    several = together[2]
    count = steps // several
    early = max(count - AHEAD, 1)

    def backward(i, carry):
        for round_, acts in sorted(todo.items()):
            if 0 <= round_ < 2 * steps:

                @pl.when(i == round_ // several)
                def _(acts=acts):
                    for act in acts:
                        act()

        lead = early + early - 1
        feed = (i < early) | ((i >= lead) & (i < lead + count - early))

        @pl.when(feed)
        def _():
            back_feed(jnp.where(i < early, i, i - lead + early) * several, several)

        @pl.when(jnp.logical_not(feed))
        def _():
            back_time(jnp.where(i < lead, i - early, i - count) * several, several)

        return carry

    lax.fori_loop(0, 2 * count, backward, 0)
    sweep(back_input, 2 * steps, together[4])
    last = [max(rounds[: total.turns]) for total, rounds in zip(sums, rounds_of)]
    for round_ in range(3 * steps, max(max(todo), *last) + 1):
        for act in todo.get(round_, []):
            act()
        for total, end in zip(sums, last):
            if round_ == max(end, 3 * steps):
                for copy in deliver(total):
                    copy.start()
    small.finish(1)
    small_out_ref[...] = small.acc[...]
    for b in range(steps):
        whole(3, b).wait_recv()
        series_out(0, b).start()
    for b in range(steps):
        for kind in range(4):
            whole(kind, b).wait_send()
    for total in sums:
        for copy in deliver(total):
            copy.wait()
    for b in range(steps):
        series_out(0, b).wait()
        series_out(1, b).wait()


def finish_kernel(
    segs, lvars, out_ref, gin_ref, small_ref, inner_ref, outer_ref, up_ref, down_ref, route_ref, join_ref,
    output_ref, gin_out_ref, ginner_ref, gouter_ref, gbias_ref, gup_ref, gupb_ref, gdown_ref, gdownb_ref, ggain_ref,
    gshift_ref, groute_ref,
):
    width = inner_ref.shape[1]

    @pl.when(pl.program_id(0) == 0)
    def _():
        for i in range(3):
            gbias_ref[i] = small_ref[S_BIAS + 3 * i : S_BIAS + 3 * i + 3, :]
        for i in range(2):
            for j in range(2):
                row = S_IN + 2 * i + j
                gupb_ref[i : i + 1, j * width : (j + 1) * width] = small_ref[row : row + 1, :]
        gdownb_ref[...] = small_ref[S_OUT : S_OUT + 2, :]
        ggain_ref[...] = small_ref[S_GAIN : S_GAIN + 4, :]
        gshift_ref[...] = small_ref[S_SHIFT : S_SHIFT + 4, :]

    for i in range(out_ref.shape[0]):
        output_ref[i] = mm(join_ref[...], out_ref[i].reshape(lvars * segs, width)).reshape(lvars, segs, width)
    gin_out_ref[...] = gin_ref[...]
    ginner_ref[...] = inner_ref[...].astype(F32)
    gouter_ref[...] = outer_ref[...].astype(F32)
    gup_ref[0, :, :width] = up_ref[0, 0].astype(F32)
    gup_ref[0, :, width:] = up_ref[0, 1].astype(F32)
    gdown_ref[...] = down_ref[...].astype(F32)
    groute_ref[...] = route_ref[...].astype(F32)


def fixed(shape, index=None):
    index = (0,) * len(shape) if index is None else index
    return pl.BlockSpec(shape, lambda b: index)


def on_device(
    var_size, seg_size,
    tokens, domain, counts, domain_mean, domain_scale, attn_inner, attn_outer, attn_bias,
    mlp_in, mlp_in_bias, mlp_out, mlp_out_bias, norm_gain, norm_bias, router, cotangent,
):
    batch, lvars, segs, width = tokens.shape
    routers = router.shape[1]
    hidden = mlp_in.shape[2]
    lsegs = segs // var_size
    nvars = lvars * var_size
    rows = lvars * segs
    lanes = SLOTS * HEADS
    me = lax.axis_index("var")

    heads = (np.arange(width)[None, :] // (width // HEADS) == np.arange(HEADS)[:, None]).astype(np.float32)
    heads_low = jnp.asarray(heads, LOW)
    heads_f = jnp.asarray(heads, F32)
    mask = jnp.asarray(np.concatenate([heads, heads], axis=0), LOW)
    order = np.arange(rows).reshape(lvars, var_size, lsegs).transpose(1, 0, 2).reshape(-1)
    split = np.eye(rows, dtype=np.float32)[order]
    order = np.arange(rows).reshape(nvars, lsegs).transpose(1, 0).reshape(-1)
    swap = np.eye(rows, dtype=np.float32)[order]
    group = np.arange(lsegs * lanes) // HEADS
    group = group % SLOTS * lsegs + group // SLOTS
    grow = (group[:, None] == np.arange(lsegs * SLOTS)[None, :]).astype(np.float32)
    sumr = (np.arange(lanes)[:, None] % HEADS == np.arange(lanes)[None, :] % HEADS).astype(np.float32)

    kept = [
        ((rows, width), LOW), ((rows, width), LOW), ((rows, width), LOW), ((rows, HEADS * segs), LOW),
        ((rows, width), LOW), ((rows, width), LOW), ((rows, 128), F32), ((rows, hidden), LOW),
        ((rows, hidden), LOW), ((rows, width), LOW), ((rows, 128), F32),
    ]
    mine = lax.dynamic_slice_in_dim(router.transpose(1, 0, 2), me * lsegs, lsegs, 1)
    mine = jnp.pad(mine, ((0, SLOTS - routers), (0, 0), (0, 0))).reshape(SLOTS * lsegs, width)
    consts = [jnp.asarray(x, LOW) for x in (split, split.T)] + [mask]
    consts += [jnp.asarray(x, LOW) for x in (grow, grow.T, sumr, swap, swap.T)]

    cores = 2 if seg_size % 2 == 0 else 1
    xs = seg_size // cores
    ys = xs if var_size % xs == 0 else 1
    zs = var_size // ys
    sizes = (cores, xs, ys, zs)
    counts_of = {"core": cores, "plane": xs * ys, "z": zs, "space": var_size * xs}
    far = ("core", "plane", "z")
    near = ("core", "space") if var_size * xs <= 16 else far
    unit = 16 * var_size * seg_size
    wanted = [(B_ROWS, far), (R_ROUTE + segs * routers, far), (M_ROWS, far), (T_ROWS, near)]
    if unit > 1024:
        starts = np.cumsum([0] + [count for count, _ in wanted])
        parts = [(0, int(start), count) for start, (count, _) in zip(starts, wanted)]
        wanted = [(int(starts[-1]), far)]
    else:
        parts = [(index, 0, count) for index, (count, _) in enumerate(wanted)]
    groups = []
    for count, names in wanted:
        groups.append((-(-count // unit) * unit, [name for name in names if counts_of[name] > 1]))
    scalars = pl.BlockSpec(memory_space=pltpu.SMEM)
    anywhere = pl.BlockSpec(memory_space=pl.ANY)
    out_shapes = [
        jax.ShapeDtypeStruct((S_ROWS, width), F32),
        jax.ShapeDtypeStruct((batch, var_size, rows // var_size, width), LOW),
        jax.ShapeDtypeStruct((batch, rows, width), F32),
        jax.ShapeDtypeStruct((9 * width, width), LOW),
        jax.ShapeDtypeStruct((3 * width, width), LOW),
        jax.ShapeDtypeStruct((4 * width, width), LOW),
        jax.ShapeDtypeStruct((2 * hidden, width), LOW),
        jax.ShapeDtypeStruct((routers * segs, width), LOW),
    ]
    in_vmem = pl.BlockSpec(memory_space=pltpu.VMEM)
    small, arrived, input_grad, inner_low, outer_low, up_low, down_low, route_low = pl.pallas_call(
        functools.partial(layer_kernel, lvars, lsegs, nvars, routers, batch, var_size, seg_size, sizes, groups, parts),
        in_specs=[scalars] * 2 + [in_vmem] * (16 + len(consts)),
        out_specs=[in_vmem] + [anywhere] * 7,
        out_shape=out_shapes,
        scratch_shapes=[
            pltpu.VMEM((4, batch, var_size, rows // var_size, width), LOW),
            pltpu.VMEM((4, batch, var_size, rows // var_size, width), LOW),
            pltpu.VMEM((lsegs * lanes, width), LOW),
            pltpu.VMEM((lsegs * lanes, width), F32),
            pltpu.VMEM((batch, rows, width), LOW),
            pltpu.VMEM((batch, rows, width), F32),
            pltpu.SemaphoreType.DMA((4, batch)),
            pltpu.SemaphoreType.DMA((4, batch)),
            pltpu.SemaphoreType.DMA((10 + 2 * batch,)),
            *[pltpu.VMEM((batch,) + shape, dtype) for shape, dtype in kept],
            *[x for count, names in groups for x in Sum.scratch(count, width, [counts_of[name] for name in names])],
            *SmallSum.scratch(S_ROWS, width, (seg_size, var_size)),
        ],
        compiler_params=pltpu.CompilerParams(
            vmem_limit_bytes=VMEM_LIMIT, collective_id=0, has_side_effects=True
        ),
        name="layer",
    )(
        domain, counts, tokens, cotangent, domain_mean, domain_scale, mine, attn_inner, attn_outer, attn_bias, mlp_in,
        mlp_in_bias, mlp_out, mlp_out_bias, norm_gain, norm_bias, heads_low, heads_f, *consts,
    )

    turns = 4

    def shares(*shape):
        shape = (shape[0] // turns,) + shape[1:]
        return pl.BlockSpec(shape, lambda i: (i,) + (0,) * (len(shape) - 1))

    piece = width * 2 // turns
    per = turns // 2
    whole = lambda x: fixed(x.shape)
    f32 = lambda x: jax.ShapeDtypeStruct(x.shape, F32)
    output, input_grad, grad_inner, grad_outer, grad_bias, grad_up, grad_up_bias, grad_down, *rest = pl.pallas_call(
        functools.partial(finish_kernel, segs, lvars),
        grid=(turns,),
        in_specs=[
            shares(*arrived.shape), shares(*input_grad.shape), whole(small),
            shares(*inner_low.shape), shares(*outer_low.shape),
            pl.BlockSpec((1, 2, piece, width), lambda i: (i // per, 0, i % per, 0)),
            shares(*down_low.shape), shares(*route_low.shape), whole(consts[1]),
        ],
        out_specs=[
            shares(*tokens.shape), shares(*input_grad.shape), shares(*inner_low.shape), shares(*outer_low.shape), whole(attn_bias),
            pl.BlockSpec((1, piece, hidden), lambda i: (i // per, i % per, 0)), whole(mlp_in_bias),
            shares(*down_low.shape), whole(mlp_out_bias), whole(norm_gain), whole(norm_bias), shares(*route_low.shape),
        ],
        out_shape=[
            f32(tokens), f32(input_grad), f32(inner_low), f32(outer_low), f32(attn_bias), f32(mlp_in), f32(mlp_in_bias),
            f32(down_low), f32(mlp_out_bias), f32(norm_gain), f32(norm_bias), f32(route_low),
        ],
        compiler_params=pltpu.CompilerParams(dimension_semantics=("arbitrary",), vmem_limit_bytes=VMEM_LIMIT),
        name="finish",
    )(
        arrived, input_grad, small, inner_low, outer_low, up_low.reshape(2, 2, width, width), down_low,
        route_low, consts[1],
    )
    grad_down_bias, grad_gain, grad_shift, grad_router = rest
    return (
        output, input_grad.reshape(tokens.shape), grad_inner.reshape(attn_inner.shape),
        grad_outer.reshape(attn_outer.shape), grad_bias, grad_up, grad_up_bias, grad_down.reshape(mlp_out.shape),
        grad_down_bias, grad_gain, grad_shift, grad_router.reshape(routers, segs, width).transpose(1, 0, 2),
    )


def solution(mesh):
    split = P("seg", "var", None, None)
    in_specs = (split, P("seg")) + (P(),) * 13 + (split,)
    out_specs = (split, split) + (P(),) * 10
    var_size, seg_size = mesh.shape["var"], mesh.shape["seg"]
    return jax.shard_map(
        functools.partial(on_device, var_size, seg_size),
        mesh=mesh, in_specs=in_specs, out_specs=out_specs, check_vma=False,
    )
```

```python
import functools

import jax
import jax.numpy as jnp
import numpy as np
from jax import lax
from jax.experimental import pallas as pl
from jax.experimental.pallas import tpu as pltpu
from jax.sharding import PartitionSpec as P

HEADS = 8
SLOTS = 16
EPS = 1e-05
MASKED = -1e30
MESH = pl.DeviceIdType.MESH
F32 = jnp.float32
LOW = jnp.bfloat16
VMEM_LIMIT = 60 * 1024 * 1024


OUT_ROUNDS = (-2, -2, 0, 2, 4, 8, 12, 14)
ATTN_ROUNDS = (0, 2, 9, 14, 17, 19, 21)
ROUTE_ROUNDS = (1, 3, 12, 16, 18, 20, 22)
FEED_ROUNDS = (12, 14, 16, 18, 20, 22, 24)
TIME_ROUNDS = (16, 17, 19, 22, 23)
ATTN_AXES = ("core", "plane", "z")
ROUTE_AXES = ("core", "plane", "z")
FEED_AXES = ("core", "plane", "z")
TOGETHER = (2, 2, 2, 2, 2)
AHEAD = 1


def mm(a, b):
    return jnp.dot(a, b, preferred_element_type=F32)


def mm_nt(a, b):
    return lax.dot_general(a, b, (((1,), (1,)), ((), ())), preferred_element_type=F32)


def mm_tn(a, b):
    return lax.dot_general(a, b, (((0,), (0,)), ((), ())), preferred_element_type=F32)


def ln_stats(a):
    mean = jnp.mean(a, axis=1, keepdims=True)
    center = a - mean
    var = jnp.mean(center * center, axis=1, keepdims=True)
    rstd = lax.rsqrt(var + EPS)
    return center * rstd, rstd


def ln_back(g, xhat, rstd, gain):
    gy = g * gain
    first = jnp.mean(gy, axis=1, keepdims=True)
    second = jnp.mean(gy * xhat, axis=1, keepdims=True)
    return rstd * (gy - first - xhat * second)


def gelu_both(z):
    k0 = np.float32(np.sqrt(2.0 / np.pi))
    k1 = np.float32(0.044715)
    square = z * z
    t = jnp.tanh(k0 * z * (1.0 + k1 * square))
    half = 0.5 * (1.0 + t)
    slope = half + 0.5 * z * (1.0 - t * t) * (k0 * (1.0 + 3.0 * k1 * square))
    return z * half, slope


def col_sum(x):
    return jnp.sum(x.astype(F32), axis=0, keepdims=True)


def spread_heads(x, heads_ref):
    return jnp.concatenate([x * heads_ref[h : h + 1, :] for h in range(HEADS)], axis=0)


def gather_heads(x, headsf_ref, rows):
    total = x[:rows] * headsf_ref[0:1, :]
    for h in range(1, HEADS):
        total = total + x[h * rows : (h + 1) * rows] * headsf_ref[h : h + 1, :]
    return total


def time_forward(
    lvars, b, several, tok_ref, offsets, factors, wi_ref, wo_ref, ab_ref, win_ref, bin_ref, wout_ref, bout_ref,
    gain_ref, shift_ref, heads_ref, headsf_ref, kept,
):
    q_ref, k_ref, v_ref, p_ref, tc_ref, x1_ref, r1_ref, f1_ref, s1_ref, x2_ref, r2_ref = kept
    segs, width = tok_ref.shape[2:]
    rows = lvars * segs
    scale = np.float32((width // HEADS) ** (-0.5))

    def keep(ref, value):
        ref[pl.ds(b, several)] = value.reshape(several, rows, value.shape[1])

    start = jnp.concatenate(
        [(tok_ref[b + i].reshape(rows, width).astype(F32) - offsets[i]) * factors[i] for i in range(several)], axis=0
    )
    low = start.astype(LOW)
    query = (mm(low, wi_ref[0, 0]) + ab_ref[0, 0:1, :]).astype(LOW)
    key = mm(low, wi_ref[0, 1]).astype(LOW)
    value = (mm(low, wi_ref[0, 2]) + ab_ref[0, 1:2, :]).astype(LOW)
    keep(q_ref, query)
    keep(k_ref, key)
    keep(v_ref, value)
    probs, contexts = [], []
    for v in range(several * lvars):
        part = slice(v * segs, (v + 1) * segs)
        scores = mm_nt(key[part], spread_heads(query[part], heads_ref))
        top = jnp.max(scores, axis=0, keepdims=True)
        expo = jnp.exp((scores - top) * scale)
        prob = (expo / jnp.sum(expo, axis=0, keepdims=True)).astype(LOW)
        probs.append(prob)
        contexts.append(gather_heads(mm_tn(prob, value[part]), headsf_ref, segs).astype(LOW))
    keep(p_ref, jnp.concatenate(probs, axis=0))
    context = jnp.concatenate(contexts, axis=0)
    keep(tc_ref, context)
    a1 = start + mm(context, wo_ref[0]) + ab_ref[0, 2:3, :]
    x1, r1 = ln_stats(a1)
    keep(x1_ref, x1.astype(LOW))
    keep(r1_ref, jnp.broadcast_to(r1, (several * rows, 128)))
    t1 = x1 * gain_ref[0:1, :] + shift_ref[0:1, :]
    act, slope = gelu_both(mm(t1.astype(LOW), win_ref[0]) + bin_ref[0:1, :])
    f1 = act.astype(LOW)
    keep(f1_ref, f1)
    keep(s1_ref, slope.astype(LOW))
    a2 = t1 + mm(f1, wout_ref[0]) + bout_ref[0:1, :]
    x2, r2 = ln_stats(a2)
    keep(x2_ref, x2.astype(LOW))
    keep(r2_ref, jnp.broadcast_to(r2, (several * rows, 128)))
    return (x2 * gain_ref[1:2, :] + shift_ref[1:2, :]).astype(LOW)


B_SK, B_SV, B_RQ, B_RK, B_RV, B_O1, B_ROWS = [256 * i for i in range(7)]
R_IN, R_OUT, R_O2, R_KQ = [256 * i for i in (0, 2, 4, 5)]
M_IN, M_OUT, M_V, M_O, M_ROWS = [256 * i for i in (0, 2, 4, 5, 6)]
T_Q, T_K, T_ROWS = [256 * i for i in (0, 1, 2)]
S_BIAS, S_IN, S_OUT, S_GAIN, S_SHIFT, S_ROWS = 0, 9, 13, 15, 19, 32


def router_start(places, router_ref, wi_ref, ab_ref, grow_ref, mask_ref, attn_ref, rest_ref, qx_ref, kq_ref):
    attn_ref[...] = jnp.zeros(attn_ref.shape, F32)
    rest_ref[...] = jnp.zeros(rest_ref.shape, F32)
    kq_ref[...] = jnp.zeros(kq_ref.shape, F32)
    mine = mm(places, router_ref[...]).astype(LOW)
    sq = (mm(mine, wi_ref[1, 0]) + ab_ref[1, 0:1, :]).astype(LOW)
    qx_ref[...] = expand(sq, grow_ref, mask_ref)


def router_end(lsegs, routers, var_size, first_seg, shrink_ref, mask_ref, rest_ref, small_ref, kq_ref):
    kq = contract(kq_ref[...], shrink_ref, mask_ref)
    small_ref[S_BIAS + 3 : S_BIAS + 4, :] = col_sum(kq)
    places = own_places(lsegs, routers, var_size, first_seg, 0)
    rest_ref[R_KQ : R_KQ + places.shape[0], :] = mm(places, kq.astype(LOW))


def own_places(lsegs, routers, var_size, first_seg, whole):
    shape = [lsegs * SLOTS] * 2
    shape[whole] = routers * lsegs * var_size
    there = lax.broadcasted_iota(jnp.int32, shape, whole)
    here = lax.broadcasted_iota(jnp.int32, shape, 1 - whole)
    here = lax.div(here, lsegs) * (lsegs * var_size) + lax.rem(here, lsegs) + first_seg
    return jnp.where(there == here, 1.0, 0.0).astype(LOW)


def expand(x, grow_ref, mask_ref):
    width = x.shape[1]
    return (mm(grow_ref[...], x).astype(LOW).reshape(-1, 16, width) * mask_ref[...][None]).reshape(-1, width)


def contract(x, shrink_ref, mask_ref):
    width = x.shape[1]
    return mm(shrink_ref[...], (x.astype(LOW).reshape(-1, 16, width) * mask_ref[...][None]).reshape(-1, width))


def router_part(
    lsegs, nvars, routers, several, arrived, leaving,
    limits, wi_ref, wo_ref, ab_ref, win_ref, bin_ref, wout_ref, bout_ref,
    gain_ref, shift_ref, mask_ref, grow_ref, shrink_ref, sumr_ref, perm_ref, back_ref,
    attn_ref, rest_ref, small_ref, qx_ref, kq_ref,
):
    series, width = perm_ref.shape[0], wo_ref.shape[1]
    rows = several * series
    lanes = SLOTS * HEADS
    scale = np.float32((width // HEADS) ** (-0.5))
    parts = range(several * lsegs)
    ns = [slice(j * nvars, (j + 1) * nvars) for j in parts]
    ls = [slice(j * lanes, (j + 1) * lanes) for j in parts]
    qs = [slice(j % lsegs * lanes, (j % lsegs + 1) * lanes) for j in parts]

    def cat(blocks):
        return jnp.concatenate(list(blocks), axis=0)

    def each(f, x):
        size = x.shape[0] // several
        return cat(f(x[i * size : (i + 1) * size]) for i in range(several))

    def grown(x):
        return each(lambda y: expand(y, grow_ref, mask_ref), x)

    def shrunk(blocks):
        return cat(contract(cat(blocks[i * lsegs : (i + 1) * lsegs]), shrink_ref, mask_ref) for i in range(several))

    def permuted(ref, x):
        return each(lambda y: mm(ref[...], y), x)

    t2 = permuted(perm_ref, arrived(0)).astype(LOW)
    sk = mm(t2, wi_ref[1, 1]).astype(LOW)
    sv = (mm(t2, wi_ref[1, 2]) + ab_ref[1, 1:2, :]).astype(LOW)
    rq = (mm(t2, wi_ref[2, 0]) + ab_ref[2, 0:1, :]).astype(LOW)
    var = lax.broadcasted_iota(jnp.int32, (nvars, lanes), 0)
    valid = [var < limit for limit in limits]

    def send_prob(j):
        real = valid[j // lsegs]
        scores = jnp.where(real, mm_nt(sk[ns[j]], qx_ref[qs[j], :]), MASKED)
        top = jnp.max(scores, axis=0, keepdims=True)
        expo = jnp.where(real, jnp.exp((scores - top) * scale), 0.0)
        return expo / jnp.sum(expo, axis=0, keepdims=True)

    sp = [send_prob(j) for j in parts]
    sp_low = [x.astype(LOW) for x in sp]
    pre_low = shrunk([mm_tn(sp_low[j], sv[ns[j]]) for j in parts]).astype(LOW)
    buffer = (mm(pre_low, wo_ref[1]) + ab_ref[1, 2:3, :]).astype(LOW)
    rkx = grown(mm(buffer, wi_ref[2, 1]).astype(LOW))
    rvx = grown((mm(buffer, wi_ref[2, 2]) + ab_ref[2, 1:2, :]).astype(LOW))
    scores = cat(mm_nt(rq[ns[j]], rkx[ls[j]]) for j in parts)
    real = lax.broadcasted_iota(jnp.int32, (rows, lanes), 1) < routers * HEADS
    scores = jnp.where(real, scores, MASKED)
    top = scores
    shift = lanes // 2
    while shift >= HEADS:
        top = jnp.maximum(top, pltpu.roll(top, shift, 1))
        shift //= 2
    expo = jnp.where(real, jnp.exp((scores - top) * scale), 0.0)
    rp = expo / mm(expo.astype(LOW), sumr_ref[...])
    rp_low = rp.astype(LOW)
    rc = cat(mm(rp_low[ns[j]], rvx[ls[j]]) for j in parts).astype(LOW)
    a3 = t2.astype(F32) + mm(rc, wo_ref[2]) + ab_ref[2, 2:3, :]
    x3, r3 = ln_stats(a3)
    t3 = x3 * gain_ref[2:3, :] + shift_ref[2:3, :]
    t3_low = t3.astype(LOW)
    act, slope = gelu_both(mm(t3_low, win_ref[1]) + bin_ref[1:2, :])
    f2 = act.astype(LOW)
    a4 = t3 + mm(f2, wout_ref[1]) + bout_ref[1:2, :]
    x4, r4 = ln_stats(a4)
    out = (x4 * gain_ref[3:4, :] + shift_ref[3:4, :]).astype(LOW)
    leaving(3, permuted(back_ref, out).astype(LOW))

    def add(row, value, ref=attn_ref):
        ref[row : row + value.shape[0], :] += value

    def add_small(row, value):
        small_ref[row : row + 1, :] += value

    cot = permuted(perm_ref, arrived(1))
    add_small(S_GAIN + 3, col_sum(cot * x4))
    add_small(S_SHIFT + 3, col_sum(cot))
    g4 = ln_back(cot, x4, r4, gain_ref[3:4, :])
    e4 = g4.astype(LOW)
    add(R_OUT, mm_tn(f2, e4), rest_ref)
    add_small(S_OUT + 1, col_sum(e4))
    e3 = (slope * mm_nt(e4, wout_ref[1])).astype(LOW)
    add(R_IN, mm_tn(t3_low, e3[:, :width]), rest_ref)
    add(R_IN + width, mm_tn(t3_low, e3[:, width:]), rest_ref)
    e3_sum = col_sum(e3)
    add_small(S_IN + 2, e3_sum[:, :width])
    add_small(S_IN + 3, e3_sum[:, width:])
    g3 = g4 + mm_nt(e3, win_ref[1])
    add_small(S_GAIN + 2, col_sum(g3 * x3))
    add_small(S_SHIFT + 2, col_sum(g3))
    g3 = ln_back(g3, x3, r3, gain_ref[2:3, :])
    eo = g3.astype(LOW)
    add(R_O2, mm_tn(rc, eo), rest_ref)
    add_small(S_BIAS + 8, col_sum(eo))
    ec = mm_nt(eo, wo_ref[2]).astype(LOW)
    dp = cat(mm_nt(ec[ns[j]], rvx[ls[j]]) for j in parts)
    ds = (scale * rp * (dp - mm((rp * dp).astype(LOW), sumr_ref[...]))).astype(LOW)
    erk = shrunk([mm_tn(ds[ns[j]], rq[ns[j]]) for j in parts]).astype(LOW)
    erv = shrunk([mm_tn(rp_low[ns[j]], ec[ns[j]]) for j in parts]).astype(LOW)
    erq = cat(mm(ds[ns[j]], rkx[ls[j]]) for j in parts).astype(LOW)
    eb = (mm_nt(erk, wi_ref[2, 1]) + mm_nt(erv, wi_ref[2, 2])).astype(LOW)
    epx = grown(mm_nt(eb, wo_ref[1]).astype(LOW))
    add(B_RQ, mm_tn(t2, erq))
    add_small(S_BIAS + 6, col_sum(erq))
    add(B_RK, mm_tn(buffer, erk))
    add(B_RV, mm_tn(buffer, erv))
    add_small(S_BIAS + 7, col_sum(erv))
    add(B_O1, mm_tn(pre_low, eb))
    add_small(S_BIAS + 5, col_sum(eb))
    dss = []
    for j in parts:
        weighted = sp[j] * mm_nt(sv[ns[j]], epx[ls[j]])
        center = jnp.sum(weighted, axis=0, keepdims=True)
        dss.append((scale * (weighted - sp[j] * center)).astype(LOW))
    esv = cat(mm(sp_low[j], epx[ls[j]]) for j in parts).astype(LOW)
    esk = cat(mm(dss[j], qx_ref[qs[j], :]) for j in parts).astype(LOW)
    g2 = g3 + mm_nt(erq, wi_ref[2, 0]) + mm_nt(esk, wi_ref[1, 1]) + mm_nt(esv, wi_ref[1, 2])
    leaving(2, permuted(back_ref, g2.astype(LOW)).astype(LOW))
    for s in range(lsegs):
        total = mm_tn(dss[s], sk[ns[s]])
        for i in range(1, several):
            total = total + mm_tn(dss[i * lsegs + s], sk[ns[i * lsegs + s]])
        kq_ref[qs[s], :] += total
    add(B_SK, mm_tn(t2, esk))
    add(B_SV, mm_tn(t2, esv))
    add_small(S_BIAS + 4, col_sum(esv))


def feed_backward(
    lvars, b, several, arrived, tok_ref, offsets, factors, wo_ref, win_ref, wout_ref, gain_ref, shift_ref, heads_ref,
    perm_ref, kept, feeds_ref, small_ref, etc_ref, g1_ref,
):
    q_ref, k_ref, v_ref, p_ref, tc_ref, x1_ref, r1_ref, f1_ref, s1_ref, x2_ref, r2_ref = kept
    segs, width = tok_ref.shape[2:]
    rows = lvars * segs

    def add(ref, row, value):
        ref[row : row + value.shape[0], :] += value

    def held(ref):
        return ref[pl.ds(b, several)].reshape(several * rows, ref.shape[2])

    def keep(ref, value):
        ref[pl.ds(b, several)] = value.reshape(several, rows, value.shape[1])

    def wide(ref):
        return jnp.concatenate([held(ref)] * (width // 128), axis=1)

    g2 = arrived(2)
    g2 = jnp.concatenate([mm(perm_ref[...], g2[i * rows : (i + 1) * rows]) for i in range(several)], axis=0)
    x2 = held(x2_ref).astype(F32)
    add(small_ref, S_GAIN + 1, col_sum(g2 * x2))
    add(small_ref, S_SHIFT + 1, col_sum(g2))
    g2 = ln_back(g2, x2, wide(r2_ref), gain_ref[1:2, :])
    e2 = g2.astype(LOW)
    add(feeds_ref, M_OUT, mm_tn(held(f1_ref), e2))
    add(small_ref, S_OUT, col_sum(e2))
    e1 = (held(s1_ref).astype(F32) * mm_nt(e2, wout_ref[0])).astype(LOW)
    x1 = held(x1_ref).astype(F32)
    t1 = (x1 * gain_ref[0:1, :] + shift_ref[0:1, :]).astype(LOW)
    add(feeds_ref, M_IN, mm_tn(t1, e1[:, :width]))
    add(feeds_ref, M_IN + width, mm_tn(t1, e1[:, width:]))
    e1_sum = col_sum(e1)
    add(small_ref, S_IN, e1_sum[:, :width])
    add(small_ref, S_IN + 1, e1_sum[:, width:])
    g1 = g2 + mm_nt(e1, win_ref[0])
    add(small_ref, S_GAIN, col_sum(g1 * x1))
    add(small_ref, S_SHIFT, col_sum(g1))
    g1 = ln_back(g1, x1, wide(r1_ref), gain_ref[0:1, :])
    keep(g1_ref, g1)
    et = g1.astype(LOW)
    add(feeds_ref, M_O, mm_tn(held(tc_ref), et))
    add(small_ref, S_BIAS + 2, col_sum(et))
    etc = mm_nt(et, wo_ref[0]).astype(LOW)
    keep(etc_ref, etc)
    prob = held(p_ref)
    grads = []
    for v in range(several * lvars):
        part = slice(v * segs, (v + 1) * segs)
        grads.append(mm(prob[part], spread_heads(etc[part], heads_ref)).astype(LOW))
    gv = jnp.concatenate(grads, axis=0)
    keep(tc_ref, gv)
    low = start_low(lvars, b, several, tok_ref, offsets, factors)
    add(feeds_ref, M_V, mm_tn(low, gv))
    add(small_ref, S_BIAS + 1, col_sum(gv))


def start_low(lvars, b, several, tok_ref, offsets, factors):
    segs, width = tok_ref.shape[2:]
    tok = [tok_ref[b + i].reshape(lvars * segs, width).astype(F32) for i in range(several)]
    return jnp.concatenate([((tok[i] - offsets[i]) * factors[i]).astype(LOW) for i in range(several)], axis=0)


def time_backward(
    lvars, b, several, tok_ref, offsets, factors, heads_ref, headsf_ref, kept, times_ref, small_ref, etc_ref
):
    q_ref, k_ref, v_ref, p_ref = kept[:4]
    segs, width = tok_ref.shape[2:]
    rows = lvars * segs
    scale = np.float32((width // HEADS) ** (-0.5))

    def add(ref, row, value):
        ref[row : row + value.shape[0], :] += value

    def held(ref):
        return ref[pl.ds(b, several)].reshape(several * rows, ref.shape[2])

    def keep(ref, value):
        ref[pl.ds(b, several)] = value.reshape(several, rows, value.shape[1])

    etc, query, key, value, probs = held(etc_ref), held(q_ref), held(k_ref), held(v_ref), held(p_ref)
    grads_q, grads_k = [], []
    for v in range(several * lvars):
        part = slice(v * segs, (v + 1) * segs)
        prob = probs[part].astype(F32)
        weighted = prob * mm_nt(value[part], spread_heads(etc[part], heads_ref))
        ets = (weighted - prob * jnp.sum(weighted, axis=0, keepdims=True)).astype(LOW)
        grads_k.append((scale * mm(ets, spread_heads(query[part], heads_ref))).astype(LOW))
        grads_q.append((scale * gather_heads(mm_tn(ets, key[part]), headsf_ref, segs)).astype(LOW))
    gq = jnp.concatenate(grads_q, axis=0)
    gk = jnp.concatenate(grads_k, axis=0)
    keep(q_ref, gq)
    keep(k_ref, gk)
    low = start_low(lvars, b, several, tok_ref, offsets, factors)
    add(times_ref, T_Q, mm_tn(low, gq))
    add(times_ref, T_K, mm_tn(low, gk))
    add(small_ref, S_BIAS, col_sum(gq))


class Sum:
    def __init__(self, axes, acc, send, total, recv, sems):
        self.acc, self.send, self.total, self.recv, self.sems = acc, send, total, recv, sems
        self.plan = []
        start, size = 0, acc.shape[0]
        for index, count, target in axes:
            size //= count
            self.plan.append((index, count, target, start, size))
            start = start + index * size
        self.levels = len(self.plan)
        self.last = 2 * self.levels

    @staticmethod
    def scratch(rows, width, counts):
        recv, size = [], rows
        for count in counts:
            size //= count
            recv.append(pltpu.VMEM((count - 1, size, width), LOW))
        copies = sum(counts) - len(counts)
        return [
            pltpu.VMEM((rows, width), F32), pltpu.VMEM((rows, width), LOW), pltpu.VMEM((rows, width), LOW),
            *[pltpu.SemaphoreType.DMA((copies,))] * 4, *recv,
        ]

    def rows(self, start, size):
        return pl.ds(start if isinstance(start, int) else pl.multiple_of(start, 16), size)

    def copies(self, level, gather):
        send_sem, recv_sem = self.sems[2:] if gather else self.sems[:2]
        index, count, target, start, size = self.plan[level]
        first = sum(entry[1] - 1 for entry in self.plan[:level])
        found = []
        for k in range(1, count):
            peer = lax.rem(index + k, count)
            rows = self.rows(start + (index if gather else peer) * size, size)
            copy = pltpu.make_async_remote_copy(
                src_ref=(self.total if gather else self.send).at[rows, :],
                dst_ref=self.total.at[rows, :] if gather else self.recv[level].at[k - 1],
                send_sem=send_sem.at[first + k - 1],
                recv_sem=recv_sem.at[first + k - 1],
                device_id=target(peer),
                device_id_type=MESH,
            )
            found.append((copy, rows))
        return found

    def advance(self, turn):
        levels = self.levels
        if 0 < turn <= levels:
            for copy, _ in self.copies(turn - 1, False):
                copy.wait()
            index, count, _, start, size = self.plan[turn - 1]
            mine = self.rows(start + index * size, size)
            value = self.acc[mine, :]
            for k in range(count - 1):
                value = value + self.recv[turn - 1][k].astype(F32)
            if turn < levels:
                self.acc[mine, :] = value
            else:
                self.total[mine, :] = value.astype(LOW)
        elif turn > levels:
            for copy, _ in self.copies(self.last - turn, True):
                copy.wait()
        if turn < levels:
            for copy, rows in self.copies(turn, False):
                self.send[rows, :] = self.acc[rows, :].astype(LOW)
                copy.start()
        elif turn < self.last:
            for copy, _ in self.copies(self.last - 1 - turn, True):
                copy.start()

    @property
    def turns(self):
        return self.last + 1


class SmallSum:
    def __init__(self, acc, sent, recvs, sems, places):
        self.acc, self.sent, self.recvs, self.sems, self.places = acc, sent, recvs, sems, places

    @staticmethod
    def scratch(rows, width, sizes):
        return [
            pltpu.VMEM((rows, width), F32), pltpu.VMEM((len(sizes), rows, width), LOW),
            *[pltpu.VMEM((size, rows, width), LOW) for size in sizes],
            *[pltpu.SemaphoreType.DMA((size,)) for size in sizes for _ in range(2)],
        ]

    def copies(self, stage):
        name, me, size = self.places[stage]
        send_sem, recv_sem = self.sems[2 * stage : 2 * stage + 2]
        return [
            pltpu.make_async_remote_copy(
                src_ref=self.sent.at[stage],
                dst_ref=self.recvs[stage].at[me],
                send_sem=send_sem.at[k],
                recv_sem=recv_sem.at[k],
                device_id={name: lax.rem(me + k, size)},
                device_id_type=MESH,
            )
            for k in range(1, size)
        ]

    def start(self, stage):
        value = self.acc[...].astype(LOW)
        self.sent[stage] = value
        self.recvs[stage][self.places[stage][1]] = value
        for copy in self.copies(stage):
            copy.start()

    def finish(self, stage):
        for copy in self.copies(stage):
            copy.wait()
        value = self.recvs[stage][0].astype(F32)
        for k in range(1, self.places[stage][2]):
            value = value + self.recvs[stage][k].astype(F32)
        self.acc[...] = value


def layer_kernel(
    lvars, lsegs, nvars, routers, steps, var_size, seg_size, sizes, groups, shares,
    dom_ref, cnt_ref, tok_ref, cot_ref, mean_ref, scale_ref, router_ref, wi_ref, wo_ref, ab_ref,
    win_ref, bin_ref, wout_ref, bout_ref, gain_ref, shift_ref, heads_ref, headsf_ref, split_ref, join_ref, mask_ref, grow_ref, shrink_ref, sumr_ref, swap_ref, back_ref,
    small_out_ref, out_ref, gin_ref, inner_ref, outer_ref, up_ref, down_ref, route_ref,
    sent_ref, came_ref, qx_ref, kq_ref, etc_ref, g1_ref, made_ref, send_sem, recv_sem, out_sem, *scratch,
):
    me = lax.axis_index("var")
    seg = lax.axis_index("seg")
    width = tok_ref.shape[3]
    rows = lvars * tok_ref.shape[2]
    block = rows // var_size
    kept, scratch = scratch[:11], scratch[11:]
    cores, xs, ys, zs = sizes
    core, xi = lax.rem(seg, cores), lax.div(seg, cores)
    yi, zi = lax.rem(me, ys), lax.div(me, ys)
    pairs = 2 if zs % 2 == 0 else 1
    zl, zh = lax.rem(zi, pairs), lax.div(zi, pairs)

    def space(i):
        return {"seg": lax.rem(i, xs) * cores + core, "var": lax.div(i, xs)}

    axes = {
        "core": (core, cores, lambda i: {"seg": xi * cores + i}),
        "plane": (yi * xs + xi, xs * ys, lambda i: space(zi * (xs * ys) + i)),
        "z": (zi, zs, lambda i: {"var": i * ys + yi}),
        "space": (me * xs + xi, var_size * xs, space),
        "x": (xi, xs, lambda i: {"seg": i * cores + core}),
        "y": (yi, ys, lambda i: {"var": zi * ys + i}),
        "pair": (zl, pairs, lambda i: {"var": (zh * pairs + i) * ys + yi}),
        "far": (zh, zs // pairs, lambda i: {"var": (i * pairs + zl) * ys + yi}),
    }
    sums = []
    for _, names in groups:
        used = 7 + len(names)
        group, scratch = scratch[:used], scratch[used:]
        sums.append(Sum([axes[name] for name in names], group[0], group[1], group[2], group[7:], group[3:7]))
    parts = []
    for index, base, count in shares:
        parts.append((sums[index], base, sums[index].acc.at[pl.ds(base, count), :]))
    attns, routes, feeds, times = parts
    small = SmallSum(scratch[0], scratch[1], scratch[2:4], scratch[4:8], [("seg", seg, seg_size), ("var", me, var_size)])

    def copy(kind, b, k):
        target = lax.rem(me + k, var_size)
        return pltpu.make_async_remote_copy(
            src_ref=sent_ref.at[kind, b, target],
            dst_ref=came_ref.at[kind, b, me],
            send_sem=send_sem.at[kind, b],
            recv_sem=recv_sem.at[kind, b],
            device_id={"var": target},
            device_id_type=MESH,
        )

    def whole(kind, b):
        others = pl.ds(0, var_size - 1)
        return pltpu.make_async_remote_copy(
            src_ref=sent_ref.at[kind, b, others],
            dst_ref=came_ref.at[kind, b, others],
            send_sem=send_sem.at[kind, b],
            recv_sem=recv_sem.at[kind, b],
            device_id={"var": lax.rem(me + 1, var_size)},
            device_id_type=MESH,
        )

    def store(kind, b, several, value):
        value = value.reshape(several, var_size, block, width)
        sent_ref[kind, pl.ds(b, several)] = value
        for i in range(several):
            came_ref[kind, b + i, me] = sent_ref[kind, b + i, me]

    def send(kind, b, several=1):
        for i in range(several):
            for k in range(1, var_size):
                copy(kind, b + i, k).start()

    def pick(b, ref):
        total = jnp.zeros((1, width), F32)
        for d in range(ref.shape[0]):
            total = total + jnp.where(dom_ref[b] == d, ref[d : d + 1, :], 0.0)
        return total

    def picks(b, several, ref):
        return [pick(b + i, ref) for i in range(several)]

    def arrived(kind, b, several):
        for i in range(several):
            whole(kind, b + i).wait_recv()
        return came_ref[kind, pl.ds(b, several)].reshape(several * rows, width)

    pieces = [
        (times, T_Q, 2 * width, inner_ref, 0), (feeds, M_V, width, inner_ref, 2 * width), (None, 0, width, inner_ref, 3 * width),
        (attns, B_SK, 5 * width, inner_ref, 4 * width),
        (feeds, M_O, width, outer_ref, 0), (attns, B_O1, width, outer_ref, width), (routes, R_O2, width, outer_ref, 2 * width),
        (feeds, M_IN, 2 * width, up_ref, 0), (routes, R_IN, 2 * width, up_ref, 2 * width),
        (feeds, M_OUT, 2 * width, down_ref, 0), (routes, R_OUT, 2 * width, down_ref, 2 * width),
        (None, width, route_ref.shape[0], route_ref, 0),
    ]

    def deliver(which):
        return [
            pltpu.make_async_copy(
                (made_ref if part is None else which.total).at[pl.ds((0 if part is None else part[1]) + row, count), :],
                ref.at[pl.ds(there, count), :],
                out_sem.at[index],
            )
            for index, (part, row, count, ref, there) in enumerate(pieces)
            if (routes if part is None else part)[0] is which
        ]

    def make_routes():
        total, base, _ = routes
        kq = total.total[base + R_KQ : base + R_KQ + route_ref.shape[0], :]
        made_ref[:width, :] = mm_tn(router_ref[...], kq).astype(LOW)
        made_ref[width:, :] = mm_nt(kq, wi_ref[1, 0]).astype(LOW)

    def series_out(kind, b):
        source, ref = ((came_ref.at[3, b], out_ref), (etc_ref.at[b], gin_ref))[kind]
        return pltpu.make_async_copy(source, ref.at[b], out_sem.at[len(pieces) + kind * steps + b])

    barrier = pltpu.get_barrier_semaphore()
    _, spaces, _ = axes["space"]
    for k in range(1, spaces):
        pl.semaphore_signal(barrier, inc=1, device_id=space(lax.rem(axes["space"][0] + k, spaces)), device_id_type=MESH)
    for k in range(1, cores):
        for i in range(xs):
            peer = {"seg": i * cores + lax.rem(core + k, cores)}
            pl.semaphore_signal(barrier, inc=1, device_id=peer, device_id_type=MESH)
    small.acc[...] = jnp.zeros_like(small.acc)
    router_start(
        own_places(lsegs, routers, var_size, me * lsegs, 1), router_ref, wi_ref, ab_ref, grow_ref, mask_ref, attns[2], routes[2], qx_ref, kq_ref
    )
    feeds[2][...] = jnp.zeros(feeds[2].shape, F32)
    times[2][...] = jnp.zeros(times[2].shape, F32)
    pl.semaphore_wait(barrier, spaces - 1 + (cores - 1) * xs)

    def forward(b, several):
        for i in range(several):
            store(1, b + i, 1, mm(split_ref[...], cot_ref[b + i].reshape(rows, width)).astype(LOW))
        send(1, b, several)
        t2 = time_forward(
            lvars, b, several, tok_ref, picks(b, several, mean_ref), picks(b, several, scale_ref), wi_ref, wo_ref,
            ab_ref, win_ref, bin_ref, wout_ref, bout_ref, gain_ref, shift_ref, heads_ref, headsf_ref, kept,
        )
        for i in range(several):
            store(0, b + i, 1, mm(split_ref[...], t2[i * rows : (i + 1) * rows]).astype(LOW))
        send(0, b, several)

    def middle(b, several):
        def leaving(kind, value):
            store(kind, b, several, value)
            if kind == 2:
                send(2, b, several)

        limits = []
        for i in range(several):
            limit = jnp.int32(0)
            for d in range(cnt_ref.shape[0]):
                limit = limit + jnp.where(dom_ref[b + i] == d, cnt_ref[d], 0)
            limits.append(limit)
        router_part(
            lsegs, nvars, routers, several, lambda kind: arrived(kind, b, several), leaving,
            limits, wi_ref, wo_ref, ab_ref, win_ref, bin_ref, wout_ref, bout_ref,
            gain_ref, shift_ref, mask_ref, grow_ref, shrink_ref, sumr_ref, swap_ref, back_ref,
            attns[2], routes[2], small.acc, qx_ref, kq_ref,
        )

    def back_feed(b, several):
        feed_backward(
            lvars, b, several, lambda kind: arrived(kind, b, several), tok_ref, picks(b, several, mean_ref),
            picks(b, several, scale_ref), wo_ref, win_ref, wout_ref, gain_ref, shift_ref, heads_ref, join_ref, kept,
            feeds[2], small.acc, etc_ref, g1_ref,
        )

    def back_time(b, several):
        time_backward(
            lvars, b, several, tok_ref, picks(b, several, mean_ref), picks(b, several, scale_ref), heads_ref, headsf_ref,
            kept, times[2], small.acc, etc_ref,
        )

    def back_input(b, several):
        def held(ref):
            return ref[pl.ds(b, several)].reshape(several * rows, width)

        grad = held(g1_ref) + mm_nt(held(kept[0]), wi_ref[0, 0]) + mm_nt(held(kept[1]), wi_ref[0, 1])
        grad = grad + mm_nt(held(kept[4]), wi_ref[0, 2])
        for i in range(several):
            etc_ref[b + i] = (grad[i * rows : (i + 1) * rows] * pick(b + i, scale_ref)).astype(LOW)
            series_out(1, b + i).start()

    todo = {}

    def plan(total, *rounds):
        for turn in range(total.turns):
            todo.setdefault(rounds[min(turn, len(rounds) - 1)], []).append(functools.partial(total.advance, turn))

    for b, round_ in enumerate(OUT_ROUNDS):
        todo.setdefault(round_, []).append(functools.partial(send, 3, b))
    rounds_of = (ATTN_ROUNDS, ROUTE_ROUNDS, FEED_ROUNDS, TIME_ROUNDS) if len(sums) > 1 else ((2 * steps, 3 * steps),)
    for total, rounds in zip(sums, rounds_of):
        plan(total, *rounds)
    todo.setdefault(2 * steps, []).append(functools.partial(small.start, 0))
    todo.setdefault(2 * steps + steps // 2, []).append(lambda: (small.finish(0), small.start(1)))

    def sweep(run, first, several):
        def body(i, carry):
            b = i * several
            for round_, acts in sorted(todo.items()):
                if first <= round_ < first + steps:

                    @pl.when(i == (round_ - first) // several)
                    def _(acts=acts):
                        for act in acts:
                            act()

            run(b, several)
            return carry

        lax.fori_loop(0, steps // several, body, 0)

    together = TOGETHER if len(sums) > 1 else (1,) * 5
    sweep(forward, -2 * steps, together[0])
    sweep(middle, -steps, together[1])
    router_end(
        lsegs, routers, var_size, me * lsegs, shrink_ref, mask_ref, routes[2], small.acc, kq_ref,
    )
    several = together[2]
    count = steps // several
    early = max(count - AHEAD, 1)

    def backward(i, carry):
        for round_, acts in sorted(todo.items()):
            if 0 <= round_ < 2 * steps:

                @pl.when(i == round_ // several)
                def _(acts=acts):
                    for act in acts:
                        act()

        lead = early + early - 1
        feed = (i < early) | ((i >= lead) & (i < lead + count - early))

        @pl.when(feed)
        def _():
            back_feed(jnp.where(i < early, i, i - lead + early) * several, several)

        @pl.when(jnp.logical_not(feed))
        def _():
            back_time(jnp.where(i < lead, i - early, i - count) * several, several)

        return carry

    lax.fori_loop(0, 2 * count, backward, 0)
    sweep(back_input, 2 * steps, together[4])
    last = [max(rounds[: total.turns]) for total, rounds in zip(sums, rounds_of)]
    for round_ in range(3 * steps, max(max(todo), 3 * steps, *last) + 1):
        for act in todo.get(round_, []):
            act()
        for total, end in zip(sums, last):
            if round_ == max(end, 3 * steps):
                if total is routes[0]:
                    make_routes()
                for copy in deliver(total):
                    copy.start()
    small.finish(1)
    small_out_ref[...] = small.acc[...]
    for b in range(steps):
        whole(3, b).wait_recv()
        series_out(0, b).start()
    for b in range(steps):
        for kind in range(4):
            whole(kind, b).wait_send()
    for total in sums:
        for copy in deliver(total):
            copy.wait()
    for b in range(steps):
        series_out(0, b).wait()
        series_out(1, b).wait()


def finish_kernel(
    segs, lvars, out_ref, gin_ref, small_ref, inner_ref, outer_ref, up_ref, down_ref, route_ref, join_ref,
    output_ref, gin_out_ref, ginner_ref, gouter_ref, gbias_ref, gup_ref, gupb_ref, gdown_ref, gdownb_ref, ggain_ref,
    gshift_ref, groute_ref,
):
    width = inner_ref.shape[1]

    @pl.when(pl.program_id(0) == 0)
    def _():
        for i in range(3):
            gbias_ref[i] = small_ref[S_BIAS + 3 * i : S_BIAS + 3 * i + 3, :]
        for i in range(2):
            for j in range(2):
                row = S_IN + 2 * i + j
                gupb_ref[i : i + 1, j * width : (j + 1) * width] = small_ref[row : row + 1, :]
        gdownb_ref[...] = small_ref[S_OUT : S_OUT + 2, :]
        ggain_ref[...] = small_ref[S_GAIN : S_GAIN + 4, :]
        gshift_ref[...] = small_ref[S_SHIFT : S_SHIFT + 4, :]

    for i in range(out_ref.shape[0]):
        output_ref[i] = mm(join_ref[...], out_ref[i].reshape(lvars * segs, width)).reshape(lvars, segs, width)
    gin_out_ref[...] = gin_ref[...].astype(F32)
    ginner_ref[...] = inner_ref[...].astype(F32)
    gouter_ref[...] = outer_ref[...].astype(F32)
    gup_ref[0, :, :width] = up_ref[0, 0].astype(F32)
    gup_ref[0, :, width:] = up_ref[0, 1].astype(F32)
    gdown_ref[...] = down_ref[...].astype(F32)
    groute_ref[...] = route_ref[...].astype(F32)


def fixed(shape, index=None):
    index = (0,) * len(shape) if index is None else index
    return pl.BlockSpec(shape, lambda b: index)


def on_device(
    var_size, seg_size,
    tokens, domain, counts, domain_mean, domain_scale, attn_inner, attn_outer, attn_bias,
    mlp_in, mlp_in_bias, mlp_out, mlp_out_bias, norm_gain, norm_bias, router, cotangent,
):
    batch, lvars, segs, width = tokens.shape
    routers = router.shape[1]
    hidden = mlp_in.shape[2]
    lsegs = segs // var_size
    nvars = lvars * var_size
    rows = lvars * segs
    lanes = SLOTS * HEADS
    heads = (np.arange(width)[None, :] // (width // HEADS) == np.arange(HEADS)[:, None]).astype(np.float32)
    heads_low = jnp.asarray(heads, LOW)
    heads_f = jnp.asarray(heads, F32)
    mask = jnp.asarray(np.concatenate([heads, heads], axis=0), LOW)
    order = np.arange(rows).reshape(lvars, var_size, lsegs).transpose(1, 0, 2).reshape(-1)
    split = np.eye(rows, dtype=np.float32)[order]
    order = np.arange(rows).reshape(nvars, lsegs).transpose(1, 0).reshape(-1)
    swap = np.eye(rows, dtype=np.float32)[order]
    group = np.arange(lsegs * lanes) // HEADS
    group = group % SLOTS * lsegs + group // SLOTS
    grow = (group[:, None] == np.arange(lsegs * SLOTS)[None, :]).astype(np.float32)
    sumr = (np.arange(lanes)[:, None] % HEADS == np.arange(lanes)[None, :] % HEADS).astype(np.float32)

    kept = [
        ((rows, width), LOW), ((rows, width), LOW), ((rows, width), LOW), ((rows, HEADS * segs), LOW),
        ((rows, width), LOW), ((rows, width), LOW), ((rows, 128), F32), ((rows, hidden), LOW),
        ((rows, hidden), LOW), ((rows, width), LOW), ((rows, 128), F32),
    ]
    routes = router.transpose(1, 0, 2).reshape(routers * segs, width)
    consts = [jnp.asarray(x, LOW) for x in (split, split.T)] + [mask]
    consts += [jnp.asarray(x, LOW) for x in (grow, grow.T, sumr, swap, swap.T)]

    cores = 2 if seg_size % 2 == 0 else 1
    xs = seg_size // cores
    ys = xs if var_size % xs == 0 else 1
    zs = var_size // ys
    sizes = (cores, xs, ys, zs)
    pairs = 2 if zs % 2 == 0 else 1
    counts_of = {
        "core": cores, "plane": xs * ys, "z": zs, "space": var_size * xs, "x": xs, "y": ys, "pair": pairs,
        "far": zs // pairs,
    }
    far = ("core", "plane", "z")
    near = ("core", "space") if var_size * xs <= 16 else far
    unit = 16 * var_size * seg_size
    wanted = [(B_ROWS, ATTN_AXES), (R_KQ + segs * routers, ROUTE_AXES), (M_ROWS, FEED_AXES), (T_ROWS, near)]
    if unit > 1024:
        starts = np.cumsum([0] + [count for count, _ in wanted])
        parts = [(0, int(start), count) for start, (count, _) in zip(starts, wanted)]
        wanted = [(int(starts[-1]), far)]
    else:
        parts = [(index, 0, count) for index, (count, _) in enumerate(wanted)]
    groups = []
    for count, names in wanted:
        groups.append((-(-count // unit) * unit, [name for name in names if counts_of[name] > 1]))
    scalars = pl.BlockSpec(memory_space=pltpu.SMEM)
    anywhere = pl.BlockSpec(memory_space=pl.ANY)
    out_shapes = [
        jax.ShapeDtypeStruct((S_ROWS, width), F32),
        jax.ShapeDtypeStruct((batch, var_size, rows // var_size, width), LOW),
        jax.ShapeDtypeStruct((batch, rows, width), LOW),
        jax.ShapeDtypeStruct((9 * width, width), LOW),
        jax.ShapeDtypeStruct((3 * width, width), LOW),
        jax.ShapeDtypeStruct((4 * width, width), LOW),
        jax.ShapeDtypeStruct((2 * hidden, width), LOW),
        jax.ShapeDtypeStruct((routers * segs, width), LOW),
    ]
    in_vmem = pl.BlockSpec(memory_space=pltpu.VMEM)
    small, arrived, input_grad, inner_low, outer_low, up_low, down_low, route_low = pl.pallas_call(
        functools.partial(layer_kernel, lvars, lsegs, nvars, routers, batch, var_size, seg_size, sizes, groups, parts),
        in_specs=[scalars] * 2 + [in_vmem] * (16 + len(consts)),
        out_specs=[in_vmem] + [anywhere] * 7,
        out_shape=out_shapes,
        scratch_shapes=[
            pltpu.VMEM((4, batch, var_size, rows // var_size, width), LOW),
            pltpu.VMEM((4, batch, var_size, rows // var_size, width), LOW),
            pltpu.VMEM((lsegs * lanes, width), LOW),
            pltpu.VMEM((lsegs * lanes, width), F32),
            pltpu.VMEM((batch, rows, width), LOW),
            pltpu.VMEM((batch, rows, width), F32),
            pltpu.VMEM((width + routers * segs, width), LOW),
            pltpu.SemaphoreType.DMA((4, batch)),
            pltpu.SemaphoreType.DMA((4, batch)),
            pltpu.SemaphoreType.DMA((12 + 2 * batch,)),
            *[pltpu.VMEM((batch,) + shape, dtype) for shape, dtype in kept],
            *[x for count, names in groups for x in Sum.scratch(count, width, [counts_of[name] for name in names])],
            *SmallSum.scratch(S_ROWS, width, (seg_size, var_size)),
        ],
        compiler_params=pltpu.CompilerParams(
            vmem_limit_bytes=VMEM_LIMIT, collective_id=0, has_side_effects=True
        ),
        name="layer",
    )(
        domain, counts, tokens, cotangent, domain_mean, domain_scale, routes, attn_inner, attn_outer, attn_bias, mlp_in,
        mlp_in_bias, mlp_out, mlp_out_bias, norm_gain, norm_bias, heads_low, heads_f, *consts,
    )

    turns = 4

    def shares(*shape):
        shape = (shape[0] // turns,) + shape[1:]
        return pl.BlockSpec(shape, lambda i: (i,) + (0,) * (len(shape) - 1))

    piece = width * 2 // turns
    per = turns // 2
    whole = lambda x: fixed(x.shape)
    f32 = lambda x: jax.ShapeDtypeStruct(x.shape, F32)
    output, input_grad, grad_inner, grad_outer, grad_bias, grad_up, grad_up_bias, grad_down, *rest = pl.pallas_call(
        functools.partial(finish_kernel, segs, lvars),
        grid=(turns,),
        in_specs=[
            shares(*arrived.shape), shares(*input_grad.shape), whole(small),
            shares(*inner_low.shape), shares(*outer_low.shape),
            pl.BlockSpec((1, 2, piece, width), lambda i: (i // per, 0, i % per, 0)),
            shares(*down_low.shape), shares(*route_low.shape), whole(consts[1]),
        ],
        out_specs=[
            shares(*tokens.shape), shares(*input_grad.shape), shares(*inner_low.shape), shares(*outer_low.shape), whole(attn_bias),
            pl.BlockSpec((1, piece, hidden), lambda i: (i // per, i % per, 0)), whole(mlp_in_bias),
            shares(*down_low.shape), whole(mlp_out_bias), whole(norm_gain), whole(norm_bias), shares(*route_low.shape),
        ],
        out_shape=[
            f32(tokens), f32(input_grad), f32(inner_low), f32(outer_low), f32(attn_bias), f32(mlp_in), f32(mlp_in_bias),
            f32(down_low), f32(mlp_out_bias), f32(norm_gain), f32(norm_bias), f32(route_low),
        ],
        compiler_params=pltpu.CompilerParams(dimension_semantics=("arbitrary",), vmem_limit_bytes=VMEM_LIMIT),
        name="finish",
    )(
        arrived, input_grad, small, inner_low, outer_low, up_low.reshape(2, 2, width, width), down_low,
        route_low, consts[1],
    )
    grad_down_bias, grad_gain, grad_shift, grad_router = rest
    return (
        output, input_grad.reshape(tokens.shape), grad_inner.reshape(attn_inner.shape),
        grad_outer.reshape(attn_outer.shape), grad_bias, grad_up, grad_up_bias, grad_down.reshape(mlp_out.shape),
        grad_down_bias, grad_gain, grad_shift, grad_router.reshape(routers, segs, width).transpose(1, 0, 2),
    )


def solution(mesh):
    split = P("seg", "var", None, None)
    in_specs = (split, P("seg")) + (P(),) * 13 + (split,)
    out_specs = (split, split) + (P(),) * 10
    var_size, seg_size = mesh.shape["var"], mesh.shape["seg"]
    return jax.shard_map(
        functools.partial(on_device, var_size, seg_size),
        mesh=mesh, in_specs=in_specs, out_specs=out_specs, check_vma=False,
    )
```

```python
import functools

import jax
import jax.numpy as jnp
import numpy as np
from jax import lax
from jax.experimental import pallas as pl
from jax.experimental.pallas import tpu as pltpu
from jax.sharding import PartitionSpec as P

HEADS = 8
SLOTS = 16
EPS = 1e-05
MASKED = -1e30
MESH = pl.DeviceIdType.MESH
F32 = jnp.float32
LOW = jnp.bfloat16
VMEM_LIMIT = 60 * 1024 * 1024


OUT_ROUNDS = (-2, 0, 2, 4, 8, 12, 16, 18)
ATTN_ROUNDS = (0, 2, 9, 14, 17, 19, 21)
ROUTE_ROUNDS = (1, 3, 12, 16, 18, 20, 22)
FEED_ROUNDS = (12, 14, 16, 18, 20, 22, 24)
TIME_ROUNDS = (16, 17, 19, 22, 23)
ATTN_AXES = ("core", "plane", "z")
ROUTE_AXES = ("core", "plane", "z")
FEED_AXES = ("core", "plane", "z")

TOGETHER = (2, 2, 2, 2, 2)
AHEAD = 1


def mm(a, b):
    return jnp.dot(a, b, preferred_element_type=F32)


def mm_nt(a, b):
    return lax.dot_general(a, b, (((1,), (1,)), ((), ())), preferred_element_type=F32)


def mm_tn(a, b):
    return lax.dot_general(a, b, (((0,), (0,)), ((), ())), preferred_element_type=F32)


def ln_stats(a):
    mean = jnp.mean(a, axis=1, keepdims=True)
    center = a - mean
    var = jnp.mean(center * center, axis=1, keepdims=True)
    rstd = lax.rsqrt(var + EPS)
    return center * rstd, rstd


def ln_back(g, xhat, rstd, gain):
    gy = g * gain
    first = jnp.mean(gy, axis=1, keepdims=True)
    second = jnp.mean(gy * xhat, axis=1, keepdims=True)
    return rstd * (gy - first - xhat * second)


def gelu_both(z):
    k0 = np.float32(np.sqrt(2.0 / np.pi))
    k1 = np.float32(0.044715)
    square = z * z
    t = jnp.tanh(k0 * z * (1.0 + k1 * square))
    half = 0.5 * (1.0 + t)
    slope = half + 0.5 * z * (1.0 - t * t) * (k0 * (1.0 + 3.0 * k1 * square))
    return z * half, slope


def col_sum(x):
    return jnp.sum(x.astype(F32), axis=0, keepdims=True)


def spread_heads(x, heads_ref):
    return jnp.concatenate([x * heads_ref[h : h + 1, :] for h in range(HEADS)], axis=0)


def gather_heads(x, headsf_ref, rows):
    total = x[:rows] * headsf_ref[0:1, :]
    for h in range(1, HEADS):
        total = total + x[h * rows : (h + 1) * rows] * headsf_ref[h : h + 1, :]
    return total


def time_forward(
    lvars, b, several, tok_ref, offsets, factors, wi_ref, wo_ref, ab_ref, win_ref, bin_ref, wout_ref, bout_ref,
    gain_ref, shift_ref, heads_ref, headsf_ref, kept,
):
    q_ref, k_ref, v_ref, p_ref, tc_ref, x1_ref, r1_ref, f1_ref, s1_ref, x2_ref, r2_ref = kept
    segs, width = tok_ref.shape[2:]
    rows = lvars * segs
    scale = np.float32((width // HEADS) ** (-0.5))

    def keep(ref, value):
        ref[pl.ds(b, several)] = value.reshape(several, rows, value.shape[1])

    start = jnp.concatenate(
        [(tok_ref[b + i].reshape(rows, width).astype(F32) - offsets[i]) * factors[i] for i in range(several)], axis=0
    )
    low = start.astype(LOW)
    query = (mm(low, wi_ref[0, 0]) + ab_ref[0, 0:1, :]).astype(LOW)
    key = mm(low, wi_ref[0, 1]).astype(LOW)
    value = (mm(low, wi_ref[0, 2]) + ab_ref[0, 1:2, :]).astype(LOW)
    keep(q_ref, query)
    keep(k_ref, key)
    keep(v_ref, value)
    probs, contexts = [], []
    for v in range(several * lvars):
        part = slice(v * segs, (v + 1) * segs)
        scores = mm_nt(key[part], spread_heads(query[part], heads_ref))
        top = jnp.max(scores, axis=0, keepdims=True)
        expo = jnp.exp((scores - top) * scale)
        prob = (expo / jnp.sum(expo, axis=0, keepdims=True)).astype(LOW)
        probs.append(prob)
        contexts.append(gather_heads(mm_tn(prob, value[part]), headsf_ref, segs).astype(LOW))
    keep(p_ref, jnp.concatenate(probs, axis=0))
    context = jnp.concatenate(contexts, axis=0)
    keep(tc_ref, context)
    a1 = start + mm(context, wo_ref[0]) + ab_ref[0, 2:3, :]
    x1, r1 = ln_stats(a1)
    keep(x1_ref, x1.astype(LOW))
    keep(r1_ref, jnp.broadcast_to(r1, (several * rows, 128)))
    t1 = x1 * gain_ref[0:1, :] + shift_ref[0:1, :]
    act, slope = gelu_both(mm(t1.astype(LOW), win_ref[0]) + bin_ref[0:1, :])
    f1 = act.astype(LOW)
    keep(f1_ref, f1)
    keep(s1_ref, slope.astype(LOW))
    a2 = t1 + mm(f1, wout_ref[0]) + bout_ref[0:1, :]
    x2, r2 = ln_stats(a2)
    keep(x2_ref, x2.astype(LOW))
    keep(r2_ref, jnp.broadcast_to(r2, (several * rows, 128)))
    return (x2 * gain_ref[1:2, :] + shift_ref[1:2, :]).astype(LOW)


B_SK, B_SV, B_RQ, B_RK, B_RV, B_O1, B_ROWS = [256 * i for i in range(7)]
R_IN, R_OUT, R_O2, R_KQ = [256 * i for i in (0, 2, 4, 5)]
M_IN, M_OUT, M_V, M_O, M_ROWS = [256 * i for i in (0, 2, 4, 5, 6)]
T_Q, T_K, T_ROWS = [256 * i for i in (0, 1, 2)]
S_BIAS, S_IN, S_OUT, S_GAIN, S_SHIFT, S_ROWS = 0, 9, 13, 15, 19, 32


def router_start(places, router_ref, wi_ref, ab_ref, grow_ref, mask_ref, attn_ref, rest_ref, qx_ref, kq_ref):
    attn_ref[...] = jnp.zeros(attn_ref.shape, F32)
    rest_ref[...] = jnp.zeros(rest_ref.shape, F32)
    kq_ref[...] = jnp.zeros(kq_ref.shape, F32)
    mine = mm(places, router_ref[...]).astype(LOW)
    sq = (mm(mine, wi_ref[1, 0]) + ab_ref[1, 0:1, :]).astype(LOW)
    qx_ref[...] = expand(sq, grow_ref, mask_ref)


def router_end(lsegs, routers, var_size, first_seg, shrink_ref, mask_ref, rest_ref, small_ref, kq_ref):
    kq = contract(kq_ref[...], shrink_ref, mask_ref)
    small_ref[S_BIAS + 3 : S_BIAS + 4, :] = col_sum(kq)
    places = own_places(lsegs, routers, var_size, first_seg, 0)
    rest_ref[R_KQ : R_KQ + places.shape[0], :] = mm(places, kq.astype(LOW))


def own_places(lsegs, routers, var_size, first_seg, whole):
    shape = [lsegs * SLOTS] * 2
    shape[whole] = routers * lsegs * var_size
    there = lax.broadcasted_iota(jnp.int32, shape, whole)
    here = lax.broadcasted_iota(jnp.int32, shape, 1 - whole)
    here = lax.div(here, lsegs) * (lsegs * var_size) + lax.rem(here, lsegs) + first_seg
    return jnp.where(there == here, 1.0, 0.0).astype(LOW)


def expand(x, grow_ref, mask_ref):
    width = x.shape[1]
    return (mm(grow_ref[...], x).astype(LOW).reshape(-1, 16, width) * mask_ref[...][None]).reshape(-1, width)


def contract(x, shrink_ref, mask_ref):
    width = x.shape[1]
    return mm(shrink_ref[...], (x.astype(LOW).reshape(-1, 16, width) * mask_ref[...][None]).reshape(-1, width))


def router_part(
    lsegs, nvars, routers, several, arrived, leaving,
    limits, wi_ref, wo_ref, ab_ref, win_ref, bin_ref, wout_ref, bout_ref,
    gain_ref, shift_ref, mask_ref, grow_ref, shrink_ref, sumr_ref, perm_ref, back_ref,
    attn_ref, rest_ref, small_ref, qx_ref, kq_ref,
):
    series, width = perm_ref.shape[0], wo_ref.shape[1]
    rows = several * series
    lanes = SLOTS * HEADS
    scale = np.float32((width // HEADS) ** (-0.5))
    parts = range(several * lsegs)
    ns = [slice(j * nvars, (j + 1) * nvars) for j in parts]
    ls = [slice(j * lanes, (j + 1) * lanes) for j in parts]
    qs = [slice(j % lsegs * lanes, (j % lsegs + 1) * lanes) for j in parts]

    def cat(blocks):
        return jnp.concatenate(list(blocks), axis=0)

    def each(f, x):
        size = x.shape[0] // several
        return cat(f(x[i * size : (i + 1) * size]) for i in range(several))

    def grown(x):
        return each(lambda y: expand(y, grow_ref, mask_ref), x)

    def shrunk(blocks):
        return cat(contract(cat(blocks[i * lsegs : (i + 1) * lsegs]), shrink_ref, mask_ref) for i in range(several))

    def permuted(ref, x):
        return each(lambda y: mm(ref[...], y), x)

    t2 = permuted(perm_ref, arrived(0)).astype(LOW)
    sk = mm(t2, wi_ref[1, 1]).astype(LOW)
    sv = (mm(t2, wi_ref[1, 2]) + ab_ref[1, 1:2, :]).astype(LOW)
    rq = (mm(t2, wi_ref[2, 0]) + ab_ref[2, 0:1, :]).astype(LOW)
    var = lax.broadcasted_iota(jnp.int32, (nvars, lanes), 0)
    valid = [var < limit for limit in limits]

    def send_prob(j):
        real = valid[j // lsegs]
        scores = jnp.where(real, mm_nt(sk[ns[j]], qx_ref[qs[j], :]), MASKED)
        top = jnp.max(scores, axis=0, keepdims=True)
        expo = jnp.where(real, jnp.exp((scores - top) * scale), 0.0)
        return expo / jnp.sum(expo, axis=0, keepdims=True)

    sp = [send_prob(j) for j in parts]
    sp_low = [x.astype(LOW) for x in sp]
    pre_low = shrunk([mm_tn(sp_low[j], sv[ns[j]]) for j in parts]).astype(LOW)
    buffer = (mm(pre_low, wo_ref[1]) + ab_ref[1, 2:3, :]).astype(LOW)
    rkx = grown(mm(buffer, wi_ref[2, 1]).astype(LOW))
    rvx = grown((mm(buffer, wi_ref[2, 2]) + ab_ref[2, 1:2, :]).astype(LOW))
    scores = cat(mm_nt(rq[ns[j]], rkx[ls[j]]) for j in parts)
    real = lax.broadcasted_iota(jnp.int32, (rows, lanes), 1) < routers * HEADS
    scores = jnp.where(real, scores, MASKED)
    top = scores
    shift = lanes // 2
    while shift >= HEADS:
        top = jnp.maximum(top, pltpu.roll(top, shift, 1))
        shift //= 2
    expo = jnp.where(real, jnp.exp((scores - top) * scale), 0.0)
    rp = expo / mm(expo.astype(LOW), sumr_ref[...])
    rp_low = rp.astype(LOW)
    rc = cat(mm(rp_low[ns[j]], rvx[ls[j]]) for j in parts).astype(LOW)
    a3 = t2.astype(F32) + mm(rc, wo_ref[2]) + ab_ref[2, 2:3, :]
    x3, r3 = ln_stats(a3)
    t3 = x3 * gain_ref[2:3, :] + shift_ref[2:3, :]
    t3_low = t3.astype(LOW)
    act, slope = gelu_both(mm(t3_low, win_ref[1]) + bin_ref[1:2, :])
    f2 = act.astype(LOW)
    a4 = t3 + mm(f2, wout_ref[1]) + bout_ref[1:2, :]
    x4, r4 = ln_stats(a4)
    out = (x4 * gain_ref[3:4, :] + shift_ref[3:4, :]).astype(LOW)
    leaving(3, permuted(back_ref, out).astype(LOW))

    def add(row, value, ref=attn_ref):
        ref[row : row + value.shape[0], :] += value

    def add_small(row, value):
        small_ref[row : row + 1, :] += value

    cot = permuted(perm_ref, arrived(1))
    add_small(S_GAIN + 3, col_sum(cot * x4))
    add_small(S_SHIFT + 3, col_sum(cot))
    g4 = ln_back(cot, x4, r4, gain_ref[3:4, :])
    e4 = g4.astype(LOW)
    add(R_OUT, mm_tn(f2, e4), rest_ref)
    add_small(S_OUT + 1, col_sum(e4))
    e3 = (slope * mm_nt(e4, wout_ref[1])).astype(LOW)
    add(R_IN, mm_tn(t3_low, e3[:, :width]), rest_ref)
    add(R_IN + width, mm_tn(t3_low, e3[:, width:]), rest_ref)
    e3_sum = col_sum(e3)
    add_small(S_IN + 2, e3_sum[:, :width])
    add_small(S_IN + 3, e3_sum[:, width:])
    g3 = g4 + mm_nt(e3, win_ref[1])
    add_small(S_GAIN + 2, col_sum(g3 * x3))
    add_small(S_SHIFT + 2, col_sum(g3))
    g3 = ln_back(g3, x3, r3, gain_ref[2:3, :])
    eo = g3.astype(LOW)
    add(R_O2, mm_tn(rc, eo), rest_ref)
    add_small(S_BIAS + 8, col_sum(eo))
    ec = mm_nt(eo, wo_ref[2]).astype(LOW)
    dp = cat(mm_nt(ec[ns[j]], rvx[ls[j]]) for j in parts)
    ds = (scale * rp * (dp - mm((rp * dp).astype(LOW), sumr_ref[...]))).astype(LOW)
    erk = shrunk([mm_tn(ds[ns[j]], rq[ns[j]]) for j in parts]).astype(LOW)
    erv = shrunk([mm_tn(rp_low[ns[j]], ec[ns[j]]) for j in parts]).astype(LOW)
    erq = cat(mm(ds[ns[j]], rkx[ls[j]]) for j in parts).astype(LOW)
    eb = (mm_nt(erk, wi_ref[2, 1]) + mm_nt(erv, wi_ref[2, 2])).astype(LOW)
    epx = grown(mm_nt(eb, wo_ref[1]).astype(LOW))
    add(B_RQ, mm_tn(t2, erq))
    add_small(S_BIAS + 6, col_sum(erq))
    add(B_RK, mm_tn(buffer, erk))
    add(B_RV, mm_tn(buffer, erv))
    add_small(S_BIAS + 7, col_sum(erv))
    add(B_O1, mm_tn(pre_low, eb))
    add_small(S_BIAS + 5, col_sum(eb))
    dss = []
    for j in parts:
        weighted = sp[j] * mm_nt(sv[ns[j]], epx[ls[j]])
        center = jnp.sum(weighted, axis=0, keepdims=True)
        dss.append((scale * (weighted - sp[j] * center)).astype(LOW))
    esv = cat(mm(sp_low[j], epx[ls[j]]) for j in parts).astype(LOW)
    esk = cat(mm(dss[j], qx_ref[qs[j], :]) for j in parts).astype(LOW)
    g2 = g3 + mm_nt(erq, wi_ref[2, 0]) + mm_nt(esk, wi_ref[1, 1]) + mm_nt(esv, wi_ref[1, 2])
    leaving(2, permuted(back_ref, g2.astype(LOW)).astype(LOW))
    for s in range(lsegs):
        total = mm_tn(dss[s], sk[ns[s]])
        for i in range(1, several):
            total = total + mm_tn(dss[i * lsegs + s], sk[ns[i * lsegs + s]])
        kq_ref[qs[s], :] += total
    add(B_SK, mm_tn(t2, esk))
    add(B_SV, mm_tn(t2, esv))
    add_small(S_BIAS + 4, col_sum(esv))


def feed_backward(
    lvars, b, several, arrived, tok_ref, offsets, factors, wo_ref, win_ref, wout_ref, gain_ref, shift_ref, heads_ref,
    perm_ref, kept, feeds_ref, small_ref, etc_ref, g1_ref,
):
    q_ref, k_ref, v_ref, p_ref, tc_ref, x1_ref, r1_ref, f1_ref, s1_ref, x2_ref, r2_ref = kept
    segs, width = tok_ref.shape[2:]
    rows = lvars * segs

    def add(ref, row, value):
        ref[row : row + value.shape[0], :] += value

    def held(ref):
        return ref[pl.ds(b, several)].reshape(several * rows, ref.shape[2])

    def keep(ref, value):
        ref[pl.ds(b, several)] = value.reshape(several, rows, value.shape[1])

    def wide(ref):
        return jnp.concatenate([held(ref)] * (width // 128), axis=1)

    g2 = arrived(2)
    g2 = jnp.concatenate([mm(perm_ref[...], g2[i * rows : (i + 1) * rows]) for i in range(several)], axis=0)
    x2 = held(x2_ref).astype(F32)
    add(small_ref, S_GAIN + 1, col_sum(g2 * x2))
    add(small_ref, S_SHIFT + 1, col_sum(g2))
    g2 = ln_back(g2, x2, wide(r2_ref), gain_ref[1:2, :])
    e2 = g2.astype(LOW)
    add(feeds_ref, M_OUT, mm_tn(held(f1_ref), e2))
    add(small_ref, S_OUT, col_sum(e2))
    e1 = (held(s1_ref).astype(F32) * mm_nt(e2, wout_ref[0])).astype(LOW)
    x1 = held(x1_ref).astype(F32)
    t1 = (x1 * gain_ref[0:1, :] + shift_ref[0:1, :]).astype(LOW)
    add(feeds_ref, M_IN, mm_tn(t1, e1[:, :width]))
    add(feeds_ref, M_IN + width, mm_tn(t1, e1[:, width:]))
    e1_sum = col_sum(e1)
    add(small_ref, S_IN, e1_sum[:, :width])
    add(small_ref, S_IN + 1, e1_sum[:, width:])
    g1 = g2 + mm_nt(e1, win_ref[0])
    add(small_ref, S_GAIN, col_sum(g1 * x1))
    add(small_ref, S_SHIFT, col_sum(g1))
    g1 = ln_back(g1, x1, wide(r1_ref), gain_ref[0:1, :])
    keep(g1_ref, g1)
    et = g1.astype(LOW)
    add(feeds_ref, M_O, mm_tn(held(tc_ref), et))
    add(small_ref, S_BIAS + 2, col_sum(et))
    etc = mm_nt(et, wo_ref[0]).astype(LOW)
    keep(etc_ref, etc)
    prob = held(p_ref)
    grads = []
    for v in range(several * lvars):
        part = slice(v * segs, (v + 1) * segs)
        grads.append(mm(prob[part], spread_heads(etc[part], heads_ref)).astype(LOW))
    gv = jnp.concatenate(grads, axis=0)
    keep(tc_ref, gv)
    low = start_low(lvars, b, several, tok_ref, offsets, factors)
    add(feeds_ref, M_V, mm_tn(low, gv))
    add(small_ref, S_BIAS + 1, col_sum(gv))


def start_low(lvars, b, several, tok_ref, offsets, factors):
    segs, width = tok_ref.shape[2:]
    tok = [tok_ref[b + i].reshape(lvars * segs, width).astype(F32) for i in range(several)]
    return jnp.concatenate([((tok[i] - offsets[i]) * factors[i]).astype(LOW) for i in range(several)], axis=0)


def time_backward(
    lvars, b, several, tok_ref, offsets, factors, heads_ref, headsf_ref, kept, times_ref, small_ref, etc_ref
):
    q_ref, k_ref, v_ref, p_ref = kept[:4]
    segs, width = tok_ref.shape[2:]
    rows = lvars * segs
    scale = np.float32((width // HEADS) ** (-0.5))

    def add(ref, row, value):
        ref[row : row + value.shape[0], :] += value

    def held(ref):
        return ref[pl.ds(b, several)].reshape(several * rows, ref.shape[2])

    def keep(ref, value):
        ref[pl.ds(b, several)] = value.reshape(several, rows, value.shape[1])

    etc, query, key, value, probs = held(etc_ref), held(q_ref), held(k_ref), held(v_ref), held(p_ref)
    grads_q, grads_k = [], []
    for v in range(several * lvars):
        part = slice(v * segs, (v + 1) * segs)
        prob = probs[part].astype(F32)
        weighted = prob * mm_nt(value[part], spread_heads(etc[part], heads_ref))
        ets = (weighted - prob * jnp.sum(weighted, axis=0, keepdims=True)).astype(LOW)
        grads_k.append((scale * mm(ets, spread_heads(query[part], heads_ref))).astype(LOW))
        grads_q.append((scale * gather_heads(mm_tn(ets, key[part]), headsf_ref, segs)).astype(LOW))
    gq = jnp.concatenate(grads_q, axis=0)
    gk = jnp.concatenate(grads_k, axis=0)
    keep(q_ref, gq)
    keep(k_ref, gk)
    low = start_low(lvars, b, several, tok_ref, offsets, factors)
    add(times_ref, T_Q, mm_tn(low, gq))
    add(times_ref, T_K, mm_tn(low, gk))
    add(small_ref, S_BIAS, col_sum(gq))


class Sum:
    def __init__(self, axes, second, acc, send, total, recv, sems):
        self.second = second
        self.acc, self.send, self.total, self.recv, self.sems = acc, send, total, recv, sems
        self.plan = []
        start, size = 0, acc.shape[0]
        for index, count, target, peer, order in axes:
            size //= count
            self.plan.append((index, count, target, start, size, peer, order))
            start = start + index * size
        self.levels = len(self.plan)
        self.last = 2 * self.levels

    @staticmethod
    def scratch(rows, width, counts):
        recv, size = [], rows
        for count in counts:
            size //= count
            recv.append(pltpu.VMEM((count - 1, size, width), LOW))
        copies = sum(counts) - len(counts)
        return [
            pltpu.VMEM((rows, width), F32), pltpu.VMEM((rows, width), LOW), pltpu.VMEM((rows, width), LOW),
            *[pltpu.SemaphoreType.DMA((copies,))] * 4, *recv,
        ]

    def rows(self, start, size):
        return pl.ds(start if isinstance(start, int) else pl.multiple_of(start, 16), size)

    def copies(self, level, gather):
        send_sem, recv_sem = self.sems[2:] if gather else self.sems[:2]
        index, count, target, start, size, peer_at, order = self.plan[level]
        first = sum(entry[1] - 1 for entry in self.plan[:level])
        found = []
        for k, k_second in zip(*order):
            k = jnp.where(self.second, k_second, k)
            peer = peer_at(k)
            rows = self.rows(start + (index if gather else peer) * size, size)
            copy = pltpu.make_async_remote_copy(
                src_ref=(self.total if gather else self.send).at[rows, :],
                dst_ref=self.total.at[rows, :] if gather else self.recv[level].at[k - 1],
                send_sem=send_sem.at[first + k - 1],
                recv_sem=recv_sem.at[first + k - 1],
                device_id=target(peer),
                device_id_type=MESH,
            )
            found.append((copy, rows))
        return found

    def advance(self, turn):
        levels = self.levels
        if 0 < turn <= levels:
            for copy, _ in self.copies(turn - 1, False):
                copy.wait()
            index, count, _, start, size = self.plan[turn - 1][:5]
            mine = self.rows(start + index * size, size)
            value = self.acc[mine, :]
            for k in range(count - 1):
                value = value + self.recv[turn - 1][k].astype(F32)
            if turn < levels:
                self.acc[mine, :] = value
            else:
                self.total[mine, :] = value.astype(LOW)
        elif turn > levels:
            for copy, _ in self.copies(self.last - turn, True):
                copy.wait()
        if turn < levels:
            for copy, rows in self.copies(turn, False):
                self.send[rows, :] = self.acc[rows, :].astype(LOW)
                copy.start()
        elif turn < self.last:
            for copy, _ in self.copies(self.last - 1 - turn, True):
                copy.start()

    @property
    def turns(self):
        return self.last + 1


class SmallSum:
    def __init__(self, acc, sent, recvs, sems, places):
        self.acc, self.sent, self.recvs, self.sems, self.places = acc, sent, recvs, sems, places

    @staticmethod
    def scratch(rows, width, sizes):
        return [
            pltpu.VMEM((rows, width), F32), pltpu.VMEM((len(sizes), rows, width), LOW),
            *[pltpu.VMEM((size, rows, width), LOW) for size in sizes],
            *[pltpu.SemaphoreType.DMA((size,)) for size in sizes for _ in range(2)],
        ]

    def copies(self, stage):
        name, me, size = self.places[stage]
        send_sem, recv_sem = self.sems[2 * stage : 2 * stage + 2]
        return [
            pltpu.make_async_remote_copy(
                src_ref=self.sent.at[stage],
                dst_ref=self.recvs[stage].at[me],
                send_sem=send_sem.at[k],
                recv_sem=recv_sem.at[k],
                device_id={name: lax.rem(me + k, size)},
                device_id_type=MESH,
            )
            for k in range(1, size)
        ]

    def start(self, stage):
        value = self.acc[...].astype(LOW)
        self.sent[stage] = value
        self.recvs[stage][self.places[stage][1]] = value
        for copy in self.copies(stage):
            copy.start()

    def finish(self, stage):
        for copy in self.copies(stage):
            copy.wait()
        value = self.recvs[stage][0].astype(F32)
        for k in range(1, self.places[stage][2]):
            value = value + self.recvs[stage][k].astype(F32)
        self.acc[...] = value


def layer_kernel(
    lvars, lsegs, nvars, routers, steps, var_size, seg_size, sizes, groups, shares,
    dom_ref, cnt_ref, tok_ref, cot_ref, mean_ref, scale_ref, router_ref, wi_ref, wo_ref, ab_ref,
    win_ref, bin_ref, wout_ref, bout_ref, gain_ref, shift_ref, heads_ref, headsf_ref, split_ref, join_ref, mask_ref, grow_ref, shrink_ref, sumr_ref, swap_ref, back_ref,
    small_out_ref, out_ref, gin_ref, inner_ref, outer_ref, up_ref, down_ref, route_ref,
    sent_ref, came_ref, qx_ref, kq_ref, etc_ref, g1_ref, made_ref, send_sem, recv_sem, out_sem, *scratch,
):
    me = lax.axis_index("var")
    seg = lax.axis_index("seg")
    width = tok_ref.shape[3]
    rows = lvars * tok_ref.shape[2]
    block = rows // var_size
    kept, scratch = scratch[:11], scratch[11:]
    cores, xs, ys, zs = sizes
    core, xi = lax.rem(seg, cores), lax.div(seg, cores)
    yi, zi = lax.rem(me, ys), lax.div(me, ys)

    def space(i):
        return {"seg": lax.rem(i, xs) * cores + core, "var": lax.div(i, xs)}

    def step(i, k, count):
        return lax.rem(i + k, count)

    def both_ways(count):
        return list(range(1, count)), list(range(count - 1, 0, -1))

    def line(index, count, target):
        return index, count, target, lambda k: step(index, k, count), both_ways(count)

    def plane_peer(k):
        return step(yi, lax.div(k, xs), ys) * xs + step(xi, lax.rem(k, xs), xs)

    def space_peer(k):
        return step(zi, lax.div(k, xs * ys), zs) * (xs * ys) + plane_peer(lax.rem(k, xs * ys))

    axes = {
        "core": line(core, cores, lambda i: {"seg": xi * cores + i}),
        "plane": (
            yi * xs + xi, xs * ys, lambda i: space(zi * (xs * ys) + i), plane_peer,
            [sorted(range(1, xs * ys), key=lambda k: (k // xs > 0 and k % xs > 0, turn * k)) for turn in (1, -1)],
        ),
        "z": line(zi, zs, lambda i: {"var": i * ys + yi}),
        "space": (me * xs + xi, var_size * xs, space, space_peer, both_ways(var_size * xs)),
    }
    second = core > 0
    sums = []
    for _, names in groups:
        used = 7 + len(names)
        group, scratch = scratch[:used], scratch[used:]
        sums.append(Sum([axes[name] for name in names], second, group[0], group[1], group[2], group[7:], group[3:7]))
    parts = []
    for index, base, count in shares:
        parts.append((sums[index], base, sums[index].acc.at[pl.ds(base, count), :]))
    attns, routes, feeds, times = parts
    small = SmallSum(scratch[0], scratch[1], scratch[2:4], scratch[4:8], [("seg", seg, seg_size), ("var", me, var_size)])

    def copy(kind, b, k):
        target = lax.rem(me + k, var_size)
        return pltpu.make_async_remote_copy(
            src_ref=sent_ref.at[kind, b, target],
            dst_ref=came_ref.at[kind, b, me],
            send_sem=send_sem.at[kind, b],
            recv_sem=recv_sem.at[kind, b],
            device_id={"var": target},
            device_id_type=MESH,
        )

    def whole(kind, b):
        others = pl.ds(0, var_size - 1)
        return pltpu.make_async_remote_copy(
            src_ref=sent_ref.at[kind, b, others],
            dst_ref=came_ref.at[kind, b, others],
            send_sem=send_sem.at[kind, b],
            recv_sem=recv_sem.at[kind, b],
            device_id={"var": lax.rem(me + 1, var_size)},
            device_id_type=MESH,
        )

    def store(kind, b, several, value):
        value = value.reshape(several, var_size, block, width)
        sent_ref[kind, pl.ds(b, several)] = value
        for i in range(several):
            came_ref[kind, b + i, me] = sent_ref[kind, b + i, me]

    def send(kind, b, several=1):
        for i in range(several):
            for k in range(1, var_size):
                copy(kind, b + i, k).start()

    def pick(b, ref):
        total = jnp.zeros((1, width), F32)
        for d in range(ref.shape[0]):
            total = total + jnp.where(dom_ref[b] == d, ref[d : d + 1, :], 0.0)
        return total

    def picks(b, several, ref):
        return [pick(b + i, ref) for i in range(several)]

    def arrived(kind, b, several):
        for i in range(several):
            whole(kind, b + i).wait_recv()
        return came_ref[kind, pl.ds(b, several)].reshape(several * rows, width)

    pieces = [
        (times, T_Q, 2 * width, inner_ref, 0), (feeds, M_V, width, inner_ref, 2 * width), (None, 0, width, inner_ref, 3 * width),
        (attns, B_SK, 5 * width, inner_ref, 4 * width),
        (feeds, M_O, width, outer_ref, 0), (attns, B_O1, width, outer_ref, width), (routes, R_O2, width, outer_ref, 2 * width),
        (feeds, M_IN, 2 * width, up_ref, 0), (routes, R_IN, 2 * width, up_ref, 2 * width),
        (feeds, M_OUT, 2 * width, down_ref, 0), (routes, R_OUT, 2 * width, down_ref, 2 * width),
        (None, width, route_ref.shape[0], route_ref, 0),
    ]

    def deliver(which):
        return [
            pltpu.make_async_copy(
                (made_ref if part is None else which.total).at[pl.ds((0 if part is None else part[1]) + row, count), :],
                ref.at[pl.ds(there, count), :],
                out_sem.at[index],
            )
            for index, (part, row, count, ref, there) in enumerate(pieces)
            if (routes if part is None else part)[0] is which
        ]

    def make_routes():
        total, base, _ = routes
        kq = total.total[base + R_KQ : base + R_KQ + route_ref.shape[0], :]
        made_ref[:width, :] = mm_tn(router_ref[...], kq).astype(LOW)
        made_ref[width:, :] = mm_nt(kq, wi_ref[1, 0]).astype(LOW)

    def series_out(kind, b):
        source, ref = ((came_ref.at[3, b], out_ref), (etc_ref.at[b], gin_ref))[kind]
        return pltpu.make_async_copy(source, ref.at[b], out_sem.at[len(pieces) + kind * steps + b])

    barrier = pltpu.get_barrier_semaphore()
    spaces = axes["space"][1]
    for k in range(1, spaces):
        pl.semaphore_signal(barrier, inc=1, device_id=space(lax.rem(axes["space"][0] + k, spaces)), device_id_type=MESH)
    for k in range(1, cores):
        for i in range(xs):
            peer = {"seg": i * cores + lax.rem(core + k, cores)}
            pl.semaphore_signal(barrier, inc=1, device_id=peer, device_id_type=MESH)
    small.acc[...] = jnp.zeros_like(small.acc)
    router_start(
        own_places(lsegs, routers, var_size, me * lsegs, 1), router_ref, wi_ref, ab_ref, grow_ref, mask_ref, attns[2], routes[2], qx_ref, kq_ref
    )
    feeds[2][...] = jnp.zeros(feeds[2].shape, F32)
    times[2][...] = jnp.zeros(times[2].shape, F32)
    pl.semaphore_wait(barrier, spaces - 1 + (cores - 1) * xs)

    def forward(b, several):
        for i in range(several):
            store(1, b + i, 1, mm(split_ref[...], cot_ref[b + i].reshape(rows, width)).astype(LOW))
        send(1, b, several)
        t2 = time_forward(
            lvars, b, several, tok_ref, picks(b, several, mean_ref), picks(b, several, scale_ref), wi_ref, wo_ref,
            ab_ref, win_ref, bin_ref, wout_ref, bout_ref, gain_ref, shift_ref, heads_ref, headsf_ref, kept,
        )
        for i in range(several):
            store(0, b + i, 1, mm(split_ref[...], t2[i * rows : (i + 1) * rows]).astype(LOW))
        send(0, b, several)

    def middle(b, several):
        def leaving(kind, value):
            store(kind, b, several, value)
            if kind == 2:
                send(2, b, several)

        limits = []
        for i in range(several):
            limit = jnp.int32(0)
            for d in range(cnt_ref.shape[0]):
                limit = limit + jnp.where(dom_ref[b + i] == d, cnt_ref[d], 0)
            limits.append(limit)
        router_part(
            lsegs, nvars, routers, several, lambda kind: arrived(kind, b, several), leaving,
            limits, wi_ref, wo_ref, ab_ref, win_ref, bin_ref, wout_ref, bout_ref,
            gain_ref, shift_ref, mask_ref, grow_ref, shrink_ref, sumr_ref, swap_ref, back_ref,
            attns[2], routes[2], small.acc, qx_ref, kq_ref,
        )

    def back_feed(b, several):
        feed_backward(
            lvars, b, several, lambda kind: arrived(kind, b, several), tok_ref, picks(b, several, mean_ref),
            picks(b, several, scale_ref), wo_ref, win_ref, wout_ref, gain_ref, shift_ref, heads_ref, join_ref, kept,
            feeds[2], small.acc, etc_ref, g1_ref,
        )

    def back_time(b, several):
        time_backward(
            lvars, b, several, tok_ref, picks(b, several, mean_ref), picks(b, several, scale_ref), heads_ref, headsf_ref,
            kept, times[2], small.acc, etc_ref,
        )

    def back_input(b, several):
        def held(ref):
            return ref[pl.ds(b, several)].reshape(several * rows, width)

        grad = held(g1_ref) + mm_nt(held(kept[0]), wi_ref[0, 0]) + mm_nt(held(kept[1]), wi_ref[0, 1])
        grad = grad + mm_nt(held(kept[4]), wi_ref[0, 2])
        for i in range(several):
            etc_ref[b + i] = (grad[i * rows : (i + 1) * rows] * pick(b + i, scale_ref)).astype(LOW)
            series_out(1, b + i).start()

    todo = {}

    def plan(total, *rounds):
        for turn in range(total.turns):
            todo.setdefault(rounds[min(turn, len(rounds) - 1)], []).append(functools.partial(total.advance, turn))

    for b, round_ in enumerate(OUT_ROUNDS):
        todo.setdefault(round_, []).append(functools.partial(send, 3, b))
    rounds_of = (ATTN_ROUNDS, ROUTE_ROUNDS, FEED_ROUNDS, TIME_ROUNDS) if len(sums) > 1 else ((2 * steps, 3 * steps),)
    for total, rounds in zip(sums, rounds_of):
        plan(total, *rounds)
    todo.setdefault(2 * steps, []).append(functools.partial(small.start, 0))
    todo.setdefault(2 * steps + steps // 2, []).append(lambda: (small.finish(0), small.start(1)))

    def sweep(run, first, several):
        def body(i, carry):
            b = i * several
            for round_, acts in sorted(todo.items()):
                if first <= round_ < first + steps:

                    @pl.when(i == (round_ - first) // several)
                    def _(acts=acts):
                        for act in acts:
                            act()

            run(b, several)
            return carry

        lax.fori_loop(0, steps // several, body, 0)

    together = TOGETHER if len(sums) > 1 else (1,) * 5
    sweep(forward, -2 * steps, together[0])
    sweep(middle, -steps, together[1])
    router_end(
        lsegs, routers, var_size, me * lsegs, shrink_ref, mask_ref, routes[2], small.acc, kq_ref,
    )
    several = together[2]
    count = steps // several
    early = max(count - AHEAD, 1)

    def backward(i, carry):
        for round_, acts in sorted(todo.items()):
            if 0 <= round_ < 2 * steps:

                @pl.when(i == round_ // several)
                def _(acts=acts):
                    for act in acts:
                        act()

        lead = early + early - 1
        feed = (i < early) | ((i >= lead) & (i < lead + count - early))

        @pl.when(feed)
        def _():
            back_feed(jnp.where(i < early, i, i - lead + early) * several, several)

        @pl.when(jnp.logical_not(feed))
        def _():
            back_time(jnp.where(i < lead, i - early, i - count) * several, several)

        return carry

    lax.fori_loop(0, 2 * count, backward, 0)
    sweep(back_input, 2 * steps, together[4])
    last = [max(rounds[: total.turns]) for total, rounds in zip(sums, rounds_of)]
    for round_ in range(3 * steps, max(max(todo), 3 * steps, *last) + 1):
        for act in todo.get(round_, []):
            act()
        for total, end in zip(sums, last):
            if round_ == max(end, 3 * steps):
                if total is routes[0]:
                    make_routes()
                for copy in deliver(total):
                    copy.start()
    small.finish(1)
    small_out_ref[...] = small.acc[...]
    for b in range(steps):
        whole(3, b).wait_recv()
        series_out(0, b).start()
    for b in range(steps):
        for kind in range(4):
            whole(kind, b).wait_send()
    for total in sums:
        for copy in deliver(total):
            copy.wait()
    for b in range(steps):
        series_out(0, b).wait()
        series_out(1, b).wait()


def finish_kernel(
    segs, lvars, out_ref, gin_ref, small_ref, inner_ref, outer_ref, up_ref, down_ref, route_ref, join_ref,
    output_ref, gin_out_ref, ginner_ref, gouter_ref, gbias_ref, gup_ref, gupb_ref, gdown_ref, gdownb_ref, ggain_ref,
    gshift_ref, groute_ref,
):
    width = inner_ref.shape[1]

    @pl.when(pl.program_id(0) == 0)
    def _():
        for i in range(3):
            gbias_ref[i] = small_ref[S_BIAS + 3 * i : S_BIAS + 3 * i + 3, :]
        for i in range(2):
            for j in range(2):
                row = S_IN + 2 * i + j
                gupb_ref[i : i + 1, j * width : (j + 1) * width] = small_ref[row : row + 1, :]
        gdownb_ref[...] = small_ref[S_OUT : S_OUT + 2, :]
        ggain_ref[...] = small_ref[S_GAIN : S_GAIN + 4, :]
        gshift_ref[...] = small_ref[S_SHIFT : S_SHIFT + 4, :]

    for i in range(out_ref.shape[0]):
        output_ref[i] = mm(join_ref[...], out_ref[i].reshape(lvars * segs, width)).reshape(lvars, segs, width)
    gin_out_ref[...] = gin_ref[...].astype(F32)
    ginner_ref[...] = inner_ref[...].astype(F32)
    gouter_ref[...] = outer_ref[...].astype(F32)
    gup_ref[0, :, :width] = up_ref[0, 0].astype(F32)
    gup_ref[0, :, width:] = up_ref[0, 1].astype(F32)
    gdown_ref[...] = down_ref[...].astype(F32)
    groute_ref[...] = route_ref[...].astype(F32)


def fixed(shape, index=None):
    index = (0,) * len(shape) if index is None else index
    return pl.BlockSpec(shape, lambda b: index)


def on_device(
    var_size, seg_size,
    tokens, domain, counts, domain_mean, domain_scale, attn_inner, attn_outer, attn_bias,
    mlp_in, mlp_in_bias, mlp_out, mlp_out_bias, norm_gain, norm_bias, router, cotangent,
):
    batch, lvars, segs, width = tokens.shape
    routers = router.shape[1]
    hidden = mlp_in.shape[2]
    lsegs = segs // var_size
    nvars = lvars * var_size
    rows = lvars * segs
    lanes = SLOTS * HEADS
    heads = (np.arange(width)[None, :] // (width // HEADS) == np.arange(HEADS)[:, None]).astype(np.float32)
    heads_low = jnp.asarray(heads, LOW)
    heads_f = jnp.asarray(heads, F32)
    mask = jnp.asarray(np.concatenate([heads, heads], axis=0), LOW)
    order = np.arange(rows).reshape(lvars, var_size, lsegs).transpose(1, 0, 2).reshape(-1)
    split = np.eye(rows, dtype=np.float32)[order]
    order = np.arange(rows).reshape(nvars, lsegs).transpose(1, 0).reshape(-1)
    swap = np.eye(rows, dtype=np.float32)[order]
    group = np.arange(lsegs * lanes) // HEADS
    group = group % SLOTS * lsegs + group // SLOTS
    grow = (group[:, None] == np.arange(lsegs * SLOTS)[None, :]).astype(np.float32)
    sumr = (np.arange(lanes)[:, None] % HEADS == np.arange(lanes)[None, :] % HEADS).astype(np.float32)

    kept = [
        ((rows, width), LOW), ((rows, width), LOW), ((rows, width), LOW), ((rows, HEADS * segs), LOW),
        ((rows, width), LOW), ((rows, width), LOW), ((rows, 128), F32), ((rows, hidden), LOW),
        ((rows, hidden), LOW), ((rows, width), LOW), ((rows, 128), F32),
    ]
    routes = router.transpose(1, 0, 2).reshape(routers * segs, width)
    consts = [jnp.asarray(x, LOW) for x in (split, split.T)] + [mask]
    consts += [jnp.asarray(x, LOW) for x in (grow, grow.T, sumr, swap, swap.T)]

    cores = 2 if seg_size % 2 == 0 else 1
    xs = seg_size // cores
    ys = xs if var_size % xs == 0 else 1
    zs = var_size // ys
    sizes = (cores, xs, ys, zs)
    counts_of = {"core": cores, "plane": xs * ys, "z": zs, "space": var_size * xs}
    far = ("core", "plane", "z")
    near = ("core", "space") if var_size * xs <= 16 else far
    unit = 16 * var_size * seg_size
    wanted = [(B_ROWS, ATTN_AXES), (R_KQ + segs * routers, ROUTE_AXES), (M_ROWS, FEED_AXES), (T_ROWS, near)]
    if unit > 1024:
        starts = np.cumsum([0] + [count for count, _ in wanted])
        parts = [(0, int(start), count) for start, (count, _) in zip(starts, wanted)]
        wanted = [(int(starts[-1]), far)]
    else:
        parts = [(index, 0, count) for index, (count, _) in enumerate(wanted)]
    groups = []
    for count, names in wanted:
        groups.append((-(-count // unit) * unit, [name for name in names if counts_of[name] > 1]))
    scalars = pl.BlockSpec(memory_space=pltpu.SMEM)
    anywhere = pl.BlockSpec(memory_space=pl.ANY)
    out_shapes = [
        jax.ShapeDtypeStruct((S_ROWS, width), F32),
        jax.ShapeDtypeStruct((batch, var_size, rows // var_size, width), LOW),
        jax.ShapeDtypeStruct((batch, rows, width), LOW),
        jax.ShapeDtypeStruct((9 * width, width), LOW),
        jax.ShapeDtypeStruct((3 * width, width), LOW),
        jax.ShapeDtypeStruct((4 * width, width), LOW),
        jax.ShapeDtypeStruct((2 * hidden, width), LOW),
        jax.ShapeDtypeStruct((routers * segs, width), LOW),
    ]
    in_vmem = pl.BlockSpec(memory_space=pltpu.VMEM)
    small, arrived, input_grad, inner_low, outer_low, up_low, down_low, route_low = pl.pallas_call(
        functools.partial(layer_kernel, lvars, lsegs, nvars, routers, batch, var_size, seg_size, sizes, groups, parts),
        in_specs=[scalars] * 2 + [in_vmem] * (16 + len(consts)),
        out_specs=[in_vmem] + [anywhere] * 7,
        out_shape=out_shapes,
        scratch_shapes=[
            pltpu.VMEM((4, batch, var_size, rows // var_size, width), LOW),
            pltpu.VMEM((4, batch, var_size, rows // var_size, width), LOW),
            pltpu.VMEM((lsegs * lanes, width), LOW),
            pltpu.VMEM((lsegs * lanes, width), F32),
            pltpu.VMEM((batch, rows, width), LOW),
            pltpu.VMEM((batch, rows, width), F32),
            pltpu.VMEM((width + routers * segs, width), LOW),
            pltpu.SemaphoreType.DMA((4, batch)),
            pltpu.SemaphoreType.DMA((4, batch)),
            pltpu.SemaphoreType.DMA((12 + 2 * batch,)),
            *[pltpu.VMEM((batch,) + shape, dtype) for shape, dtype in kept],
            *[x for count, names in groups for x in Sum.scratch(count, width, [counts_of[name] for name in names])],
            *SmallSum.scratch(S_ROWS, width, (seg_size, var_size)),
        ],
        compiler_params=pltpu.CompilerParams(
            vmem_limit_bytes=VMEM_LIMIT, collective_id=0, has_side_effects=True
        ),
        name="layer",
    )(
        domain, counts, tokens, cotangent, domain_mean, domain_scale, routes, attn_inner, attn_outer, attn_bias, mlp_in,
        mlp_in_bias, mlp_out, mlp_out_bias, norm_gain, norm_bias, heads_low, heads_f, *consts,
    )

    turns = 2

    def shares(*shape):
        shape = (shape[0] // turns,) + shape[1:]
        return pl.BlockSpec(shape, lambda i: (i,) + (0,) * (len(shape) - 1))

    piece = width * 2 // turns
    per = turns // 2
    whole = lambda x: fixed(x.shape)
    f32 = lambda x: jax.ShapeDtypeStruct(x.shape, F32)
    output, input_grad, grad_inner, grad_outer, grad_bias, grad_up, grad_up_bias, grad_down, *rest = pl.pallas_call(
        functools.partial(finish_kernel, segs, lvars),
        grid=(turns,),
        in_specs=[
            shares(*arrived.shape), shares(*input_grad.shape), whole(small),
            shares(*inner_low.shape), shares(*outer_low.shape),
            pl.BlockSpec((1, 2, piece, width), lambda i: (i // per, 0, i % per, 0)),
            shares(*down_low.shape), shares(*route_low.shape), whole(consts[1]),
        ],
        out_specs=[
            shares(*tokens.shape), shares(*input_grad.shape), shares(*inner_low.shape), shares(*outer_low.shape), whole(attn_bias),
            pl.BlockSpec((1, piece, hidden), lambda i: (i // per, i % per, 0)), whole(mlp_in_bias),
            shares(*down_low.shape), whole(mlp_out_bias), whole(norm_gain), whole(norm_bias), shares(*route_low.shape),
        ],
        out_shape=[
            f32(tokens), f32(input_grad), f32(inner_low), f32(outer_low), f32(attn_bias), f32(mlp_in), f32(mlp_in_bias),
            f32(down_low), f32(mlp_out_bias), f32(norm_gain), f32(norm_bias), f32(route_low),
        ],
        compiler_params=pltpu.CompilerParams(dimension_semantics=("arbitrary",), vmem_limit_bytes=VMEM_LIMIT),
        name="finish",
    )(
        arrived, input_grad, small, inner_low, outer_low, up_low.reshape(2, 2, width, width), down_low,
        route_low, consts[1],
    )
    grad_down_bias, grad_gain, grad_shift, grad_router = rest
    return (
        output, input_grad.reshape(tokens.shape), grad_inner.reshape(attn_inner.shape),
        grad_outer.reshape(attn_outer.shape), grad_bias, grad_up, grad_up_bias, grad_down.reshape(mlp_out.shape),
        grad_down_bias, grad_gain, grad_shift, grad_router.reshape(routers, segs, width).transpose(1, 0, 2),
    )


def solution(mesh):
    split = P("seg", "var", None, None)
    in_specs = (split, P("seg")) + (P(),) * 13 + (split,)
    out_specs = (split, split) + (P(),) * 10
    var_size, seg_size = mesh.shape["var"], mesh.shape["seg"]
    return jax.shard_map(
        functools.partial(on_device, var_size, seg_size),
        mesh=mesh, in_specs=in_specs, out_specs=out_specs, check_vma=False,
    )
```

```python
import functools

import jax
import jax.numpy as jnp
import numpy as np
from jax import lax
from jax.experimental import pallas as pl
from jax.experimental.pallas import tpu as pltpu
from jax.sharding import PartitionSpec as P

HEADS = 8
SLOTS = 16
EPS = 1e-05
MASKED = -1e30
MESH = pl.DeviceIdType.MESH
F32 = jnp.float32
LOW = jnp.bfloat16
VMEM_LIMIT = 60 * 1024 * 1024


OUT_ROUNDS = (-2, 0, 2, 4, 8, 12, 16, 18)
ATTN_ROUNDS = (0, 2, 9, 14, 17, 19, 21)
ROUTE_ROUNDS = (1, 3, 12, 16, 18, 20, 22)
FEED_ROUNDS = (12, 14, 16, 18, 20, 22, 24)
TIME_ROUNDS = (16, 17, 19, 22, 23)
ATTN_AXES = ("core", "plane", "z")
ROUTE_AXES = ("core", "plane", "z")
FEED_AXES = ("core", "plane", "z")

TOGETHER = (2, 2, 2, 2, 4)
AHEAD = 1


def mm(a, b):
    return jnp.dot(a, b, preferred_element_type=F32)


def mm_nt(a, b):
    return lax.dot_general(a, b, (((1,), (1,)), ((), ())), preferred_element_type=F32)


def mm_tn(a, b):
    return lax.dot_general(a, b, (((0,), (0,)), ((), ())), preferred_element_type=F32)


def ln_stats(a):
    mean = jnp.mean(a, axis=1, keepdims=True)
    center = a - mean
    var = jnp.mean(center * center, axis=1, keepdims=True)
    rstd = lax.rsqrt(var + EPS)
    return center * rstd, rstd


def ln_back(g, xhat, rstd, gain):
    gy = g * gain
    first = jnp.mean(gy, axis=1, keepdims=True)
    second = jnp.mean(gy * xhat, axis=1, keepdims=True)
    return rstd * (gy - first - xhat * second)


def gelu_both(z):
    k0 = np.float32(np.sqrt(2.0 / np.pi))
    k1 = np.float32(0.044715)
    square = z * z
    t = jnp.tanh(k0 * z * (1.0 + k1 * square))
    half = 0.5 * (1.0 + t)
    slope = half + 0.5 * z * (1.0 - t * t) * (k0 * (1.0 + 3.0 * k1 * square))
    return z * half, slope


def col_sum(x):
    return jnp.sum(x.astype(F32), axis=0, keepdims=True)


def spread_heads(x, heads_ref):
    return jnp.concatenate([x * heads_ref[h : h + 1, :] for h in range(HEADS)], axis=0)


def gather_heads(x, headsf_ref, rows):
    total = x[:rows] * headsf_ref[0:1, :]
    for h in range(1, HEADS):
        total = total + x[h * rows : (h + 1) * rows] * headsf_ref[h : h + 1, :]
    return total


def time_forward(
    lvars, b, several, tok_ref, offsets, factors, wi_ref, wo_ref, ab_ref, win_ref, bin_ref, wout_ref, bout_ref,
    gain_ref, shift_ref, heads_ref, headsf_ref, kept,
):
    q_ref, k_ref, v_ref, p_ref, tc_ref, x1_ref, r1_ref, f1_ref, s1_ref, x2_ref, r2_ref = kept
    segs, width = tok_ref.shape[2:]
    rows = lvars * segs
    scale = np.float32((width // HEADS) ** (-0.5))

    def keep(ref, value):
        ref[pl.ds(b, several)] = value.reshape(several, rows, value.shape[1])

    start = jnp.concatenate(
        [(tok_ref[b + i].reshape(rows, width).astype(F32) - offsets[i]) * factors[i] for i in range(several)], axis=0
    )
    low = start.astype(LOW)
    query = (mm(low, wi_ref[0, 0]) + ab_ref[0, 0:1, :]).astype(LOW)
    key = mm(low, wi_ref[0, 1]).astype(LOW)
    value = (mm(low, wi_ref[0, 2]) + ab_ref[0, 1:2, :]).astype(LOW)
    keep(q_ref, query)
    keep(k_ref, key)
    keep(v_ref, value)
    probs, contexts = [], []
    for v in range(several * lvars):
        part = slice(v * segs, (v + 1) * segs)
        scores = mm_nt(key[part], spread_heads(query[part], heads_ref))
        top = jnp.max(scores, axis=0, keepdims=True)
        expo = jnp.exp((scores - top) * scale)
        prob = (expo / jnp.sum(expo, axis=0, keepdims=True)).astype(LOW)
        probs.append(prob)
        contexts.append(gather_heads(mm_tn(prob, value[part]), headsf_ref, segs).astype(LOW))
    keep(p_ref, jnp.concatenate(probs, axis=0))
    context = jnp.concatenate(contexts, axis=0)
    keep(tc_ref, context)
    a1 = start + mm(context, wo_ref[0]) + ab_ref[0, 2:3, :]
    x1, r1 = ln_stats(a1)
    keep(x1_ref, x1.astype(LOW))
    keep(r1_ref, jnp.broadcast_to(r1, (several * rows, 128)))
    t1 = x1 * gain_ref[0:1, :] + shift_ref[0:1, :]
    act, slope = gelu_both(mm(t1.astype(LOW), win_ref[0]) + bin_ref[0:1, :])
    f1 = act.astype(LOW)
    keep(f1_ref, f1)
    keep(s1_ref, slope.astype(LOW))
    a2 = t1 + mm(f1, wout_ref[0]) + bout_ref[0:1, :]
    x2, r2 = ln_stats(a2)
    keep(x2_ref, x2.astype(LOW))
    keep(r2_ref, jnp.broadcast_to(r2, (several * rows, 128)))
    return (x2 * gain_ref[1:2, :] + shift_ref[1:2, :]).astype(LOW)


B_SK, B_SV, B_RQ, B_RK, B_RV, B_O1, B_ROWS = [256 * i for i in range(7)]
R_IN, R_OUT, R_O2, R_KQ = [256 * i for i in (0, 2, 4, 5)]
M_IN, M_OUT, M_V, M_O, M_ROWS = [256 * i for i in (0, 2, 4, 5, 6)]
T_Q, T_K, T_ROWS = [256 * i for i in (0, 1, 2)]
S_BIAS, S_IN, S_OUT, S_GAIN, S_SHIFT, S_ROWS = 0, 9, 13, 15, 19, 32


def router_start(places, router_ref, wi_ref, ab_ref, grow_ref, mask_ref, attn_ref, rest_ref, qx_ref, kq_ref):
    attn_ref[...] = jnp.zeros(attn_ref.shape, F32)
    rest_ref[...] = jnp.zeros(rest_ref.shape, F32)
    kq_ref[...] = jnp.zeros(kq_ref.shape, F32)
    mine = mm(places, router_ref[...]).astype(LOW)
    sq = (mm(mine, wi_ref[1, 0]) + ab_ref[1, 0:1, :]).astype(LOW)
    qx_ref[...] = expand(sq, grow_ref, mask_ref)


def router_end(lsegs, routers, var_size, first_seg, shrink_ref, mask_ref, rest_ref, small_ref, kq_ref):
    kq = contract(kq_ref[...], shrink_ref, mask_ref)
    small_ref[S_BIAS + 3 : S_BIAS + 4, :] = col_sum(kq)
    places = own_places(lsegs, routers, var_size, first_seg, 0)
    rest_ref[R_KQ : R_KQ + places.shape[0], :] = mm(places, kq.astype(LOW))


def own_places(lsegs, routers, var_size, first_seg, whole):
    shape = [lsegs * SLOTS] * 2
    shape[whole] = routers * lsegs * var_size
    there = lax.broadcasted_iota(jnp.int32, shape, whole)
    here = lax.broadcasted_iota(jnp.int32, shape, 1 - whole)
    here = lax.div(here, lsegs) * (lsegs * var_size) + lax.rem(here, lsegs) + first_seg
    return jnp.where(there == here, 1.0, 0.0).astype(LOW)


def expand(x, grow_ref, mask_ref):
    width = x.shape[1]
    return (mm(grow_ref[...], x).astype(LOW).reshape(-1, 16, width) * mask_ref[...][None]).reshape(-1, width)


def contract(x, shrink_ref, mask_ref):
    width = x.shape[1]
    return mm(shrink_ref[...], (x.astype(LOW).reshape(-1, 16, width) * mask_ref[...][None]).reshape(-1, width))


def router_part(
    lsegs, nvars, routers, several, arrived, leaving,
    limits, wi_ref, wo_ref, ab_ref, win_ref, bin_ref, wout_ref, bout_ref,
    gain_ref, shift_ref, mask_ref, grow_ref, shrink_ref, sumr_ref, perm_ref, back_ref,
    attn_ref, rest_ref, small_ref, qx_ref, kq_ref,
):
    series, width = perm_ref.shape[0], wo_ref.shape[1]
    rows = several * series
    lanes = SLOTS * HEADS
    scale = np.float32((width // HEADS) ** (-0.5))
    parts = range(several * lsegs)
    ns = [slice(j * nvars, (j + 1) * nvars) for j in parts]
    ls = [slice(j * lanes, (j + 1) * lanes) for j in parts]
    qs = [slice(j % lsegs * lanes, (j % lsegs + 1) * lanes) for j in parts]

    def cat(blocks):
        return jnp.concatenate(list(blocks), axis=0)

    def each(f, x):
        size = x.shape[0] // several
        return cat(f(x[i * size : (i + 1) * size]) for i in range(several))

    def grown(x):
        return each(lambda y: expand(y, grow_ref, mask_ref), x)

    def shrunk(blocks):
        return cat(contract(cat(blocks[i * lsegs : (i + 1) * lsegs]), shrink_ref, mask_ref) for i in range(several))

    def permuted(ref, x):
        return each(lambda y: mm(ref[...], y), x)

    t2 = permuted(perm_ref, arrived(0)).astype(LOW)
    sk = mm(t2, wi_ref[1, 1]).astype(LOW)
    sv = (mm(t2, wi_ref[1, 2]) + ab_ref[1, 1:2, :]).astype(LOW)
    rq = (mm(t2, wi_ref[2, 0]) + ab_ref[2, 0:1, :]).astype(LOW)
    var = lax.broadcasted_iota(jnp.int32, (nvars, lanes), 0)
    valid = [var < limit for limit in limits]

    def send_prob(j):
        real = valid[j // lsegs]
        scores = jnp.where(real, mm_nt(sk[ns[j]], qx_ref[qs[j], :]), MASKED)
        top = jnp.max(scores, axis=0, keepdims=True)
        expo = jnp.where(real, jnp.exp((scores - top) * scale), 0.0)
        return expo / jnp.sum(expo, axis=0, keepdims=True)

    sp = [send_prob(j) for j in parts]
    sp_low = [x.astype(LOW) for x in sp]
    pre_low = shrunk([mm_tn(sp_low[j], sv[ns[j]]) for j in parts]).astype(LOW)
    buffer = (mm(pre_low, wo_ref[1]) + ab_ref[1, 2:3, :]).astype(LOW)
    rkx = grown(mm(buffer, wi_ref[2, 1]).astype(LOW))
    rvx = grown((mm(buffer, wi_ref[2, 2]) + ab_ref[2, 1:2, :]).astype(LOW))
    scores = cat(mm_nt(rq[ns[j]], rkx[ls[j]]) for j in parts)
    real = lax.broadcasted_iota(jnp.int32, (rows, lanes), 1) < routers * HEADS
    scores = jnp.where(real, scores, MASKED)
    top = scores
    shift = lanes // 2
    while shift >= HEADS:
        top = jnp.maximum(top, pltpu.roll(top, shift, 1))
        shift //= 2
    expo = jnp.where(real, jnp.exp((scores - top) * scale), 0.0)
    rp = expo / mm(expo.astype(LOW), sumr_ref[...])
    rp_low = rp.astype(LOW)
    rc = cat(mm(rp_low[ns[j]], rvx[ls[j]]) for j in parts).astype(LOW)
    a3 = t2.astype(F32) + mm(rc, wo_ref[2]) + ab_ref[2, 2:3, :]
    x3, r3 = ln_stats(a3)
    t3 = x3 * gain_ref[2:3, :] + shift_ref[2:3, :]
    t3_low = t3.astype(LOW)
    act, slope = gelu_both(mm(t3_low, win_ref[1]) + bin_ref[1:2, :])
    f2 = act.astype(LOW)
    a4 = t3 + mm(f2, wout_ref[1]) + bout_ref[1:2, :]
    x4, r4 = ln_stats(a4)
    out = (x4 * gain_ref[3:4, :] + shift_ref[3:4, :]).astype(LOW)
    leaving(3, permuted(back_ref, out).astype(LOW))

    def add(row, value, ref=attn_ref):
        ref[row : row + value.shape[0], :] += value

    def add_small(row, value):
        small_ref[row : row + 1, :] += value

    cot = permuted(perm_ref, arrived(1))
    add_small(S_GAIN + 3, col_sum(cot * x4))
    add_small(S_SHIFT + 3, col_sum(cot))
    g4 = ln_back(cot, x4, r4, gain_ref[3:4, :])
    e4 = g4.astype(LOW)
    add(R_OUT, mm_tn(f2, e4), rest_ref)
    add_small(S_OUT + 1, col_sum(e4))
    e3 = (slope * mm_nt(e4, wout_ref[1])).astype(LOW)
    add(R_IN, mm_tn(t3_low, e3[:, :width]), rest_ref)
    add(R_IN + width, mm_tn(t3_low, e3[:, width:]), rest_ref)
    e3_sum = col_sum(e3)
    add_small(S_IN + 2, e3_sum[:, :width])
    add_small(S_IN + 3, e3_sum[:, width:])
    g3 = g4 + mm_nt(e3, win_ref[1])
    add_small(S_GAIN + 2, col_sum(g3 * x3))
    add_small(S_SHIFT + 2, col_sum(g3))
    g3 = ln_back(g3, x3, r3, gain_ref[2:3, :])
    eo = g3.astype(LOW)
    add(R_O2, mm_tn(rc, eo), rest_ref)
    add_small(S_BIAS + 8, col_sum(eo))
    ec = mm_nt(eo, wo_ref[2]).astype(LOW)
    dp = cat(mm_nt(ec[ns[j]], rvx[ls[j]]) for j in parts)
    ds = (scale * rp * (dp - mm((rp * dp).astype(LOW), sumr_ref[...]))).astype(LOW)
    erk = shrunk([mm_tn(ds[ns[j]], rq[ns[j]]) for j in parts]).astype(LOW)
    erv = shrunk([mm_tn(rp_low[ns[j]], ec[ns[j]]) for j in parts]).astype(LOW)
    erq = cat(mm(ds[ns[j]], rkx[ls[j]]) for j in parts).astype(LOW)
    eb = (mm_nt(erk, wi_ref[2, 1]) + mm_nt(erv, wi_ref[2, 2])).astype(LOW)
    epx = grown(mm_nt(eb, wo_ref[1]).astype(LOW))
    add(B_RQ, mm_tn(t2, erq))
    add_small(S_BIAS + 6, col_sum(erq))
    add(B_RK, mm_tn(buffer, erk))
    add(B_RV, mm_tn(buffer, erv))
    add_small(S_BIAS + 7, col_sum(erv))
    add(B_O1, mm_tn(pre_low, eb))
    add_small(S_BIAS + 5, col_sum(eb))
    dss = []
    for j in parts:
        weighted = sp[j] * mm_nt(sv[ns[j]], epx[ls[j]])
        center = jnp.sum(weighted, axis=0, keepdims=True)
        dss.append((scale * (weighted - sp[j] * center)).astype(LOW))
    esv = cat(mm(sp_low[j], epx[ls[j]]) for j in parts).astype(LOW)
    esk = cat(mm(dss[j], qx_ref[qs[j], :]) for j in parts).astype(LOW)
    g2 = g3 + mm_nt(erq, wi_ref[2, 0]) + mm_nt(esk, wi_ref[1, 1]) + mm_nt(esv, wi_ref[1, 2])
    leaving(2, permuted(back_ref, g2.astype(LOW)).astype(LOW))
    for s in range(lsegs):
        total = mm_tn(dss[s], sk[ns[s]])
        for i in range(1, several):
            total = total + mm_tn(dss[i * lsegs + s], sk[ns[i * lsegs + s]])
        kq_ref[qs[s], :] += total
    add(B_SK, mm_tn(t2, esk))
    add(B_SV, mm_tn(t2, esv))
    add_small(S_BIAS + 4, col_sum(esv))


def feed_backward(
    lvars, b, several, arrived, tok_ref, offsets, factors, wo_ref, win_ref, wout_ref, gain_ref, shift_ref, heads_ref,
    perm_ref, kept, feeds_ref, small_ref, etc_ref, g1_ref,
):
    q_ref, k_ref, v_ref, p_ref, tc_ref, x1_ref, r1_ref, f1_ref, s1_ref, x2_ref, r2_ref = kept
    segs, width = tok_ref.shape[2:]
    rows = lvars * segs

    def add(ref, row, value):
        ref[row : row + value.shape[0], :] += value

    def held(ref):
        return ref[pl.ds(b, several)].reshape(several * rows, ref.shape[2])

    def keep(ref, value):
        ref[pl.ds(b, several)] = value.reshape(several, rows, value.shape[1])

    def wide(ref):
        return jnp.concatenate([held(ref)] * (width // 128), axis=1)

    g2 = arrived(2)
    g2 = jnp.concatenate([mm(perm_ref[...], g2[i * rows : (i + 1) * rows]) for i in range(several)], axis=0)
    x2 = held(x2_ref).astype(F32)
    add(small_ref, S_GAIN + 1, col_sum(g2 * x2))
    add(small_ref, S_SHIFT + 1, col_sum(g2))
    g2 = ln_back(g2, x2, wide(r2_ref), gain_ref[1:2, :])
    e2 = g2.astype(LOW)
    add(feeds_ref, M_OUT, mm_tn(held(f1_ref), e2))
    add(small_ref, S_OUT, col_sum(e2))
    e1 = (held(s1_ref).astype(F32) * mm_nt(e2, wout_ref[0])).astype(LOW)
    x1 = held(x1_ref).astype(F32)
    t1 = (x1 * gain_ref[0:1, :] + shift_ref[0:1, :]).astype(LOW)
    add(feeds_ref, M_IN, mm_tn(t1, e1[:, :width]))
    add(feeds_ref, M_IN + width, mm_tn(t1, e1[:, width:]))
    e1_sum = col_sum(e1)
    add(small_ref, S_IN, e1_sum[:, :width])
    add(small_ref, S_IN + 1, e1_sum[:, width:])
    g1 = g2 + mm_nt(e1, win_ref[0])
    add(small_ref, S_GAIN, col_sum(g1 * x1))
    add(small_ref, S_SHIFT, col_sum(g1))
    g1 = ln_back(g1, x1, wide(r1_ref), gain_ref[0:1, :])
    keep(g1_ref, g1)
    et = g1.astype(LOW)
    add(feeds_ref, M_O, mm_tn(held(tc_ref), et))
    add(small_ref, S_BIAS + 2, col_sum(et))
    etc = mm_nt(et, wo_ref[0]).astype(LOW)
    keep(etc_ref, etc)
    prob = held(p_ref)
    grads = []
    for v in range(several * lvars):
        part = slice(v * segs, (v + 1) * segs)
        grads.append(mm(prob[part], spread_heads(etc[part], heads_ref)).astype(LOW))
    gv = jnp.concatenate(grads, axis=0)
    keep(tc_ref, gv)
    low = start_low(lvars, b, several, tok_ref, offsets, factors)
    add(feeds_ref, M_V, mm_tn(low, gv))
    add(small_ref, S_BIAS + 1, col_sum(gv))


def start_low(lvars, b, several, tok_ref, offsets, factors):
    segs, width = tok_ref.shape[2:]
    tok = [tok_ref[b + i].reshape(lvars * segs, width).astype(F32) for i in range(several)]
    return jnp.concatenate([((tok[i] - offsets[i]) * factors[i]).astype(LOW) for i in range(several)], axis=0)


def time_backward(
    lvars, b, several, tok_ref, offsets, factors, heads_ref, headsf_ref, kept, times_ref, small_ref, etc_ref
):
    q_ref, k_ref, v_ref, p_ref = kept[:4]
    segs, width = tok_ref.shape[2:]
    rows = lvars * segs
    scale = np.float32((width // HEADS) ** (-0.5))

    def add(ref, row, value):
        ref[row : row + value.shape[0], :] += value

    def held(ref):
        return ref[pl.ds(b, several)].reshape(several * rows, ref.shape[2])

    def keep(ref, value):
        ref[pl.ds(b, several)] = value.reshape(several, rows, value.shape[1])

    etc, query, key, value, probs = held(etc_ref), held(q_ref), held(k_ref), held(v_ref), held(p_ref)
    grads_q, grads_k = [], []
    for v in range(several * lvars):
        part = slice(v * segs, (v + 1) * segs)
        prob = probs[part].astype(F32)
        weighted = prob * mm_nt(value[part], spread_heads(etc[part], heads_ref))
        ets = (weighted - prob * jnp.sum(weighted, axis=0, keepdims=True)).astype(LOW)
        grads_k.append((scale * mm(ets, spread_heads(query[part], heads_ref))).astype(LOW))
        grads_q.append((scale * gather_heads(mm_tn(ets, key[part]), headsf_ref, segs)).astype(LOW))
    gq = jnp.concatenate(grads_q, axis=0)
    gk = jnp.concatenate(grads_k, axis=0)
    keep(q_ref, gq)
    keep(k_ref, gk)
    low = start_low(lvars, b, several, tok_ref, offsets, factors)
    add(times_ref, T_Q, mm_tn(low, gq))
    add(times_ref, T_K, mm_tn(low, gk))
    add(small_ref, S_BIAS, col_sum(gq))


class Sum:
    def __init__(self, axes, second, acc, send, total, recv, sems):
        self.second = second
        self.acc, self.send, self.total, self.recv, self.sems = acc, send, total, recv, sems
        self.plan = []
        start, size = 0, acc.shape[0]
        for index, count, target, peer, order in axes:
            size //= count
            self.plan.append((index, count, target, start, size, peer, order))
            start = start + index * size
        self.levels = len(self.plan)
        self.last = 2 * self.levels

    @staticmethod
    def scratch(rows, width, counts):
        recv, size = [], rows
        for count in counts:
            size //= count
            recv.append(pltpu.VMEM((count - 1, size, width), LOW))
        copies = sum(counts) - len(counts)
        return [
            pltpu.VMEM((rows, width), F32), pltpu.VMEM((rows, width), LOW), pltpu.VMEM((rows, width), LOW),
            *[pltpu.SemaphoreType.DMA((copies,))] * 4, *recv,
        ]

    def rows(self, start, size):
        return pl.ds(start if isinstance(start, int) else pl.multiple_of(start, 16), size)

    def copies(self, level, gather):
        send_sem, recv_sem = self.sems[2:] if gather else self.sems[:2]
        index, count, target, start, size, peer_at, order = self.plan[level]
        first = sum(entry[1] - 1 for entry in self.plan[:level])
        found = []
        for k, k_second in zip(*order):
            k = jnp.where(self.second, k_second, k)
            peer = peer_at(k)
            rows = self.rows(start + (index if gather else peer) * size, size)
            copy = pltpu.make_async_remote_copy(
                src_ref=(self.total if gather else self.send).at[rows, :],
                dst_ref=self.total.at[rows, :] if gather else self.recv[level].at[k - 1],
                send_sem=send_sem.at[first + k - 1],
                recv_sem=recv_sem.at[first + k - 1],
                device_id=target(peer),
                device_id_type=MESH,
            )
            found.append((copy, rows))
        return found

    def advance(self, turn):
        levels = self.levels
        if 0 < turn <= levels:
            for copy, _ in self.copies(turn - 1, False):
                copy.wait_recv()
            index, count, _, start, size = self.plan[turn - 1][:5]
            mine = self.rows(start + index * size, size)
            value = self.acc[mine, :]
            for k in range(count - 1):
                value = value + self.recv[turn - 1][k].astype(F32)
            if turn < levels:
                self.acc[mine, :] = value
            else:
                self.total[mine, :] = value.astype(LOW)
        elif turn > levels:
            for copy, _ in self.copies(self.last - turn, True):
                copy.wait_recv()
        if turn < levels:
            for copy, rows in self.copies(turn, False):
                self.send[rows, :] = self.acc[rows, :].astype(LOW)
                copy.start()
        elif turn < self.last:
            for copy, _ in self.copies(self.last - 1 - turn, True):
                copy.start()

    def sent(self):
        for level in range(self.levels):
            for gather in (False, True):
                for copy, _ in self.copies(level, gather):
                    copy.wait_send()

    @property
    def turns(self):
        return self.last + 1


class SmallSum:
    def __init__(self, acc, sent, recvs, sems, places):
        self.acc, self.sent, self.recvs, self.sems, self.places = acc, sent, recvs, sems, places

    @staticmethod
    def scratch(rows, width, sizes):
        return [
            pltpu.VMEM((rows, width), F32), pltpu.VMEM((len(sizes), rows, width), LOW),
            *[pltpu.VMEM((size, rows, width), LOW) for size in sizes],
            *[pltpu.SemaphoreType.DMA((size,)) for size in sizes for _ in range(2)],
        ]

    def copies(self, stage):
        name, me, size = self.places[stage]
        send_sem, recv_sem = self.sems[2 * stage : 2 * stage + 2]
        return [
            pltpu.make_async_remote_copy(
                src_ref=self.sent.at[stage],
                dst_ref=self.recvs[stage].at[me],
                send_sem=send_sem.at[k],
                recv_sem=recv_sem.at[k],
                device_id={name: lax.rem(me + k, size)},
                device_id_type=MESH,
            )
            for k in range(1, size)
        ]

    def start(self, stage):
        value = self.acc[...].astype(LOW)
        self.sent[stage] = value
        self.recvs[stage][self.places[stage][1]] = value
        for copy in self.copies(stage):
            copy.start()

    def finish(self, stage):
        for copy in self.copies(stage):
            copy.wait()
        value = self.recvs[stage][0].astype(F32)
        for k in range(1, self.places[stage][2]):
            value = value + self.recvs[stage][k].astype(F32)
        self.acc[...] = value


def layer_kernel(
    lvars, lsegs, nvars, routers, steps, var_size, seg_size, sizes, groups, shares,
    dom_ref, cnt_ref, tok_ref, cot_ref, mean_ref, scale_ref, router_ref, wi_ref, wo_ref, ab_ref,
    win_ref, bin_ref, wout_ref, bout_ref, gain_ref, shift_ref, heads_ref, headsf_ref, split_ref, join_ref, mask_ref, grow_ref, shrink_ref, sumr_ref, swap_ref, back_ref,
    small_out_ref, out_ref, gin_ref, inner_ref, outer_ref, up_ref, down_ref, route_ref,
    sent_ref, came_ref, qx_ref, kq_ref, etc_ref, g1_ref, made_ref, send_sem, recv_sem, out_sem, *scratch,
):
    me = lax.axis_index("var")
    seg = lax.axis_index("seg")
    width = tok_ref.shape[3]
    rows = lvars * tok_ref.shape[2]
    block = rows // var_size
    kept, scratch = scratch[:11], scratch[11:]
    cores, xs, ys, zs = sizes
    core, xi = lax.rem(seg, cores), lax.div(seg, cores)
    yi, zi = lax.rem(me, ys), lax.div(me, ys)

    def space(i):
        return {"seg": lax.rem(i, xs) * cores + core, "var": lax.div(i, xs)}

    def step(i, k, count):
        return lax.rem(i + k, count)

    def both_ways(count):
        return list(range(1, count)), list(range(count - 1, 0, -1))

    def line(index, count, target):
        return index, count, target, lambda k: step(index, k, count), both_ways(count)

    def plane_peer(k):
        return step(yi, lax.div(k, xs), ys) * xs + step(xi, lax.rem(k, xs), xs)

    def space_peer(k):
        return step(zi, lax.div(k, xs * ys), zs) * (xs * ys) + plane_peer(lax.rem(k, xs * ys))

    axes = {
        "core": line(core, cores, lambda i: {"seg": xi * cores + i}),
        "plane": (
            yi * xs + xi, xs * ys, lambda i: space(zi * (xs * ys) + i), plane_peer,
            [sorted(range(1, xs * ys), key=lambda k: (k // xs > 0 and k % xs > 0, turn * k)) for turn in (1, -1)],
        ),
        "z": line(zi, zs, lambda i: {"var": i * ys + yi}),
        "space": (me * xs + xi, var_size * xs, space, space_peer, both_ways(var_size * xs)),
    }
    second = core > 0
    sums = []
    for _, names in groups:
        used = 7 + len(names)
        group, scratch = scratch[:used], scratch[used:]
        sums.append(Sum([axes[name] for name in names], second, group[0], group[1], group[2], group[7:], group[3:7]))
    parts = []
    for index, base, count in shares:
        parts.append((sums[index], base, sums[index].acc.at[pl.ds(base, count), :]))
    attns, routes, feeds, times = parts
    small = SmallSum(scratch[0], scratch[1], scratch[2:4], scratch[4:8], [("seg", seg, seg_size), ("var", me, var_size)])

    def copy(kind, b, k):
        target = lax.rem(me + k, var_size)
        return pltpu.make_async_remote_copy(
            src_ref=sent_ref.at[kind, b, target],
            dst_ref=came_ref.at[kind, b, me],
            send_sem=send_sem.at[kind, b],
            recv_sem=recv_sem.at[kind, b],
            device_id={"var": target},
            device_id_type=MESH,
        )

    def whole(kind, b):
        others = pl.ds(0, var_size - 1)
        return pltpu.make_async_remote_copy(
            src_ref=sent_ref.at[kind, b, others],
            dst_ref=came_ref.at[kind, b, others],
            send_sem=send_sem.at[kind, b],
            recv_sem=recv_sem.at[kind, b],
            device_id={"var": lax.rem(me + 1, var_size)},
            device_id_type=MESH,
        )

    def store(kind, b, several, value):
        value = value.reshape(several, var_size, block, width)
        sent_ref[kind, pl.ds(b, several)] = value
        for i in range(several):
            came_ref[kind, b + i, me] = sent_ref[kind, b + i, me]

    def send(kind, b, several=1):
        for i in range(several):
            for k in range(1, var_size):
                copy(kind, b + i, k).start()

    def pick(b, ref):
        total = jnp.zeros((1, width), F32)
        for d in range(ref.shape[0]):
            total = total + jnp.where(dom_ref[b] == d, ref[d : d + 1, :], 0.0)
        return total

    def picks(b, several, ref):
        return [pick(b + i, ref) for i in range(several)]

    def arrived(kind, b, several):
        for i in range(several):
            whole(kind, b + i).wait_recv()
        return came_ref[kind, pl.ds(b, several)].reshape(several * rows, width)

    pieces = [
        (times, T_Q, 2 * width, inner_ref, 0), (feeds, M_V, width, inner_ref, 2 * width), (None, 0, width, inner_ref, 3 * width),
        (attns, B_SK, 5 * width, inner_ref, 4 * width),
        (feeds, M_O, width, outer_ref, 0), (attns, B_O1, width, outer_ref, width), (routes, R_O2, width, outer_ref, 2 * width),
        (feeds, M_IN, 2 * width, up_ref, 0), (routes, R_IN, 2 * width, up_ref, 2 * width),
        (feeds, M_OUT, 2 * width, down_ref, 0), (routes, R_OUT, 2 * width, down_ref, 2 * width),
        (None, width, route_ref.shape[0], route_ref, 0),
    ]

    def deliver(which):
        return [
            pltpu.make_async_copy(
                (made_ref if part is None else which.total).at[pl.ds((0 if part is None else part[1]) + row, count), :],
                ref.at[pl.ds(there, count), :],
                out_sem.at[index],
            )
            for index, (part, row, count, ref, there) in enumerate(pieces)
            if (routes if part is None else part)[0] is which
        ]

    def make_routes():
        total, base, _ = routes
        kq = total.total[base + R_KQ : base + R_KQ + route_ref.shape[0], :]
        made_ref[:width, :] = mm_tn(router_ref[...], kq).astype(LOW)
        made_ref[width:, :] = mm_nt(kq, wi_ref[1, 0]).astype(LOW)

    def series_out(kind, b):
        source, ref = ((came_ref.at[3, b], out_ref), (etc_ref.at[b], gin_ref))[kind]
        return pltpu.make_async_copy(source, ref.at[b], out_sem.at[len(pieces) + kind * steps + b])

    barrier = pltpu.get_barrier_semaphore()
    spaces = axes["space"][1]
    for k in range(1, spaces):
        pl.semaphore_signal(barrier, inc=1, device_id=space(lax.rem(axes["space"][0] + k, spaces)), device_id_type=MESH)
    for k in range(1, cores):
        for i in range(xs):
            peer = {"seg": i * cores + lax.rem(core + k, cores)}
            pl.semaphore_signal(barrier, inc=1, device_id=peer, device_id_type=MESH)
    small.acc[...] = jnp.zeros_like(small.acc)
    router_start(
        own_places(lsegs, routers, var_size, me * lsegs, 1), router_ref, wi_ref, ab_ref, grow_ref, mask_ref, attns[2], routes[2], qx_ref, kq_ref
    )
    feeds[2][...] = jnp.zeros(feeds[2].shape, F32)
    times[2][...] = jnp.zeros(times[2].shape, F32)
    pl.semaphore_wait(barrier, spaces - 1 + (cores - 1) * xs)

    def forward(b, several):
        for i in range(several):
            store(1, b + i, 1, mm(split_ref[...], cot_ref[b + i].reshape(rows, width)).astype(LOW))
        send(1, b, several)
        t2 = time_forward(
            lvars, b, several, tok_ref, picks(b, several, mean_ref), picks(b, several, scale_ref), wi_ref, wo_ref,
            ab_ref, win_ref, bin_ref, wout_ref, bout_ref, gain_ref, shift_ref, heads_ref, headsf_ref, kept,
        )
        for i in range(several):
            store(0, b + i, 1, mm(split_ref[...], t2[i * rows : (i + 1) * rows]).astype(LOW))
        send(0, b, several)

    def middle(b, several):
        def leaving(kind, value):
            store(kind, b, several, value)
            if kind == 2:
                send(2, b, several)

        limits = []
        for i in range(several):
            limit = jnp.int32(0)
            for d in range(cnt_ref.shape[0]):
                limit = limit + jnp.where(dom_ref[b + i] == d, cnt_ref[d], 0)
            limits.append(limit)
        router_part(
            lsegs, nvars, routers, several, lambda kind: arrived(kind, b, several), leaving,
            limits, wi_ref, wo_ref, ab_ref, win_ref, bin_ref, wout_ref, bout_ref,
            gain_ref, shift_ref, mask_ref, grow_ref, shrink_ref, sumr_ref, swap_ref, back_ref,
            attns[2], routes[2], small.acc, qx_ref, kq_ref,
        )

    def back_feed(b, several):
        feed_backward(
            lvars, b, several, lambda kind: arrived(kind, b, several), tok_ref, picks(b, several, mean_ref),
            picks(b, several, scale_ref), wo_ref, win_ref, wout_ref, gain_ref, shift_ref, heads_ref, join_ref, kept,
            feeds[2], small.acc, etc_ref, g1_ref,
        )

    def back_time(b, several):
        time_backward(
            lvars, b, several, tok_ref, picks(b, several, mean_ref), picks(b, several, scale_ref), heads_ref, headsf_ref,
            kept, times[2], small.acc, etc_ref,
        )

    def back_input(b, several):
        def held(ref):
            return ref[pl.ds(b, several)].reshape(several * rows, width)

        grad = held(g1_ref) + mm_nt(held(kept[0]), wi_ref[0, 0]) + mm_nt(held(kept[1]), wi_ref[0, 1])
        grad = grad + mm_nt(held(kept[4]), wi_ref[0, 2])
        for i in range(several):
            etc_ref[b + i] = (grad[i * rows : (i + 1) * rows] * pick(b + i, scale_ref)).astype(LOW)
            series_out(1, b + i).start()

    todo = {}

    def plan(total, *rounds):
        for turn in range(total.turns):
            todo.setdefault(rounds[min(turn, len(rounds) - 1)], []).append(functools.partial(total.advance, turn))

    for b, round_ in enumerate(OUT_ROUNDS):
        todo.setdefault(round_, []).append(functools.partial(send, 3, b))
    rounds_of = (ATTN_ROUNDS, ROUTE_ROUNDS, FEED_ROUNDS, TIME_ROUNDS) if len(sums) > 1 else ((2 * steps, 3 * steps),)
    for total, rounds in zip(sums, rounds_of):
        plan(total, *rounds)
    todo.setdefault(2 * steps, []).append(functools.partial(small.start, 0))
    todo.setdefault(2 * steps + steps // 2, []).append(lambda: (small.finish(0), small.start(1)))

    def sweep(run, first, several):
        def body(i, carry):
            b = i * several
            for round_, acts in sorted(todo.items()):
                if first <= round_ < first + steps:

                    @pl.when(i == (round_ - first) // several)
                    def _(acts=acts):
                        for act in acts:
                            act()

            run(b, several)
            return carry

        lax.fori_loop(0, steps // several, body, 0)

    together = TOGETHER if len(sums) > 1 else (1,) * 5
    sweep(forward, -2 * steps, together[0])
    sweep(middle, -steps, together[1])
    router_end(
        lsegs, routers, var_size, me * lsegs, shrink_ref, mask_ref, routes[2], small.acc, kq_ref,
    )
    several = together[2]
    count = steps // several
    early = max(count - AHEAD, 1)

    def backward(i, carry):
        for round_, acts in sorted(todo.items()):
            if 0 <= round_ < 2 * steps:

                @pl.when(i == round_ // several)
                def _(acts=acts):
                    for act in acts:
                        act()

        lead = early + early - 1
        feed = (i < early) | ((i >= lead) & (i < lead + count - early))

        @pl.when(feed)
        def _():
            back_feed(jnp.where(i < early, i, i - lead + early) * several, several)

        @pl.when(jnp.logical_not(feed))
        def _():
            back_time(jnp.where(i < lead, i - early, i - count) * several, several)

        return carry

    lax.fori_loop(0, 2 * count, backward, 0)
    sweep(back_input, 2 * steps, together[4])
    last = [max(rounds[: total.turns]) for total, rounds in zip(sums, rounds_of)]
    for round_ in range(3 * steps, max(max(todo), 3 * steps, *last) + 1):
        for act in todo.get(round_, []):
            act()
        for total, end in zip(sums, last):
            if round_ == max(end, 3 * steps):
                if total is routes[0]:
                    make_routes()
                for copy in deliver(total):
                    copy.start()
    small.finish(1)
    small_out_ref[...] = small.acc[...]
    for b in range(steps):
        whole(3, b).wait_recv()
        series_out(0, b).start()
    for b in range(steps):
        for kind in range(4):
            whole(kind, b).wait_send()
    for total in sums:
        total.sent()
        for copy in deliver(total):
            copy.wait()
    for b in range(steps):
        series_out(0, b).wait()
        series_out(1, b).wait()


def finish_kernel(
    segs, lvars, out_ref, gin_ref, small_ref, inner_ref, outer_ref, up_ref, down_ref, route_ref, join_ref,
    output_ref, gin_out_ref, ginner_ref, gouter_ref, gbias_ref, gup_ref, gupb_ref, gdown_ref, gdownb_ref, ggain_ref,
    gshift_ref, groute_ref,
):
    width = inner_ref.shape[1]

    @pl.when(pl.program_id(0) == 0)
    def _():
        for i in range(3):
            gbias_ref[i] = small_ref[S_BIAS + 3 * i : S_BIAS + 3 * i + 3, :]
        for i in range(2):
            for j in range(2):
                row = S_IN + 2 * i + j
                gupb_ref[i : i + 1, j * width : (j + 1) * width] = small_ref[row : row + 1, :]
        gdownb_ref[...] = small_ref[S_OUT : S_OUT + 2, :]
        ggain_ref[...] = small_ref[S_GAIN : S_GAIN + 4, :]
        gshift_ref[...] = small_ref[S_SHIFT : S_SHIFT + 4, :]

    for i in range(out_ref.shape[0]):
        output_ref[i] = mm(join_ref[...], out_ref[i].reshape(lvars * segs, width)).reshape(lvars, segs, width)
    gin_out_ref[...] = gin_ref[...].astype(F32)
    ginner_ref[...] = inner_ref[...].astype(F32)
    gouter_ref[...] = outer_ref[...].astype(F32)
    gup_ref[0, :, :width] = up_ref[0, 0].astype(F32)
    gup_ref[0, :, width:] = up_ref[0, 1].astype(F32)
    gdown_ref[...] = down_ref[...].astype(F32)
    groute_ref[...] = route_ref[...].astype(F32)


def fixed(shape, index=None):
    index = (0,) * len(shape) if index is None else index
    return pl.BlockSpec(shape, lambda b: index)


def on_device(
    var_size, seg_size,
    tokens, domain, counts, domain_mean, domain_scale, attn_inner, attn_outer, attn_bias,
    mlp_in, mlp_in_bias, mlp_out, mlp_out_bias, norm_gain, norm_bias, router, cotangent,
):
    batch, lvars, segs, width = tokens.shape
    routers = router.shape[1]
    hidden = mlp_in.shape[2]
    lsegs = segs // var_size
    nvars = lvars * var_size
    rows = lvars * segs
    lanes = SLOTS * HEADS
    heads = (np.arange(width)[None, :] // (width // HEADS) == np.arange(HEADS)[:, None]).astype(np.float32)
    heads_low = jnp.asarray(heads, LOW)
    heads_f = jnp.asarray(heads, F32)
    mask = jnp.asarray(np.concatenate([heads, heads], axis=0), LOW)
    order = np.arange(rows).reshape(lvars, var_size, lsegs).transpose(1, 0, 2).reshape(-1)
    split = np.eye(rows, dtype=np.float32)[order]
    order = np.arange(rows).reshape(nvars, lsegs).transpose(1, 0).reshape(-1)
    swap = np.eye(rows, dtype=np.float32)[order]
    group = np.arange(lsegs * lanes) // HEADS
    group = group % SLOTS * lsegs + group // SLOTS
    grow = (group[:, None] == np.arange(lsegs * SLOTS)[None, :]).astype(np.float32)
    sumr = (np.arange(lanes)[:, None] % HEADS == np.arange(lanes)[None, :] % HEADS).astype(np.float32)

    kept = [
        ((rows, width), LOW), ((rows, width), LOW), ((rows, width), LOW), ((rows, HEADS * segs), LOW),
        ((rows, width), LOW), ((rows, width), LOW), ((rows, 128), F32), ((rows, hidden), LOW),
        ((rows, hidden), LOW), ((rows, width), LOW), ((rows, 128), F32),
    ]
    routes = router.transpose(1, 0, 2).reshape(routers * segs, width)
    consts = [jnp.asarray(x, LOW) for x in (split, split.T)] + [mask]
    consts += [jnp.asarray(x, LOW) for x in (grow, grow.T, sumr, swap, swap.T)]

    cores = 2 if seg_size % 2 == 0 else 1
    xs = seg_size // cores
    ys = xs if var_size % xs == 0 else 1
    zs = var_size // ys
    sizes = (cores, xs, ys, zs)
    counts_of = {"core": cores, "plane": xs * ys, "z": zs, "space": var_size * xs}
    far = ("core", "plane", "z")
    near = ("core", "space") if var_size * xs <= 16 else far
    unit = 16 * var_size * seg_size
    wanted = [(B_ROWS, ATTN_AXES), (R_KQ + segs * routers, ROUTE_AXES), (M_ROWS, FEED_AXES), (T_ROWS, near)]
    if unit > 1024:
        starts = np.cumsum([0] + [count for count, _ in wanted])
        parts = [(0, int(start), count) for start, (count, _) in zip(starts, wanted)]
        wanted = [(int(starts[-1]), far)]
    else:
        parts = [(index, 0, count) for index, (count, _) in enumerate(wanted)]
    groups = []
    for count, names in wanted:
        groups.append((-(-count // unit) * unit, [name for name in names if counts_of[name] > 1]))
    scalars = pl.BlockSpec(memory_space=pltpu.SMEM)
    anywhere = pl.BlockSpec(memory_space=pl.ANY)
    out_shapes = [
        jax.ShapeDtypeStruct((S_ROWS, width), F32),
        jax.ShapeDtypeStruct((batch, var_size, rows // var_size, width), LOW),
        jax.ShapeDtypeStruct((batch, rows, width), LOW),
        jax.ShapeDtypeStruct((9 * width, width), LOW),
        jax.ShapeDtypeStruct((3 * width, width), LOW),
        jax.ShapeDtypeStruct((4 * width, width), LOW),
        jax.ShapeDtypeStruct((2 * hidden, width), LOW),
        jax.ShapeDtypeStruct((routers * segs, width), LOW),
    ]
    in_vmem = pl.BlockSpec(memory_space=pltpu.VMEM)
    small, arrived, input_grad, inner_low, outer_low, up_low, down_low, route_low = pl.pallas_call(
        functools.partial(layer_kernel, lvars, lsegs, nvars, routers, batch, var_size, seg_size, sizes, groups, parts),
        in_specs=[scalars] * 2 + [in_vmem] * (16 + len(consts)),
        out_specs=[in_vmem] + [anywhere] * 7,
        out_shape=out_shapes,
        scratch_shapes=[
            pltpu.VMEM((4, batch, var_size, rows // var_size, width), LOW),
            pltpu.VMEM((4, batch, var_size, rows // var_size, width), LOW),
            pltpu.VMEM((lsegs * lanes, width), LOW),
            pltpu.VMEM((lsegs * lanes, width), F32),
            pltpu.VMEM((batch, rows, width), LOW),
            pltpu.VMEM((batch, rows, width), F32),
            pltpu.VMEM((width + routers * segs, width), LOW),
            pltpu.SemaphoreType.DMA((4, batch)),
            pltpu.SemaphoreType.DMA((4, batch)),
            pltpu.SemaphoreType.DMA((12 + 2 * batch,)),
            *[pltpu.VMEM((batch,) + shape, dtype) for shape, dtype in kept],
            *[x for count, names in groups for x in Sum.scratch(count, width, [counts_of[name] for name in names])],
            *SmallSum.scratch(S_ROWS, width, (seg_size, var_size)),
        ],
        compiler_params=pltpu.CompilerParams(
            vmem_limit_bytes=VMEM_LIMIT, collective_id=0, has_side_effects=True
        ),
        name="layer",
    )(
        domain, counts, tokens, cotangent, domain_mean, domain_scale, routes, attn_inner, attn_outer, attn_bias, mlp_in,
        mlp_in_bias, mlp_out, mlp_out_bias, norm_gain, norm_bias, heads_low, heads_f, *consts,
    )

    turns = 2

    def shares(*shape):
        shape = (shape[0] // turns,) + shape[1:]
        return pl.BlockSpec(shape, lambda i: (i,) + (0,) * (len(shape) - 1))

    piece = width * 2 // turns
    per = turns // 2
    whole = lambda x: fixed(x.shape)
    f32 = lambda x: jax.ShapeDtypeStruct(x.shape, F32)
    output, input_grad, grad_inner, grad_outer, grad_bias, grad_up, grad_up_bias, grad_down, *rest = pl.pallas_call(
        functools.partial(finish_kernel, segs, lvars),
        grid=(turns,),
        in_specs=[
            shares(*arrived.shape), shares(*input_grad.shape), whole(small),
            shares(*inner_low.shape), shares(*outer_low.shape),
            pl.BlockSpec((1, 2, piece, width), lambda i: (i // per, 0, i % per, 0)),
            shares(*down_low.shape), shares(*route_low.shape), whole(consts[1]),
        ],
        out_specs=[
            shares(*tokens.shape), shares(*input_grad.shape), shares(*inner_low.shape), shares(*outer_low.shape), whole(attn_bias),
            pl.BlockSpec((1, piece, hidden), lambda i: (i // per, i % per, 0)), whole(mlp_in_bias),
            shares(*down_low.shape), whole(mlp_out_bias), whole(norm_gain), whole(norm_bias), shares(*route_low.shape),
        ],
        out_shape=[
            f32(tokens), f32(input_grad), f32(inner_low), f32(outer_low), f32(attn_bias), f32(mlp_in), f32(mlp_in_bias),
            f32(down_low), f32(mlp_out_bias), f32(norm_gain), f32(norm_bias), f32(route_low),
        ],
        compiler_params=pltpu.CompilerParams(dimension_semantics=("arbitrary",), vmem_limit_bytes=VMEM_LIMIT),
        name="finish",
    )(
        arrived, input_grad, small, inner_low, outer_low, up_low.reshape(2, 2, width, width), down_low,
        route_low, consts[1],
    )
    grad_down_bias, grad_gain, grad_shift, grad_router = rest
    return (
        output, input_grad.reshape(tokens.shape), grad_inner.reshape(attn_inner.shape),
        grad_outer.reshape(attn_outer.shape), grad_bias, grad_up, grad_up_bias, grad_down.reshape(mlp_out.shape),
        grad_down_bias, grad_gain, grad_shift, grad_router.reshape(routers, segs, width).transpose(1, 0, 2),
    )


def solution(mesh):
    split = P("seg", "var", None, None)
    in_specs = (split, P("seg")) + (P(),) * 13 + (split,)
    out_specs = (split, split) + (P(),) * 10
    var_size, seg_size = mesh.shape["var"], mesh.shape["seg"]
    return jax.shard_map(
        functools.partial(on_device, var_size, seg_size),
        mesh=mesh, in_specs=in_specs, out_specs=out_specs, check_vma=False,
    )
```
